32 devices in a mesh: dp: 16 (over z, y, x), tensor: 2 (over core).
Axes of the slice: x: 2, y: 2, z: 4, core: 2. Of those that a mesh axis runs over, the one named last changes fastest.
Arguments:
- tokens: bfloat16 [3152, 768], P('dp')
- grad_out: bfloat16 [3152, 768], P('dp'), may hold values from -6 to 6
- valid_mask: int32 [3152], P('dp'), may hold values from 0 to 1, as said below
- routes: int32 [3152, 2], P('dp'), may hold values from 0 to 15, as said below
- slot_index: int32 [3152, 2], P('dp'), may hold values from 0 to 36, as said below
- ln1_gain: float32 [768], replicated, may hold values from 0.5 to 1.5
- ln1_bias: float32 [768], replicated, may hold values from -1 to 1
- w_qkv: bfloat16 [768, 3, 768], P(None, None, 'tensor'), may hold values from -0.21875 to 0.21875
- bias_qv: float32 [2, 768], P(None, 'tensor'), may hold values from -1 to 1
- w_attn_out: bfloat16 [768, 768], P('tensor'), may hold values from -1.75 to 1.75
- b_attn_out: float32 [768], replicated, may hold values from -1 to 1
- ln2_gain: float32 [768], replicated, may hold values from 0.5 to 1.5
- ln2_bias: float32 [768], replicated, may hold values from -1 to 1
- router: bfloat16 [768, 16], replicated, may hold values from -0.15625 to 0.15625
- w_expert_in: bfloat16 [16, 768, 3072], P('dp', None, 'tensor'), may hold values from -0.21875 to 0.21875
- b_expert_in: float32 [16, 3072], P('dp', 'tensor'), may hold values from -1 to 1
- w_expert_out: bfloat16 [16, 3072, 768], P('dp', 'tensor'), may hold values from -0.15625 to 0.15625
- b_expert_out: float32 [16, 768], P('dp'), may hold values from -1 to 1
Outputs:
- out_tokens: bfloat16 [3152, 768], P('dp')
- grad_tokens: float32 [3152, 768], P('dp')
- grad_ln1_gain: float32 [768], replicated
- grad_ln1_bias: float32 [768], replicated
- grad_w_qkv: float32 [768, 3, 768], P(None, None, 'tensor')
- grad_bias_qv: float32 [2, 768], P(None, 'tensor')
- grad_w_attn_out: float32 [768, 768], P('tensor')
- grad_b_attn_out: float32 [768], replicated
- grad_ln2_gain: float32 [768], replicated
- grad_ln2_bias: float32 [768], replicated
- grad_router: float32 [768, 16], replicated
- grad_w_expert_in: float32 [16, 768, 3072], P('dp', None, 'tensor')
- grad_b_expert_in: float32 [16, 3072], P('dp', 'tensor')
- grad_w_expert_out: float32 [16, 3072, 768], P('dp', 'tensor')
- grad_b_expert_out: float32 [16, 768], P('dp')
- rms_values: float32 [4], replicated
The draws below stay inside these ranges and needn't reach their ends.
Inputs may be any that keep to these rules, and one draw needn't show every extreme that they name: `routes`: each token names two different experts. `slot_index`: 36 means that the route is not sent. Among the tokens of one index of dp, the sent routes of one expert take distinct slots, given in token order until 36 is reached; routes of tokens with valid_mask 0 are never sent; on every index of dp some expert has all 36 slots taken. `valid_mask`: the first token of every image is valid.
All inputs are finite; a program needn't handle non-finite values.
Results may differ from the reference program's by a relative error of at most 0.013.
Values may be sent and summed in bfloat16 or wider, within the bound.
A program may use at most 128 MiB of HBM per device.

```python
import math
import jax
import jax.numpy as jnp
from jax import lax

D = 768
HEADS = 12
HEAD = 64
FF = 3072
SEQ = 197
IMG_DEV = 1
TOK_DEV = 197
IMAGES = 16
TOKENS = 3152
EXPERTS = 16
CAP = 36
N_DP = 16


def routing_tables(key):
    key_hot, key_first, key_second, key_keep = jax.random.split(key, 4)
    block_count = TOKENS // TOK_DEV
    position = jnp.arange(TOKENS, dtype=jnp.int32)
    hot_expert = jax.random.randint(key_hot, (), 0, EXPERTS, dtype=jnp.int32)
    first_choice = jax.random.randint(key_first, (TOKENS,), 0, EXPERTS, dtype=jnp.int32)
    first_choice = jnp.where(position % TOK_DEV % 4 == 0, hot_expert, first_choice)
    offset = jax.random.randint(key_second, (TOKENS,), 1, EXPERTS, dtype=jnp.int32)
    second = (first_choice + offset) % EXPERTS
    keep_flags = jax.random.randint(key_keep, (TOKENS,), 0, 8, dtype=jnp.int32) < 7
    keep_flags = jnp.logical_or(keep_flags, position % SEQ == 0).astype(jnp.int32)
    route_pair = jnp.stack([first_choice, second], axis=1)
    one_hot = (route_pair[:, :, None] == jnp.arange(EXPERTS, dtype=jnp.int32)[None, None, :]).astype(jnp.int32)
    one_hot = one_hot * keep_flags[:, None, None]
    one_hot = one_hot.reshape(block_count, TOK_DEV * 2, EXPERTS)
    earlier = jnp.cumsum(one_hot, axis=1) - one_hot
    place_index = jnp.sum(earlier * one_hot, axis=-1).reshape(TOKENS, 2)
    slot_table = jnp.where((keep_flags[:, None] > 0) & (place_index < CAP), place_index, CAP)
    return (route_pair, slot_table.astype(jnp.int32), keep_flags)


def draw_routes(key, part):
    route_pair, slot_table, keep_flags = routing_tables(key)
    return route_pair


def draw_slot_index(key, part):
    route_pair, slot_table, keep_flags = routing_tables(key)
    return slot_table


def draw_valid_mask(key, part):
    route_pair, slot_table, keep_flags = routing_tables(key)
    return keep_flags


def draw_tokens(key, part):
    key = jax.random.fold_in(key, 11)
    image_index = jnp.arange(TOKENS, dtype=jnp.int32) // SEQ
    ramp_value = image_index.astype(jnp.float32) / max(IMAGES - 1, 1)
    noise_draw = jnp.clip(jax.random.normal(key, (TOKENS, D), jnp.float32), -5.0, 5.0)
    scale_rows = 0.5 * jnp.power(6.0, ramp_value)
    return (noise_draw * scale_rows[:, None]).astype(jnp.bfloat16)


def shard_levels(stream_key, dims, shards, smallest, high):
    loudness = 1.0
    for axis_at, parts in shards:
        steps = jax.random.uniform(jax.random.fold_in(jax.random.fold_in(stream_key, 6), axis_at), (parts,), jnp.float32, smallest / len(shards), high / len(shards))
        loudness = loudness * jnp.repeat(jnp.exp(steps), dims[axis_at] // parts).reshape((-1,) + (1,) * (len(dims) - 1 - axis_at))
    return loudness


def noise(key, dims, width, bound, shards=(), kind=jnp.bfloat16):
    drawn = jax.random.normal(key, dims, jnp.float32) * width
    if len(shards) > 0:
        drawn = shard_levels(key, dims, shards, -0.22, 0.18) * drawn
    return jnp.clip(drawn, min=-bound, max=bound).astype(kind)


def setup_inputs(seed: int = 0) -> dict:
    splits = jax.random.split(jax.random.key(seed), 19)
    tokens = draw_tokens(jax.random.fold_in(splits[18], 71), 0)
    grad_out = noise(splits[1], (TOKENS, D), 1.0, 6.0, ((0, 16),))
    valid_mask = draw_valid_mask(jax.random.fold_in(splits[18], 71), 0)
    routes = draw_routes(jax.random.fold_in(splits[18], 71), 0)
    slot_index = draw_slot_index(jax.random.fold_in(splits[18], 71), 0)
    ln1_gain = jnp.clip(1.0 + 0.1 * jax.random.normal(splits[5], (D,), jnp.float32), 0.5, 1.5)
    ln1_bias = noise(splits[6], (D,), 0.2, 1.0, (), jnp.float32)
    w_qkv = noise(splits[7], (D, 3, HEADS * HEAD), D ** -0.5, 0.21875, ((2, 2),))
    bias_qv = noise(splits[8], (2, HEADS * HEAD), 0.2, 1.0, ((1, 2),), jnp.float32)
    w_attn_out = noise(splits[9], (HEADS * HEAD, D), (HEADS * HEAD // 64) ** -0.5, 1.75, ((0, 2),))
    b_attn_out = noise(splits[10], (D,), 0.2, 1.0, (), jnp.float32)
    ln2_gain = jnp.clip(1.0 + 0.1 * jax.random.normal(splits[11], (D,), jnp.float32), 0.5, 1.5)
    ln2_bias = noise(splits[12], (D,), 0.2, 1.0, (), jnp.float32)
    router = noise(splits[13], (D, EXPERTS), (2 * D) ** -0.5, 0.15625)
    w_expert_in = noise(splits[14], (EXPERTS, D, FF), D ** -0.5, 0.21875, ((0, 16), (2, 2)))
    b_expert_in = noise(splits[15], (EXPERTS, FF), 0.2, 1.0, ((0, 16), (1, 2)), jnp.float32)
    w_expert_out = noise(splits[16], (EXPERTS, FF, D), (FF // 2) ** -0.5, 0.15625, ((0, 16), (1, 2)))
    b_expert_out = noise(splits[17], (EXPERTS, D), 0.2, 1.0, ((0, 16),), jnp.float32)
    return {"tokens": tokens, "grad_out": grad_out, "valid_mask": valid_mask, "routes": routes, "slot_index": slot_index, "ln1_gain": ln1_gain, "ln1_bias": ln1_bias, "w_qkv": w_qkv, "bias_qv": bias_qv, "w_attn_out": w_attn_out, "b_attn_out": b_attn_out, "ln2_gain": ln2_gain, "ln2_bias": ln2_bias, "router": router, "w_expert_in": w_expert_in, "b_expert_in": b_expert_in, "w_expert_out": w_expert_out, "b_expert_out": b_expert_out}


HIGHEST = lax.Precision.HIGHEST

@jax.custom_vjp
def low(v):
    return lax.optimization_barrier(v.astype(jnp.bfloat16)).astype(jnp.float32)

@jax.custom_vjp
def low_back(v):
    return v

def low_keep(v):
    return (low(v), None)

def low_pass(kept, grad):
    return (grad,)

def back_keep(v):
    return (v, None)

def back_low(kept, grad):
    return (low(grad),)
low.defvjp(low_keep, low_pass)
low_back.defvjp(back_keep, back_low)

def layer_norm(values, gain_vec, shift_vec):
    center = values - lax.optimization_barrier(jnp.mean(values, axis=-1, keepdims=True))
    inverse = lax.rsqrt(lax.optimization_barrier(jnp.mean(center * center, axis=-1, keepdims=True)) + 1e-06)
    return center * inverse * gain_vec + shift_vec

def attend_group(packed):
    projected, keep_group = packed
    queries = projected[:, :, 0]
    keys_img = projected[:, :, 1]
    values_img = projected[:, :, 2]
    scores = jnp.einsum('iqhd,ikhd->ihqk', queries, keys_img, precision=HIGHEST) * (1.0 / math.sqrt(HEAD))
    scores = jnp.where(keep_group[:, None, None, :] > 0, scores, -1000000000.0)
    scores = low_back(scores)
    top_score = lax.optimization_barrier(jnp.max(scores, axis=-1, keepdims=True))
    weights = jnp.exp(scores - top_score)
    attn_probs = weights / lax.optimization_barrier(jnp.sum(weights, axis=-1, keepdims=True))
    return jnp.einsum('ihqk,ikhd->iqhd', low(attn_probs), values_img, precision=HIGHEST)

def reference(tokens, grad_out, valid_mask, routes, slot_index, ln1_gain, ln1_bias, w_qkv, bias_qv, w_attn_out, b_attn_out, ln2_gain, ln2_bias, router, w_expert_in, b_expert_in, w_expert_out, b_expert_out):
    keep_flags = valid_mask.astype(jnp.float32)
    source = jnp.arange(TOKENS, dtype=jnp.int32)[:, None] // TOK_DEV
    slot_count = N_DP * EXPERTS * CAP
    target = jnp.where(slot_index < CAP, (source * EXPERTS + routes) * CAP + slot_index, slot_count).reshape(-1)

    def forward(stream, ln1_gain, ln1_bias, w_qkv, bias_qv, w_attn_out, b_attn_out, ln2_gain, ln2_bias, router, w_expert_in, b_expert_in, w_expert_out, b_expert_out):
        normed_one = low(layer_norm(stream, ln1_gain, ln1_bias))
        bias_full = jnp.stack([bias_qv[0], jnp.zeros_like(bias_qv[0]), bias_qv[1]], axis=0)
        projected = jnp.einsum('td,dcf->tcf', normed_one, w_qkv, precision=HIGHEST) + bias_full
        projected = low(low_back(projected))
        grouped = projected.reshape(-1, IMG_DEV, SEQ, 3, HEADS, HEAD)
        keep_grouped = keep_flags.reshape(-1, IMG_DEV, SEQ)
        mixed_heads = lax.map(jax.checkpoint(attend_group), (grouped, keep_grouped))
        mixed_heads = low(low_back(mixed_heads.reshape(TOKENS, HEADS * HEAD)))
        attention = low_back(jnp.dot(mixed_heads, w_attn_out, precision=HIGHEST) + b_attn_out)
        middle = stream + attention
        normed_two = low(layer_norm(middle, ln2_gain, ln2_bias))
        logits = jnp.dot(normed_two, router, precision=HIGHEST)
        chosen = jnp.take_along_axis(logits, routes, axis=1)
        gate_values = jax.nn.softmax(chosen, axis=-1)
        buffer = jnp.zeros((slot_count + 1, D), jnp.float32).at[target].set(jnp.repeat(normed_two, 2, axis=0))
        buffer = low_back(buffer[:slot_count])
        slot_input = buffer.reshape(N_DP, EXPERTS, CAP, D).transpose(1, 0, 2, 3).reshape(EXPERTS, N_DP * CAP, D)
        pre_act = jnp.einsum('erd,edf->erf', slot_input, w_expert_in, precision=HIGHEST) + b_expert_in[:, None, :]
        pre_act = low_back(pre_act)
        hidden = low(jax.nn.gelu(pre_act))
        slot_output = jnp.einsum('erf,efd->erd', hidden, w_expert_out, precision=HIGHEST) + b_expert_out[:, None, :]
        slot_output = low(low_back(slot_output))
        slot_output = slot_output.reshape(EXPERTS, N_DP, CAP, D).transpose(1, 0, 2, 3).reshape(slot_count, D)
        slot_output = jnp.concatenate([slot_output, jnp.zeros((1, D), jnp.float32)], axis=0)
        arrived = slot_output[target].reshape(TOKENS, 2, D)
        branch = lax.optimization_barrier(jnp.sum(gate_values[:, :, None] * arrived, axis=1))
        output = middle + branch
        return (output, (attention, branch))
    params = tuple((item.astype(jnp.float32) for item in (tokens, ln1_gain, ln1_bias, w_qkv, bias_qv, w_attn_out, b_attn_out, ln2_gain, ln2_bias, router, w_expert_in, b_expert_in, w_expert_out, b_expert_out)))
    output, pullback, extras = jax.vjp(forward, *params, has_aux=True)
    gradients = pullback(grad_out.astype(jnp.float32))
    attention, branch = extras
    keep_col = keep_flags[:, None]
    valid_count = jnp.sum(keep_flags) * D
    rms_values = jnp.stack([jnp.sqrt(jnp.sum(keep_col * item * item) / valid_count) for item in (params[0], attention, branch, output)])
    return (output.astype(jnp.bfloat16), gradients[0], gradients[1], gradients[2], gradients[3], gradients[4], gradients[5], gradients[6], gradients[7], gradients[8], gradients[9], gradients[10], gradients[11], gradients[12], gradients[13], rms_values)
```

```python
import functools
import math

import jax
import jax.numpy as jnp
from jax import lax
from jax.experimental import pallas as pl
from jax.experimental.pallas import tpu as pltpu
from jax.sharding import PartitionSpec as P

HEAD = 64
SEQ = 197
LANE = 128
EPS = 1e-06
ROOT = math.sqrt(2.0 / math.pi)
CUBE = 0.044715
BUNCH = 16
MESH = pl.DeviceIdType.MESH
F32 = jnp.float32
BF16 = jnp.bfloat16
DMA = pltpu.SemaphoreType.DMA


def up_to(value, step):
    return -(-value // step) * step


def dot(a, b):
    return lax.dot_general(a, b, (((1,), (0,)), ((), ())), preferred_element_type=F32)


def dot_bt(a, b):
    return lax.dot_general(a, b, (((1,), (1,)), ((), ())), preferred_element_type=F32)


def dot_at(a, b):
    return lax.dot_general(a, b, (((0,), (0,)), ((), ())), preferred_element_type=F32)


def iota(shape, dim):
    return lax.broadcasted_iota(jnp.int32, shape, dim)


def one(cond, kind=BF16):
    return jnp.where(cond, 1.0, 0.0).astype(kind)


def split(value):
    high = value.astype(BF16)
    return high, (value - high.astype(F32)).astype(BF16)


def norm_parts(values):
    scale = 1.0 / values.shape[-1]
    center = values - jnp.sum(values, axis=-1, keepdims=True) * scale
    inverse = lax.rsqrt(jnp.sum(center * center, axis=-1, keepdims=True) * scale + EPS)
    return center * inverse, inverse


def norm_backward(incoming, normal, inverse, gain_vec):
    scale = 1.0 / incoming.shape[-1]
    scaled = incoming * gain_vec
    return inverse * (
        scaled
        - jnp.sum(scaled, axis=-1, keepdims=True) * scale
        - normal * (jnp.sum(scaled * normal, axis=-1, keepdims=True) * scale)
    )


def remote(src, dst, send_sem, recv_sem, device):
    return pltpu.make_async_remote_copy(
        src_ref=src,
        dst_ref=dst,
        send_sem=send_sem,
        recv_sem=recv_sem,
        device_id=device,
        device_id_type=MESH,
    )


class Sizes:
    def __init__(self, n, tok, width, heads_width, ff, experts):
        self.n = n
        self.tok = tok
        self.tp = up_to(tok, 16)
        self.tk = up_to(tok, LANE)
        self.width = width
        self.hw = heads_width
        self.pairs = heads_width // LANE
        self.ff = ff
        self.experts = experts
        self.cap = 2 * (3 * tok // (2 * n))
        self.main = self.cap // 16 * 16
        self.tail = self.cap - self.main
        self.half = width // 2
        self.blocks = self.half // LANE
        self.msg = self.main * self.blocks + 16
        self.nm = n * self.main
        self.slots = n * self.cap
        self.bt = BUNCH * self.tail
        self.bits = [1 << i for i in range(n.bit_length() - 1)]
        self.chunk = up_to(up_to(heads_width * width // LANE, n) // n, 16)
        self.small_rows = up_to(experts + 7, 16)
        self.small = up_to(up_to(self.small_rows * width // LANE, n) // n, 16)
        fits = 0 < self.tail * self.blocks <= 14 and n % BUNCH == 0
        if not fits or experts != n or (1 << len(self.bits)) != n:
            raise ValueError("unsupported sizes")


def chain_orders(bits):
    k = len(bits)
    if k < 4:
        return [bits] * 4
    a = list(bits)
    return [a, a[1:3] + a[:1] + a[3:], a[2:3] + a[:2] + a[3:], a]


def mega_kernel(
    z,
    tokens_ref,
    grad_out_ref,
    valid_ref,
    routes_ref,
    slots_ref,
    ln1g_ref,
    ln1b_ref,
    wqkv_hbm,
    bqv_ref,
    wo_hbm,
    bo_ref,
    ln2g_ref,
    ln2b_ref,
    router_ref,
    win_hbm,
    bin_ref,
    wout_hbm,
    bout_ref,
    o_tok,
    o_gtok,
    o_x,
    o_sg,
    o_hid,
    o_gp,
    o_red,
    o_small,
    o_bei,
    o_beo,
    o_rms,
    wqkv,
    wo,
    win,
    wout,
    xf,
    normal1,
    n1,
    n1t,
    upk,
    q_s,
    k_s,
    v_s,
    probs,
    mix,
    part,
    part_in,
    mid,
    normal2,
    n2,
    onehot,
    rows8,
    cols8,
    u_s,
    x_s,
    y_s,
    gh,
    pre,
    hid,
    gp,
    sg,
    gcol_s,
    ggv,
    half_out,
    half_in,
    gm,
    ag,
    dm,
    gpr,
    gn_out,
    gn_in,
    smallf,
    stat,
    s_msg,
    r_msg,
    f_msg,
    chain_g,
    chain_small,
    *rest,
):
    nbits = len(z.bits)
    chain_r = rest[:nbits]
    small_r = rest[nbits : 2 * nbits]
    chain_a, small_a, wsem, osem, hs, hr, ss, rs, fs, fr, cs, cr, as_, ar, sts, str_ = rest[
        2 * nbits :
    ]
    n = z.n
    me, core = lax.axis_index("dp"), lax.axis_index("tensor")
    sib = (me, 1 - core)
    tok, tp, tk, width, hw, half = z.tok, z.tp, z.tk, z.width, z.hw, z.half
    mine = pl.multiple_of(core * half, LANE)
    other = pl.multiple_of((1 - core) * half, LANE)

    barrier = pltpu.get_barrier_semaphore()

    def greet(j, carry):
        pl.semaphore_signal(
            barrier, inc=1, device_id=(lax.rem(me + j, n), core), device_id_type=MESH
        )
        return carry

    lax.fori_loop(1, n, greet, 0)
    pl.semaphore_signal(barrier, inc=1, device_id=sib, device_id_type=MESH)

    weights = [
        pltpu.make_async_copy(a, b, wsem.at[i])
        for i, (a, b) in enumerate(
            ((wqkv_hbm, wqkv), (wo_hbm, wo), (wout_hbm, wout), (win_hbm, win))
        )
    ]
    for copy in weights:
        copy.start()

    def a2a_send(i):
        r_msg[i, me] = s_msg[i, me]

        def go(j, carry):
            p = lax.rem(me + j, n)
            remote(
                s_msg.at[i, p], r_msg.at[i, me], ss.at[i, p], rs.at[i, me], (p, core)
            ).start()
            return carry

        lax.fori_loop(1, n, go, 0)
        remote(r_msg.at[i, me], f_msg.at[i, me], fs.at[i, me], fr.at[i, me], sib).start()

    def a2a_forward(i):
        def go(j, carry):
            p = lax.rem(me + n - j, n)
            remote(
                s_msg.at[i, p], r_msg.at[i, p], ss.at[i, p], rs.at[i, p], (p, core)
            ).wait_recv()
            remote(r_msg.at[i, p], f_msg.at[i, p], fs.at[i, p], fr.at[i, p], sib).start()
            return carry

        lax.fori_loop(1, n, go, 0)

    def a2a_finish(i):
        def go(j, carry):
            remote(r_msg.at[i, j], f_msg.at[i, j], fs.at[i, j], fr.at[i, j], sib).wait()
            return carry

        lax.fori_loop(0, n, go, 0)

    def a2a_sent(i):
        def go(j, carry):
            p = lax.rem(me + j, n)
            remote(
                s_msg.at[i, p], r_msg.at[i, me], ss.at[i, p], rs.at[i, me], (p, core)
            ).wait_send()
            return carry

        lax.fori_loop(1, n, go, 0)

    def assemble(i, out):
        tails = []
        for src, at in ((r_msg, mine), (f_msg, other)):
            for b in range(z.blocks):
                lanes = pl.ds(pl.multiple_of(at + b * LANE, LANE), LANE)
                if z.main:
                    rows = src[i, :, b * z.main : (b + 1) * z.main, :]
                    out[0 : z.nm, lanes] = rows.reshape(z.nm, LANE)
            for g in range(n // BUNCH):
                tail = tail_of(i, src, g)
                q, r = iota((z.bt, BUNCH * 16), 0), iota((z.bt, BUNCH * 16), 1)
                base = q // z.tail * 16 + q % z.tail
                for b in range(z.blocks):
                    lanes = pl.ds(pl.multiple_of(at + b * LANE, LANE), LANE)
                    pick = one(r == base + b * z.tail)
                    out[z.nm + g * z.bt : z.nm + (g + 1) * z.bt, lanes] = dot(pick, tail).astype(
                        BF16
                    )

    def tail_of(i, src, g):
        rows = src[i, g * BUNCH : (g + 1) * BUNCH, z.msg - 16 : z.msg, :]
        return rows.reshape(BUNCH * 16, LANE)

    def pack(i, value, extra):
        if z.main:
            for b in range(z.blocks):
                s_msg[i, :, b * z.main : (b + 1) * z.main, :] = value[
                    0 : z.nm, b * LANE : (b + 1) * LANE
                ].reshape(n, z.main, LANE)
        q, r = iota((BUNCH * 16, z.bt), 1), iota((BUNCH * 16, z.bt), 0)
        base = q // z.tail * 16 + q % z.tail
        for g in range(n // BUNCH):
            tail = None if extra is None else extra[g]
            for b in range(z.blocks):
                put = one(r == base + b * z.tail)
                rows = value[z.nm + g * z.bt : z.nm + (g + 1) * z.bt, b * LANE : (b + 1) * LANE]
                piece = dot(put, rows)
                tail = piece if tail is None else tail + piece
            s_msg[i, g * BUNCH : (g + 1) * BUNCH, z.msg - 16 : z.msg, :] = tail.astype(
                BF16
            ).reshape(BUNCH, 16, LANE)

    gate_row = 14

    rows8[...] = jnp.full(rows8.shape, -1.0, F32)
    rows8[0:2, 0:tok] = routes_ref[...].astype(F32)
    rows8[2:4, 0:tok] = slots_ref[...].astype(F32)
    rows8[4:5, 0:tok] = valid_ref[...].astype(F32)
    table = rows8[...]
    r_row = [table[k : k + 1, :].astype(jnp.int32) for k in range(2)]
    j_row = [table[2 + k : 3 + k, :].astype(jnp.int32) for k in range(2)]
    keep_row = table[4:5, :] > 0.5

    def targets(r, j):
        sent = (r >= 0) & (j < z.cap)
        flat = jnp.where(j < z.main, r * z.main + j, z.nm + r * z.tail + (j - z.main))
        return sent, jnp.where(sent, flat, -1)

    sent_row, flat_row = zip(*[targets(r, j) for r, j in zip(r_row, j_row)])
    cols8[...] = jnp.transpose(table)
    r_col = [cols8[0:tp, k : k + 1].astype(jnp.int32) for k in range(2)]
    j_col = [cols8[0:tp, 2 + k : 3 + k].astype(jnp.int32) for k in range(2)]
    keep_col = jnp.where(cols8[0:tp, 4:5] > 0.5, 1.0, 0.0)
    sent_col, flat_col = zip(*[targets(r, j) for r, j in zip(r_col, j_col)])

    slot_id = iota((z.slots, tk), 0)
    onehot[...] = one((slot_id == flat_row[0]) | (slot_id == flat_row[1]))
    tail_id = iota((BUNCH * 16, tk), 0)
    tail_row = [
        jnp.where(s & (j >= z.main), r * 16 + (j - z.main), -1000)
        for s, r, j in zip(sent_row, r_row, j_row)
    ]

    def place(src, i, extra):
        if z.main:
            for b in range(z.blocks):
                lanes = pl.ds(pl.multiple_of(mine + b * LANE, LANE), LANE)
                rows = dot(onehot[0 : z.nm, :], src[:, lanes]).astype(BF16)
                s_msg[i, :, b * z.main : (b + 1) * z.main, :] = rows.reshape(n, z.main, LANE)
        for g in range(n // BUNCH):
            tail = None if extra is None else extra[g]
            for b in range(z.blocks):
                lanes = pl.ds(pl.multiple_of(mine + b * LANE, LANE), LANE)
                at = b * z.tail - g * BUNCH * 16
                put = one((tail_id == tail_row[0] + at) | (tail_id == tail_row[1] + at))
                piece = dot(put, src[:, lanes])
                tail = piece if tail is None else tail + piece
            s_msg[i, g * BUNCH : (g + 1) * BUNCH, z.msg - 16 : z.msg, :] = tail.astype(
                BF16
            ).reshape(BUNCH, 16, LANE)

    upk[tok // 16 * 16 :, :] = jnp.zeros((tk - tok // 16 * 16, width), BF16)
    upk[0:tok, :] = grad_out_ref[...]
    place(upk, 0, None)

    xf[tok // 8 * 8 :, :] = jnp.zeros((tp - tok // 8 * 8, width), F32)
    xf[0:tok, :] = tokens_ref[...].astype(F32)
    normal, inverse1 = norm_parts(xf[...])
    normal1[...] = normal
    n1[tp:, :] = jnp.zeros((tk - tp, width), BF16)
    n1[0:tp, :] = (normal * ln1g_ref[...] + ln1b_ref[...]).astype(BF16)

    pl.semaphore_wait(barrier, n)
    a2a_send(0)

    weights[0].wait()
    for c, (dst, bias) in enumerate(((q_s, bqv_ref[0:1, :]), (k_s, None), (v_s, bqv_ref[1:2, :]))):
        value = dot(n1[0:tp, :], wqkv[c])
        if bias is not None:
            value = value + bias
        dst[tp:, :] = jnp.zeros((tk - tp, hw), BF16)
        dst[0:tp, :] = value.astype(BF16)

    score_scale = 1.0 / math.sqrt(HEAD)
    low_lane = iota((1, LANE), 1) < HEAD
    head_mask = [one(low_lane), one(jnp.logical_not(low_lane))]
    for p in range(z.pairs):
        lanes = slice(p * LANE, (p + 1) * LANE)
        qp, kp, vp = q_s[0:tp, lanes], k_s[:, lanes], v_s[:, lanes]
        outs = []
        for h in range(2):
            scores = dot_bt(qp * head_mask[h], kp) * score_scale
            scores = jnp.where(keep_row, scores, -1000000000.0)
            weights_h = jnp.exp(scores - jnp.max(scores, axis=-1, keepdims=True))
            prob = weights_h / jnp.sum(weights_h, axis=-1, keepdims=True)
            probs[2 * p + h] = prob
            outs.append(dot(prob.astype(BF16), vp))
        mix[0:tp, lanes] = jnp.where(low_lane, outs[0], outs[1]).astype(BF16)
    mix[tp:, :] = jnp.zeros((tk - tp, hw), BF16)
    weights[1].wait()
    part[...] = dot(mix[0:tp, :], wo[...])
    swap = remote(part, part_in, hs.at[0], hr.at[0], sib)
    swap.start()
    n1t[...] = jnp.transpose(n1[...])
    swap.wait()

    attention = part[...] + part_in[...] + bo_ref[...]
    stat_attn = jnp.sum(keep_col * attention * attention)
    middle = xf[...] + attention
    mid[...] = middle
    normal, inverse2 = norm_parts(middle)
    normal2[...] = normal
    n2[tp:, :] = jnp.zeros((tk - tp, width), BF16)
    n2[0:tp, :] = (normal * ln2g_ref[...] + ln2b_ref[...]).astype(BF16)
    logits = dot_bt(router_ref[...], n2[...])
    expert_id = iota((z.experts, tk), 0)
    chosen = [
        jnp.sum(jnp.where(expert_id == r, logits, 0.0), axis=0, keepdims=True) for r in r_row
    ]
    top = jnp.maximum(chosen[0], chosen[1])
    raw = [jnp.exp(c - top) for c in chosen]
    total = raw[0] + raw[1]
    gate_rows = [r / total for r in raw]
    cols8[0:tk, :] = jnp.transpose(
        jnp.concatenate(gate_rows + [jnp.zeros((6, tk), F32)], axis=0)
    )
    gate = [cols8[0:tp, k : k + 1] for k in range(2)]

    slot_lane = iota((tk, LANE), 1)
    numbers = []
    pad_col = [
        jnp.concatenate([j, jnp.full((tk - tp, 1), -1, jnp.int32)], axis=0) for j in j_col
    ]
    for g in range(n // BUNCH):
        number = None
        for k in range(2):
            high, low = split(gate_rows[k])
            at = r_row[k] * 16 + (gate_row - g * BUNCH * 16)
            lift = jnp.where(
                sent_row[k] & (tail_id == at), high.astype(F32), 0.0
            ) + jnp.where(sent_row[k] & (tail_id == at + 1), low.astype(F32), 0.0)
            piece = dot(lift.astype(BF16), one(slot_lane == pad_col[k]))
            number = piece if number is None else number + piece
        numbers.append(number)
    place(n2, 1, numbers)
    a2a_send(1)

    a2a_forward(0)
    a2a_finish(0)
    assemble(0, u_s)
    weights[2].wait()
    gh[...] = dot_bt(u_s[...], wout[...])

    weights[3].wait()
    a2a_forward(1)
    a2a_finish(1)
    assemble(1, x_s)

    def numbered(rows, per, first):
        q, r = iota((rows, BUNCH * 16), 0), iota((rows, BUNCH * 16), 1)
        pick = r == q // per * 16 + gate_row
        lane = iota((rows, LANE), 1) == iota((rows, LANE), 0) % per + first
        return pick, r == q // per * 16 + gate_row + 1, lane

    parts = [(0, BUNCH * z.main, z.main, 0)] if z.main else []
    parts += [(z.nm, z.bt, z.tail, z.main)]
    for g in range(n // BUNCH):
        tail = tail_of(1, r_msg, g)
        for at, rows, per, first in parts:
            high, low, lane = numbered(rows, per, first)
            picked = dot(one(high | low), tail)
            gcol_s[at + g * rows : at + (g + 1) * rows, :] = jnp.sum(
                jnp.where(lane, picked, 0.0), axis=-1, keepdims=True
            )
    pre[...] = dot(x_s[...], win[...])
    step = 16

    def activate(i, carry):
        rows = pl.ds(pl.multiple_of(i * step, step), step)
        v = pre[rows, :] + bin_ref[...]
        v2 = v * v
        t = jnp.tanh(ROOT * v * (1.0 + CUBE * v2))
        half_sum = 0.5 + 0.5 * t
        act = v * half_sum
        back = half_sum + (0.5 * ROOT) * v * (1.0 - t * t) * (1.0 + (3.0 * CUBE) * v2)
        g = gh[rows, :]
        hid[rows, :] = act.astype(BF16)
        gp[rows, :] = (gcol_s[rows, :] * g * back).astype(BF16)
        ggv[rows, :] = jnp.sum(g * act, axis=-1, keepdims=True)
        return carry

    lax.fori_loop(0, z.slots // step, activate, 0)

    half_out[0] = dot_bt(gp[...], win[pl.ds(other, half), :])
    swap = remote(half_out.at[0], half_in.at[0], hs.at[1], hr.at[1], sib)
    swap.start()
    own = dot_bt(gp[...], win[pl.ds(mine, half), :])
    bias_half = bout_ref[:, pl.ds(mine, half)]
    gg = ggv[...] + jnp.sum(
        u_s[:, pl.ds(mine, half)].astype(F32) * bias_half, axis=-1, keepdims=True
    )
    numbers = []
    for g in range(n // BUNCH):
        number = None
        for at, rows, per, first in parts:
            q, r = iota((BUNCH * 16, rows), 1), iota((BUNCH * 16, rows), 0)
            lane = iota((rows, LANE), 1) == iota((rows, LANE), 0) % per + first
            high, low = split(jnp.where(lane, gg[at + g * rows : at + (g + 1) * rows, :], 0.0))
            piece = dot(one(r == q // per * 16 + gate_row), high) + dot(
                one(r == q // per * 16 + gate_row + 1), low
            )
            number = piece if number is None else number + piece
        numbers.append(number)
    swap.wait()
    pack(2, (own + half_in[0]).astype(BF16), numbers)
    a2a_send(2)

    half_out[1] = dot(hid[...], wout[:, pl.ds(other, half)])
    swap = remote(half_out.at[1], half_in.at[1], hs.at[2], hr.at[2], sib)
    swap.start()
    own = dot(hid[...], wout[:, pl.ds(mine, half)]) + bias_half
    swap.wait()
    pack(3, (own + half_in[1]).astype(BF16), None)
    a2a_send(3)

    sg[...] = (gcol_s[...] * u_s[...].astype(F32)).astype(BF16)
    o_beo[...] = jnp.sum(sg[...].astype(F32), axis=0, keepdims=True)
    o_bei[...] = jnp.sum(gp[...].astype(F32), axis=0, keepdims=True)
    stores = [
        pltpu.make_async_copy(a, b, osem.at[i])
        for i, (a, b) in enumerate(((x_s, o_x), (sg, o_sg), (hid, o_hid), (gp, o_gp)))
    ]
    for copy in stores:
        copy.start()
    mix_t = jnp.transpose(mix[...])

    flat_id = iota((tp, z.slots), 1)
    back_one = [one(flat_id == f) for f in flat_col]
    a2a_forward(2)
    a2a_finish(2)
    assemble(2, y_s)
    tail_lane = iota((tp, BUNCH * 16), 1)
    grad_gate = []
    for k in range(2):
        row = None
        for g in range(n // BUNCH):
            at = r_col[k] * 16 + (gate_row - g * BUNCH * 16)
            pick = one(sent_col[k] & ((tail_lane == at) | (tail_lane == at + 1)))
            piece = dot(pick, tail_of(2, r_msg, g)) + dot(pick, tail_of(2, f_msg, g))
            row = piece if row is None else row + piece
        row = jnp.where(iota((tp, LANE), 1) == j_col[k], row, 0.0)
        grad_gate.append(jnp.sum(row, axis=-1, keepdims=True))
    mean_gate = gate[0] * grad_gate[0] + gate[1] * grad_gate[1]
    e_pad = up_to(z.experts, LANE)
    e_lane = iota((tp, e_pad), 1)
    grad_logits = jnp.where(
        e_lane == r_col[0], gate[0] * (grad_gate[0] - mean_gate), 0.0
    ) + jnp.where(e_lane == r_col[1], gate[1] * (grad_gate[1] - mean_gate), 0.0)
    gl_high, gl_low = split(grad_logits)
    router_pad = router_ref[...]
    if e_pad > z.experts:
        router_pad = jnp.concatenate(
            [router_pad, jnp.zeros((e_pad - z.experts, width), BF16)], axis=0
        )
    grad_n2 = (
        dot(back_one[0] + back_one[1], y_s[...])
        + dot(gl_high, router_pad)
        + dot(gl_low, router_pad)
    )
    grad_router = dot_at(gl_high, n2[0:tp, :]) + dot_at(gl_low, n2[0:tp, :])
    smallf[...] = jnp.zeros(smallf.shape, F32)
    ne = z.experts
    smallf[0:ne, :] = grad_router[0:ne, :]
    normal = normal2[...]
    smallf[ne + 2 : ne + 3, :] = jnp.sum(grad_n2 * normal, axis=0, keepdims=True)
    smallf[ne + 3 : ne + 4, :] = jnp.sum(grad_n2, axis=0, keepdims=True)
    gm[...] = upk[0:tp, :].astype(F32) + norm_backward(grad_n2, normal, inverse2, ln2g_ref[...])
    ag[tp:, :] = jnp.zeros((tk - tp, width), BF16)
    ag[0:tp, :] = gm[...].astype(BF16)
    smallf[ne + 4 : ne + 5, :] = jnp.sum(ag[...].astype(F32), axis=0, keepdims=True)

    groups = []
    for order in chain_orders(z.bits) + [z.bits]:
        start, size, steps = 0, n, []
        for b in order:
            bit = lax.rem(me // b, 2)
            peer = me + b * (1 - 2 * bit)
            size = size // 2
            steps.append((peer, start + (1 - bit) * size, start + bit * size, size))
            start = start + bit * size
        groups.append((steps, start))
    n_main = len(groups) - 1

    def chain_of(g):
        if g < n_main:
            return chain_g.at[g], [r.at[g] for r in chain_r], chain_a.at[g], z.chunk
        return chain_small, list(small_r), small_a, z.small

    def region(ref, at, count, rows):
        return ref.at[pl.ds(pl.multiple_of(at * rows, 16), count * rows)]

    def rs_copy(g, s):
        src, bufs, _, rows = chain_of(g)
        peer, give, _, size = groups[g][0][s]
        return remote(
            region(src, give, size, rows), bufs[s], cs.at[g, s], cr.at[g, s], (peer, core)
        )

    def rs_add(g, s, at, count, dst):
        src, bufs, _, rows = chain_of(g)
        keep = groups[g][0][s][2]

        def go(i, carry):
            here = pl.ds(pl.multiple_of((at + i) * rows, 16), rows)
            there = pl.ds(pl.multiple_of((at + i - keep) * rows, 16), rows)
            dst[here, :] = (src[here, :].astype(F32) + bufs[s][there, :].astype(F32)).astype(BF16)
            return carry

        lax.fori_loop(0, count, go, 0)

    def rs_step(g, s):
        src, _, out, _ = chain_of(g)
        rs_copy(g, s).wait()
        if s + 1 < nbits:
            _, give, keep, size = groups[g][0][s + 1]
            rs_add(g, s, give, size, src)
            rs_copy(g, s + 1).start()
            rs_add(g, s, keep, size, src)
        else:
            rs_add(g, s, groups[g][1], 1, out)
            ag_copy(g, s).start()

    def ag_copy(g, s):
        _, _, out, rows = chain_of(g)
        peer, _, keep, size = groups[g][0][s]
        piece = region(out, keep, size, rows)
        return remote(piece, piece, as_.at[g, s], ar.at[g, s], (peer, core))

    def ag_step(g, s):
        _, _, out, rows = chain_of(g)
        peer, give, _, size = groups[g][0][s]
        ag_copy(g, s).wait_send()
        piece = region(out, give, size, rows)
        remote(piece, piece, as_.at[g, s], ar.at[g, s], (peer, core)).wait_recv()
        if s > 0:
            ag_copy(g, s - 1).start()

    def fill(g, value, row):
        for b in range(value.shape[1] // LANE):
            chain_g[g, row : row + value.shape[0], :] = value[
                :, b * LANE : (b + 1) * LANE
            ].astype(BF16)
            row += value.shape[0]
        return row

    pad_from = hw * width // LANE
    if pad_from < n * z.chunk:
        for g in range(n_main):
            chain_g[g, pad_from:, :] = jnp.zeros((n * z.chunk - pad_from, LANE), BF16)
    fill(0, dot(mix_t, ag[...]), 0)
    rs_copy(0, 0).start()

    dm[...] = dot_bt(ag[0:tp, :], wo[...]).astype(BF16)
    for p in range(z.pairs):
        lanes = slice(p * LANE, (p + 1) * LANE)
        qp, kp, vp, dp = q_s[0:tp, lanes], k_s[:, lanes], v_s[:, lanes], dm[:, lanes]
        dq, dk, dv = [], [], []
        for h in range(2):
            prob = probs[2 * p + h]
            gprob = dot_bt(dp * head_mask[h], vp)
            inner = jnp.sum(prob * gprob, axis=-1, keepdims=True)
            gs = (prob * (gprob - inner)).astype(BF16)
            dq.append(dot(gs, kp))
            dk.append(dot_at(gs, qp))
            dv.append(dot_at(prob.astype(BF16), dp))
        for c, (pair, scale) in enumerate(((dq, score_scale), (dk, score_scale), (dv, 1.0))):
            value = (jnp.where(low_lane, pair[0], pair[1]) * scale).astype(BF16)
            at = slice(c * hw + p * LANE, c * hw + (p + 1) * LANE)
            if c == 0:
                gpr[0:tp, at] = value
                gpr[tp:, at] = jnp.zeros((tk - tp, LANE), BF16)
            else:
                gpr[:, at] = value
        joined = jnp.concatenate(
            [gpr[:, c * hw + p * LANE : c * hw + (p + 1) * LANE] for c in range(3)], axis=1
        )
        fill(1 + p, dot(n1t[...], joined), 0)
        rs_copy(1 + p, 0).start()

    head_part = None
    for c in range(3):
        piece = dot_bt(gpr[0:tp, c * hw : (c + 1) * hw], wqkv[c])
        head_part = piece if head_part is None else head_part + piece
    gn_out[...] = head_part.astype(BF16)
    swap = remote(gn_out, gn_in, hs.at[3], hr.at[3], sib)
    swap.start()
    smallf[ne + 5 : ne + 6, 0:hw] = jnp.sum(gpr[:, 0:hw].astype(F32), axis=0, keepdims=True)
    smallf[ne + 6 : ne + 7, 0:hw] = jnp.sum(
        gpr[:, 2 * hw : 3 * hw].astype(F32), axis=0, keepdims=True
    )
    swap.wait()
    grad_n1 = gn_out[...].astype(F32) + gn_in[...].astype(F32)
    normal = normal1[...]
    smallf[ne : ne + 1, :] = jnp.sum(grad_n1 * normal, axis=0, keepdims=True)
    smallf[ne + 1 : ne + 2, :] = jnp.sum(grad_n1, axis=0, keepdims=True)
    back = gm[...] + norm_backward(grad_n1, normal, inverse1, ln1g_ref[...])
    o_gtok[...] = back[0:tok, :]
    used = z.small_rows * (width // LANE)
    for b in range(width // LANE):
        chain_small[b * z.small_rows : (b + 1) * z.small_rows, :] = smallf[
            :, b * LANE : (b + 1) * LANE
        ].astype(BF16)
    if used < n * z.small:
        chain_small[used:, :] = jnp.zeros((n * z.small - used, LANE), BF16)
    rs_copy(n_main, 0).start()

    a2a_forward(3)
    a2a_finish(3)
    assemble(3, y_s)
    branch = gate[0] * dot(back_one[0], y_s[...]) + gate[1] * dot(back_one[1], y_s[...])
    output = mid[...] + branch
    o_tok[...] = output[0:tok, :].astype(BF16)
    lane_id = iota((1, LANE), 1)
    x_all = xf[...]
    line = jnp.zeros((1, LANE), F32)
    for i, number in enumerate(
        (
            jnp.sum(keep_col * x_all * x_all),
            stat_attn,
            jnp.sum(keep_col * branch * branch),
            jnp.sum(keep_col * output * output),
            jnp.sum(keep_col),
        )
    ):
        line = jnp.where(lane_id == i, number, line)
    stat[me] = jnp.broadcast_to(line, (8, LANE))

    def stat_go(j, carry):
        p = lax.rem(me + j, n)
        remote(stat.at[me], stat.at[me], sts.at[p], str_.at[me], (p, core)).start()
        return carry

    lax.fori_loop(1, n, stat_go, 0)

    for s in range(nbits):
        for g in range(n_main + 1):
            rs_step(g, s)

    def stat_wait(j, carry):
        p = lax.rem(me + j, n)
        remote(stat.at[me], stat.at[me], sts.at[p], str_.at[me], (p, core)).wait_send()
        remote(stat.at[p], stat.at[p], sts.at[p], str_.at[p], (p, core)).wait_recv()
        return carry

    lax.fori_loop(1, n, stat_wait, 0)
    totals = jnp.sum(stat[...], axis=0)
    count = jnp.sum(jnp.where(iota((8, LANE), 1) == 4, totals, 0.0), axis=-1, keepdims=True)
    o_rms[...] = jnp.sqrt(totals / (count * width))

    for s in range(nbits - 1, -1, -1):
        for g in range(n_main + 1):
            ag_step(g, s)
    for g in range(n_main):
        copy = pltpu.make_async_copy(chain_a.at[g], o_red.at[g], osem.at[4 + g])
        copy.start()
        stores.append(copy)
    for b in range(width // LANE):
        o_small[:, b * LANE : (b + 1) * LANE] = small_a[
            b * z.small_rows : (b + 1) * z.small_rows, :
        ].astype(F32)
    for i in range(4):
        a2a_sent(i)
    for copy in stores:
        copy.wait()


def per_device(
    tokens,
    grad_out,
    valid_mask,
    routes,
    slot_index,
    ln1_gain,
    ln1_bias,
    w_qkv,
    bias_qv,
    w_attn_out,
    b_attn_out,
    ln2_gain,
    ln2_bias,
    router,
    w_expert_in,
    b_expert_in,
    w_expert_out,
    b_expert_out,
):
    tok, width = tokens.shape
    hw = w_qkv.shape[2]
    ff = w_expert_in.shape[2]
    z = Sizes(lax.axis_size("dp"), tok, width, hw, ff, router.shape[1])
    n, tp, tk = z.n, z.tp, z.tk
    nbits = len(z.bits)
    vmem = pl.BlockSpec(memory_space=pltpu.VMEM)
    any_ = pl.BlockSpec(memory_space=pl.ANY)
    shape = jax.ShapeDtypeStruct
    groups = 1 + z.pairs
    V = pltpu.VMEM
    scratch = [
        V((3, width, hw), BF16),
        V((hw, width), BF16),
        V((width, ff), BF16),
        V((ff, width), BF16),
        V((tp, width), F32),
        V((tp, width), F32),
        V((tk, width), BF16),
        V((width, tk), BF16),
        V((tk, width), BF16),
        V((tk, hw), BF16),
        V((tk, hw), BF16),
        V((tk, hw), BF16),
        V((2 * z.pairs, tp, tk), F32),
        V((tk, hw), BF16),
        V((tp, width), F32),
        V((tp, width), F32),
        V((tp, width), F32),
        V((tp, width), F32),
        V((tk, width), BF16),
        V((z.slots, tk), BF16),
        V((8, tk), F32),
        V((tk, 8), F32),
        V((z.slots, width), BF16),
        V((z.slots, width), BF16),
        V((z.slots, width), BF16),
        V((z.slots, ff), F32),
        V((z.slots, ff), F32),
        V((z.slots, ff), BF16),
        V((z.slots, ff), BF16),
        V((z.slots, width), BF16),
        V((z.slots, 1), F32),
        V((z.slots, 1), F32),
        V((2, z.slots, z.half), F32),
        V((2, z.slots, z.half), F32),
        V((tp, width), F32),
        V((tk, width), BF16),
        V((tp, hw), BF16),
        V((tk, 3 * hw), BF16),
        V((tp, width), BF16),
        V((tp, width), BF16),
        V((z.small_rows, width), F32),
        V((n, 8, LANE), F32),
        V((4, n, z.msg, LANE), BF16),
        V((4, n, z.msg, LANE), BF16),
        V((4, n, z.msg, LANE), BF16),
        V((groups, n * z.chunk, LANE), BF16),
        V((n * z.small, LANE), BF16),
    ]
    scratch += [V((groups, (n >> (s + 1)) * z.chunk, LANE), BF16) for s in range(nbits)]
    scratch += [V(((n >> (s + 1)) * z.small, LANE), BF16) for s in range(nbits)]
    scratch += [
        V((groups, n * z.chunk, LANE), BF16),
        V((n * z.small, LANE), BF16),
        DMA((4,)),
        DMA((4 + groups,)),
        DMA((4,)),
        DMA((4,)),
        DMA((4, n)),
        DMA((4, n)),
        DMA((4, n)),
        DMA((4, n)),
        DMA((groups + 1, nbits)),
        DMA((groups + 1, nbits)),
        DMA((groups + 1, nbits)),
        DMA((groups + 1, nbits)),
        DMA((n,)),
        DMA((n,)),
    ]
    row = lambda v: v.reshape(1, -1)
    outs = pl.pallas_call(
        functools.partial(mega_kernel, z),
        out_shape=(
            shape((tok, width), BF16),
            shape((tok, width), F32),
            shape((z.slots, width), BF16),
            shape((z.slots, width), BF16),
            shape((z.slots, ff), BF16),
            shape((z.slots, ff), BF16),
            shape((groups, n * z.chunk, LANE), BF16),
            shape((z.small_rows, width), F32),
            shape((1, ff), F32),
            shape((1, width), F32),
            shape((8, LANE), F32),
        ),
        in_specs=[vmem] * 7
        + [any_, vmem, any_, vmem, vmem, vmem, vmem, any_, vmem, any_, vmem],
        out_specs=(vmem, vmem, any_, any_, any_, any_, any_, vmem, vmem, vmem, vmem),
        scratch_shapes=scratch,
        compiler_params=pltpu.CompilerParams(
            collective_id=0, has_side_effects=True, vmem_limit_bytes=60 * 2**20
        ),
    )(
        tokens,
        grad_out,
        row(valid_mask),
        routes.T,
        slot_index.T,
        row(ln1_gain),
        row(ln1_bias),
        jnp.transpose(w_qkv, (1, 0, 2)),
        bias_qv,
        w_attn_out,
        row(b_attn_out),
        row(ln2_gain),
        row(ln2_bias),
        router.T,
        w_expert_in[0],
        b_expert_in,
        w_expert_out[0],
        b_expert_out,
    )
    o_tok, o_gtok, o_x, o_sg, o_hid, o_gp, o_red, o_small, o_bei, o_beo, o_rms = outs
    gwin = lax.dot_general(
        o_x, o_gp, (((0,), (0,)), ((), ())), preferred_element_type=F32
    )
    gwout = lax.dot_general(
        o_hid, o_sg, (((0,), (0,)), ((), ())), preferred_element_type=F32
    )
    used = hw * width // LANE
    red = o_red[:, :used].astype(F32)
    gwo = jnp.transpose(red[0].reshape(width // LANE, hw, LANE), (1, 0, 2)).reshape(hw, width)
    gq = red[1:].reshape(z.pairs, 3, width, LANE)
    gwqkv = jnp.transpose(gq, (2, 1, 0, 3)).reshape(width, 3, hw)
    ne = z.experts
    return (
        o_tok,
        o_gtok,
        o_small[ne],
        o_small[ne + 1],
        gwqkv,
        o_small[ne + 5 : ne + 7, :hw],
        gwo,
        o_small[ne + 4],
        o_small[ne + 2],
        o_small[ne + 3],
        o_small[:ne].T,
        gwin[None],
        o_bei,
        gwout[None],
        o_beo,
        o_rms[0, :4],
    )


def solution(mesh):
    return jax.shard_map(
        per_device,
        mesh=mesh,
        in_specs=(
            P("dp", None),
            P("dp", None),
            P("dp"),
            P("dp", None),
            P("dp", None),
            P(),
            P(),
            P(None, None, "tensor"),
            P(None, "tensor"),
            P("tensor", None),
            P(),
            P(),
            P(),
            P(),
            P("dp", None, "tensor"),
            P("dp", "tensor"),
            P("dp", "tensor", None),
            P("dp", None),
        ),
        out_specs=(
            P("dp", None),
            P("dp", None),
            P(),
            P(),
            P(None, None, "tensor"),
            P(None, "tensor"),
            P("tensor", None),
            P(),
            P(),
            P(),
            P(),
            P("dp", None, "tensor"),
            P("dp", "tensor"),
            P("dp", "tensor", None),
            P("dp", None),
            P(),
        ),
        check_vma=False,
    )
```

```python
import functools
import math

import jax
import jax.numpy as jnp
from jax import lax
from jax.experimental import pallas as pl
from jax.experimental.pallas import tpu as pltpu
from jax.sharding import PartitionSpec as P

HEAD = 64
SEQ = 197
LANE = 128
EPS = 1e-06
ROOT = math.sqrt(2.0 / math.pi)
CUBE = 0.044715
BUNCH = 16
TILE = 256
MESH = pl.DeviceIdType.MESH
F32 = jnp.float32
BF16 = jnp.bfloat16
DMA = pltpu.SemaphoreType.DMA


def up_to(value, step):
    return -(-value // step) * step


def dot(a, b):
    return lax.dot_general(a, b, (((1,), (0,)), ((), ())), preferred_element_type=F32)


def dot_bt(a, b):
    return lax.dot_general(a, b, (((1,), (1,)), ((), ())), preferred_element_type=F32)


def dot_at(a, b):
    return lax.dot_general(a, b, (((0,), (0,)), ((), ())), preferred_element_type=F32)


def row_of(ref):
    return ref[...].reshape(1, ref.shape[0])


def iota(shape, dim):
    return lax.broadcasted_iota(jnp.int32, shape, dim)


def one(cond, kind=BF16):
    return jnp.where(cond, 1.0, 0.0).astype(kind)


def split(value):
    high = value.astype(BF16)
    return high, (value - high.astype(F32)).astype(BF16)


def norm_parts(values):
    scale = 1.0 / values.shape[-1]
    center = values - jnp.sum(values, axis=-1, keepdims=True) * scale
    inverse = lax.rsqrt(jnp.sum(center * center, axis=-1, keepdims=True) * scale + EPS)
    return center * inverse, inverse


def norm_backward(incoming, normal, inverse, gain_vec):
    scale = 1.0 / incoming.shape[-1]
    scaled = incoming * gain_vec
    return inverse * (
        scaled
        - jnp.sum(scaled, axis=-1, keepdims=True) * scale
        - normal * (jnp.sum(scaled * normal, axis=-1, keepdims=True) * scale)
    )


def remote(src, dst, send_sem, recv_sem, device):
    return pltpu.make_async_remote_copy(
        src_ref=src,
        dst_ref=dst,
        send_sem=send_sem,
        recv_sem=recv_sem,
        device_id=device,
        device_id_type=MESH,
    )


class Sizes:
    def __init__(self, n, tok, width, heads_width, ff, experts):
        self.n = n
        self.tok = tok
        self.tp = up_to(tok, 16)
        self.tk = up_to(tok, LANE)
        self.width = width
        self.hw = heads_width
        self.pairs = heads_width // LANE
        self.ff = ff
        self.experts = experts
        self.cap = 2 * (3 * tok // (2 * n))
        self.main = self.cap // 16 * 16
        self.tail = self.cap - self.main
        self.half = width // 2
        self.blocks = self.half // LANE
        self.msg = self.main * self.blocks + 16
        self.nm = n * self.main
        self.slots = n * self.cap
        self.bt = BUNCH * self.tail
        self.bits = [1 << i for i in range(n.bit_length() - 1)]
        self.pack_rows = 4 * heads_width * width // LANE
        self.chains = 6
        self.chain_rows = self.pack_rows // self.chains
        self.chunk = up_to(up_to(self.chain_rows, n) // n, 16)
        self.small_rows = up_to(experts + 7, 16)
        self.small = up_to(up_to(self.small_rows * width // LANE, n) // n, 16)
        fits = 0 < self.tail * self.blocks <= 14 and n % BUNCH == 0
        fits = fits and self.chain_rows % heads_width == 0 and self.chain_rows % width == 0
        if not fits or experts != n or (1 << len(self.bits)) != n:
            raise ValueError("unsupported sizes")


def chain_orders(bits):
    k = len(bits)
    if k < 3:
        return [bits] * 6
    order = ((0, 1, 2), (1, 2, 0), (2, 0, 1), (0, 2, 1), (1, 0, 2), (2, 1, 0))
    return [[bits[i] for i in head] + bits[3:] for head in order]


def mega_kernel(
    z,
    tokens_ref,
    grad_out_ref,
    valid_ref,
    routes_ref,
    slots_ref,
    ln1g_ref,
    ln1b_ref,
    wqkv_hbm,
    bqv_ref,
    wo_hbm,
    bo_ref,
    ln2g_ref,
    ln2b_ref,
    router_ref,
    win_hbm,
    bin_ref,
    wout_hbm,
    bout_ref,
    o_tok,
    o_gtok,
    o_x,
    o_sg,
    o_hid,
    o_gp,
    o_red,
    o_small,
    o_bei,
    o_beo,
    o_rms,
    wqkv,
    wo,
    win,
    wout,
    xf,
    normal1,
    n1,
    n1t,
    upk,
    q_s,
    k_s,
    v_s,
    probs,
    mix,
    part,
    part_in,
    mid,
    normal2,
    n2,
    onehot,
    rows8,
    cols8,
    u_s,
    x_s,
    y_s,
    gh,
    pre,
    hid,
    gp,
    sg,
    x_t,
    hid_t,
    gcol_s,
    ggv,
    half_out,
    half_in,
    gm,
    ag,
    dm,
    gpr,
    gn_out,
    gn_in,
    smallf,
    stat,
    s_msg,
    r_msg,
    f_msg,
    chain_g,
    chain_small,
    *rest,
):
    nbits = len(z.bits)
    chain_r = rest[:nbits]
    small_r = rest[nbits : 2 * nbits]
    chain_a, small_a, wsem, osem, hs, hr, ss, rs, fs, fr, cs, cr, as_, ar, sts, str_ = rest[
        2 * nbits :
    ]
    n = z.n
    me, core = lax.axis_index("dp"), lax.axis_index("tensor")
    sib = (me, 1 - core)
    tok, tp, tk, width, hw, half = z.tok, z.tp, z.tk, z.width, z.hw, z.half
    mine = pl.multiple_of(core * half, LANE)
    other = pl.multiple_of((1 - core) * half, LANE)

    barrier = pltpu.get_barrier_semaphore()

    def greet(j, carry):
        pl.semaphore_signal(
            barrier, inc=1, device_id=(lax.rem(me + j, n), core), device_id_type=MESH
        )
        return carry

    lax.fori_loop(1, n, greet, 0)
    pl.semaphore_signal(barrier, inc=1, device_id=sib, device_id_type=MESH)

    weights = [
        pltpu.make_async_copy(a, b, wsem.at[i])
        for i, (a, b) in enumerate(
            ((wqkv_hbm, wqkv), (wo_hbm, wo), (wout_hbm, wout), (win_hbm, win))
        )
    ]
    for copy in weights:
        copy.start()

    def a2a_send(i):
        r_msg[i, me] = s_msg[i, me]

        def go(j, carry):
            p = lax.rem(me + j, n)
            remote(
                s_msg.at[i, p], r_msg.at[i, me], ss.at[i, p], rs.at[i, me], (p, core)
            ).start()
            return carry

        lax.fori_loop(1, n, go, 0)
        remote(r_msg.at[i, me], f_msg.at[i, me], fs.at[i, me], fr.at[i, me], sib).start()

    def a2a_forward(i):
        def go(j, carry):
            p = lax.rem(me + n - j, n)
            remote(
                s_msg.at[i, p], r_msg.at[i, p], ss.at[i, p], rs.at[i, p], (p, core)
            ).wait_recv()
            remote(r_msg.at[i, p], f_msg.at[i, p], fs.at[i, p], fr.at[i, p], sib).start()
            return carry

        lax.fori_loop(1, n, go, 0)

    def a2a_finish(i):
        def go(j, carry):
            remote(r_msg.at[i, j], f_msg.at[i, j], fs.at[i, j], fr.at[i, j], sib).wait()
            return carry

        lax.fori_loop(0, n, go, 0)

    def a2a_sent(i):
        def go(j, carry):
            p = lax.rem(me + j, n)
            remote(
                s_msg.at[i, p], r_msg.at[i, me], ss.at[i, p], rs.at[i, me], (p, core)
            ).wait_send()
            return carry

        lax.fori_loop(1, n, go, 0)

    def assemble(i, out):
        tails = []
        for src, at in ((r_msg, mine), (f_msg, other)):
            for b in range(z.blocks):
                lanes = pl.ds(pl.multiple_of(at + b * LANE, LANE), LANE)
                if z.main:
                    rows = src[i, :, b * z.main : (b + 1) * z.main, :]
                    out[0 : z.nm, lanes] = rows.reshape(z.nm, LANE)
            for g in range(n // BUNCH):
                tail = tail_of(i, src, g)
                q, r = iota((z.bt, BUNCH * 16), 0), iota((z.bt, BUNCH * 16), 1)
                base = q // z.tail * 16 + q % z.tail
                for b in range(z.blocks):
                    lanes = pl.ds(pl.multiple_of(at + b * LANE, LANE), LANE)
                    pick = one(r == base + b * z.tail)
                    out[z.nm + g * z.bt : z.nm + (g + 1) * z.bt, lanes] = dot(pick, tail).astype(
                        BF16
                    )

    def tail_of(i, src, g):
        rows = src[i, g * BUNCH : (g + 1) * BUNCH, z.msg - 16 : z.msg, :]
        return rows.reshape(BUNCH * 16, LANE)

    def pack(i, value, extra):
        if z.main:
            for b in range(z.blocks):
                s_msg[i, :, b * z.main : (b + 1) * z.main, :] = value[
                    0 : z.nm, b * LANE : (b + 1) * LANE
                ].reshape(n, z.main, LANE)
        q, r = iota((BUNCH * 16, z.bt), 1), iota((BUNCH * 16, z.bt), 0)
        base = q // z.tail * 16 + q % z.tail
        for g in range(n // BUNCH):
            tail = None if extra is None else extra[g]
            for b in range(z.blocks):
                put = one(r == base + b * z.tail)
                rows = value[z.nm + g * z.bt : z.nm + (g + 1) * z.bt, b * LANE : (b + 1) * LANE]
                piece = dot(put, rows)
                tail = piece if tail is None else tail + piece
            s_msg[i, g * BUNCH : (g + 1) * BUNCH, z.msg - 16 : z.msg, :] = tail.astype(
                BF16
            ).reshape(BUNCH, 16, LANE)

    gate_row = 14

    rows8[...] = jnp.full(rows8.shape, -1.0, F32)
    rows8[0:2, 0:tok] = routes_ref[...].astype(F32)
    rows8[2:4, 0:tok] = slots_ref[...].astype(F32)
    rows8[4:5, 0:tok] = valid_ref[...].astype(F32)
    table = rows8[...]
    r_row = [table[k : k + 1, :].astype(jnp.int32) for k in range(2)]
    j_row = [table[2 + k : 3 + k, :].astype(jnp.int32) for k in range(2)]
    keep_row = table[4:5, :] > 0.5

    def targets(r, j):
        sent = (r >= 0) & (j < z.cap)
        flat = jnp.where(j < z.main, r * z.main + j, z.nm + r * z.tail + (j - z.main))
        return sent, jnp.where(sent, flat, -1)

    sent_row, flat_row = zip(*[targets(r, j) for r, j in zip(r_row, j_row)])
    cols8[...] = jnp.transpose(table)
    r_col = [cols8[0:tp, k : k + 1].astype(jnp.int32) for k in range(2)]
    j_col = [cols8[0:tp, 2 + k : 3 + k].astype(jnp.int32) for k in range(2)]
    keep_col = jnp.where(cols8[0:tp, 4:5] > 0.5, 1.0, 0.0)
    sent_col, flat_col = zip(*[targets(r, j) for r, j in zip(r_col, j_col)])

    slot_id = iota((z.slots, tk), 0)
    onehot[...] = one((slot_id == flat_row[0]) | (slot_id == flat_row[1]))
    tail_id = iota((BUNCH * 16, tk), 0)
    tail_row = [
        jnp.where(s & (j >= z.main), r * 16 + (j - z.main), -1000)
        for s, r, j in zip(sent_row, r_row, j_row)
    ]

    def place(src, i, extra):
        if z.main:
            for b in range(z.blocks):
                lanes = pl.ds(pl.multiple_of(mine + b * LANE, LANE), LANE)
                rows = dot(onehot[0 : z.nm, :], src[:, lanes]).astype(BF16)
                s_msg[i, :, b * z.main : (b + 1) * z.main, :] = rows.reshape(n, z.main, LANE)
        for g in range(n // BUNCH):
            tail = None if extra is None else extra[g]
            for b in range(z.blocks):
                lanes = pl.ds(pl.multiple_of(mine + b * LANE, LANE), LANE)
                at = b * z.tail - g * BUNCH * 16
                put = one((tail_id == tail_row[0] + at) | (tail_id == tail_row[1] + at))
                piece = dot(put, src[:, lanes])
                tail = piece if tail is None else tail + piece
            s_msg[i, g * BUNCH : (g + 1) * BUNCH, z.msg - 16 : z.msg, :] = tail.astype(
                BF16
            ).reshape(BUNCH, 16, LANE)

    upk[tok // 16 * 16 :, :] = jnp.zeros((tk - tok // 16 * 16, width), BF16)
    upk[0:tok, :] = grad_out_ref[...]
    place(upk, 0, None)

    xf[tok // 8 * 8 :, :] = jnp.zeros((tp - tok // 8 * 8, width), F32)
    xf[0:tok, :] = tokens_ref[...].astype(F32)
    normal, inverse1 = norm_parts(xf[...])
    normal1[...] = normal
    n1[tp:, :] = jnp.zeros((tk - tp, width), BF16)
    n1[0:tp, :] = (normal * row_of(ln1g_ref) + row_of(ln1b_ref)).astype(BF16)

    pl.semaphore_wait(barrier, n)
    a2a_send(0)

    weights[0].wait()
    for c, (dst, bias) in enumerate(((q_s, bqv_ref[0:1, :]), (k_s, None), (v_s, bqv_ref[1:2, :]))):
        value = dot(n1[0:tp, :], wqkv[c])
        if bias is not None:
            value = value + bias
        dst[tp:, :] = jnp.zeros((tk - tp, hw), BF16)
        dst[0:tp, :] = value.astype(BF16)

    score_scale = 1.0 / math.sqrt(HEAD)
    low_lane = iota((1, LANE), 1) < HEAD
    head_mask = [one(low_lane), one(jnp.logical_not(low_lane))]
    for p in range(z.pairs):
        lanes = slice(p * LANE, (p + 1) * LANE)
        qp, kp, vp = q_s[0:tp, lanes], k_s[:, lanes], v_s[:, lanes]
        outs = []
        for h in range(2):
            scores = dot_bt(qp * head_mask[h], kp) * score_scale
            scores = jnp.where(keep_row, scores, -1000000000.0)
            weights_h = jnp.exp(scores - jnp.max(scores, axis=-1, keepdims=True))
            prob = weights_h / jnp.sum(weights_h, axis=-1, keepdims=True)
            probs[2 * p + h] = prob
            outs.append(dot(prob.astype(BF16), vp))
        mix[0:tp, lanes] = jnp.where(low_lane, outs[0], outs[1]).astype(BF16)
    mix[tp:, :] = jnp.zeros((tk - tp, hw), BF16)
    weights[1].wait()
    part[...] = dot(mix[0:tp, :], wo[...])
    swap = remote(part, part_in, hs.at[0], hr.at[0], sib)
    swap.start()
    n1t[...] = jnp.transpose(n1[...])
    swap.wait()

    attention = part[...] + part_in[...] + row_of(bo_ref)
    stat_attn = jnp.sum(keep_col * attention * attention)
    middle = xf[...] + attention
    mid[...] = middle
    normal, inverse2 = norm_parts(middle)
    normal2[...] = normal
    n2[tp:, :] = jnp.zeros((tk - tp, width), BF16)
    n2[0:tp, :] = (normal * row_of(ln2g_ref) + row_of(ln2b_ref)).astype(BF16)
    logits = dot_bt(router_ref[...], n2[...])
    expert_id = iota((z.experts, tk), 0)
    chosen = [
        jnp.sum(jnp.where(expert_id == r, logits, 0.0), axis=0, keepdims=True) for r in r_row
    ]
    top = jnp.maximum(chosen[0], chosen[1])
    raw = [jnp.exp(c - top) for c in chosen]
    total = raw[0] + raw[1]
    gate_rows = [r / total for r in raw]
    cols8[0:tk, :] = jnp.transpose(
        jnp.concatenate(gate_rows + [jnp.zeros((6, tk), F32)], axis=0)
    )
    gate = [cols8[0:tp, k : k + 1] for k in range(2)]

    slot_lane = iota((tk, LANE), 1)
    numbers = []
    pad_col = [
        jnp.concatenate([j, jnp.full((tk - tp, 1), -1, jnp.int32)], axis=0) for j in j_col
    ]
    for g in range(n // BUNCH):
        number = None
        for k in range(2):
            high, low = split(gate_rows[k])
            at = r_row[k] * 16 + (gate_row - g * BUNCH * 16)
            lift = jnp.where(
                sent_row[k] & (tail_id == at), high.astype(F32), 0.0
            ) + jnp.where(sent_row[k] & (tail_id == at + 1), low.astype(F32), 0.0)
            piece = dot(lift.astype(BF16), one(slot_lane == pad_col[k]))
            number = piece if number is None else number + piece
        numbers.append(number)
    place(n2, 1, numbers)
    a2a_send(1)

    a2a_forward(0)
    a2a_finish(0)
    assemble(0, u_s)
    weights[2].wait()
    gh[...] = dot_bt(u_s[...], wout[...])

    weights[3].wait()
    a2a_forward(1)
    a2a_finish(1)
    assemble(1, x_s)

    def numbered(rows, per, first):
        q, r = iota((rows, BUNCH * 16), 0), iota((rows, BUNCH * 16), 1)
        pick = r == q // per * 16 + gate_row
        lane = iota((rows, LANE), 1) == iota((rows, LANE), 0) % per + first
        return pick, r == q // per * 16 + gate_row + 1, lane

    parts = [(0, BUNCH * z.main, z.main, 0)] if z.main else []
    parts += [(z.nm, z.bt, z.tail, z.main)]
    for g in range(n // BUNCH):
        tail = tail_of(1, r_msg, g)
        for at, rows, per, first in parts:
            high, low, lane = numbered(rows, per, first)
            picked = dot(one(high | low), tail)
            gcol_s[at + g * rows : at + (g + 1) * rows, :] = jnp.sum(
                jnp.where(lane, picked, 0.0), axis=-1, keepdims=True
            )
    pre[...] = dot(x_s[...], win[...])
    step = 16

    def activate(i, carry):
        rows = pl.ds(pl.multiple_of(i * step, step), step)
        v = pre[rows, :] + bin_ref[...]
        v2 = v * v
        t = jnp.tanh(ROOT * v * (1.0 + CUBE * v2))
        half_sum = 0.5 + 0.5 * t
        act = v * half_sum
        back = half_sum + (0.5 * ROOT) * v * (1.0 - t * t) * (1.0 + (3.0 * CUBE) * v2)
        g = gh[rows, :]
        hid[rows, :] = act.astype(BF16)
        gp[rows, :] = (gcol_s[rows, :] * g * back).astype(BF16)
        ggv[rows, :] = jnp.sum(g * act, axis=-1, keepdims=True)
        return carry

    lax.fori_loop(0, z.slots // step, activate, 0)

    half_out[0] = dot_bt(gp[...], win[pl.ds(other, half), :])
    swap = remote(half_out.at[0], half_in.at[0], hs.at[1], hr.at[1], sib)
    swap.start()
    own = dot_bt(gp[...], win[pl.ds(mine, half), :])
    bias_half = bout_ref[:, pl.ds(mine, half)]
    gg = ggv[...] + jnp.sum(
        u_s[:, pl.ds(mine, half)].astype(F32) * bias_half, axis=-1, keepdims=True
    )
    numbers = []
    for g in range(n // BUNCH):
        number = None
        for at, rows, per, first in parts:
            q, r = iota((BUNCH * 16, rows), 1), iota((BUNCH * 16, rows), 0)
            lane = iota((rows, LANE), 1) == iota((rows, LANE), 0) % per + first
            high, low = split(jnp.where(lane, gg[at + g * rows : at + (g + 1) * rows, :], 0.0))
            piece = dot(one(r == q // per * 16 + gate_row), high) + dot(
                one(r == q // per * 16 + gate_row + 1), low
            )
            number = piece if number is None else number + piece
        numbers.append(number)
    swap.wait()
    pack(2, (own + half_in[0]).astype(BF16), numbers)
    a2a_send(2)

    half_out[1] = dot(hid[...], wout[:, pl.ds(other, half)])
    swap = remote(half_out.at[1], half_in.at[1], hs.at[2], hr.at[2], sib)
    swap.start()
    own = dot(hid[...], wout[:, pl.ds(mine, half)]) + bias_half
    swap.wait()
    pack(3, (own + half_in[1]).astype(BF16), None)

    sg[...] = (gcol_s[...] * u_s[...].astype(F32)).astype(BF16)
    x_t[...] = jnp.transpose(x_s[...])
    hid_t[...] = jnp.transpose(hid[...])
    o_beo[...] = jnp.sum(sg[...].astype(F32), axis=0, keepdims=True)
    o_bei[...] = jnp.sum(gp[...].astype(F32), axis=0, keepdims=True)
    stores = [
        pltpu.make_async_copy(a, b, osem.at[i])
        for i, (a, b) in enumerate(((x_t, o_x), (sg, o_sg), (hid_t, o_hid), (gp, o_gp)))
    ]
    for copy in stores:
        copy.start()
    mix_t = jnp.transpose(mix[...])

    flat_id = iota((tp, z.slots), 1)
    back_one = [one(flat_id == f) for f in flat_col]
    a2a_forward(2)
    a2a_send(3)
    a2a_finish(2)
    assemble(2, y_s)
    tail_lane = iota((tp, BUNCH * 16), 1)
    grad_gate = []
    for k in range(2):
        row = None
        for g in range(n // BUNCH):
            at = r_col[k] * 16 + (gate_row - g * BUNCH * 16)
            pick = one(sent_col[k] & ((tail_lane == at) | (tail_lane == at + 1)))
            piece = dot(pick, tail_of(2, r_msg, g)) + dot(pick, tail_of(2, f_msg, g))
            row = piece if row is None else row + piece
        row = jnp.where(iota((tp, LANE), 1) == j_col[k], row, 0.0)
        grad_gate.append(jnp.sum(row, axis=-1, keepdims=True))
    mean_gate = gate[0] * grad_gate[0] + gate[1] * grad_gate[1]
    e_pad = up_to(z.experts, LANE)
    e_lane = iota((tp, e_pad), 1)
    grad_logits = jnp.where(
        e_lane == r_col[0], gate[0] * (grad_gate[0] - mean_gate), 0.0
    ) + jnp.where(e_lane == r_col[1], gate[1] * (grad_gate[1] - mean_gate), 0.0)
    gl_high, gl_low = split(grad_logits)
    router_pad = router_ref[...]
    if e_pad > z.experts:
        router_pad = jnp.concatenate(
            [router_pad, jnp.zeros((e_pad - z.experts, width), BF16)], axis=0
        )
    grad_n2 = (
        dot(back_one[0] + back_one[1], y_s[...])
        + dot(gl_high, router_pad)
        + dot(gl_low, router_pad)
    )
    grad_router = dot_at(gl_high, n2[0:tp, :]) + dot_at(gl_low, n2[0:tp, :])
    smallf[...] = jnp.zeros(smallf.shape, F32)
    ne = z.experts
    smallf[0:ne, :] = grad_router[0:ne, :]
    normal = normal2[...]
    smallf[ne + 2 : ne + 3, :] = jnp.sum(grad_n2 * normal, axis=0, keepdims=True)
    smallf[ne + 3 : ne + 4, :] = jnp.sum(grad_n2, axis=0, keepdims=True)
    gm[...] = upk[0:tp, :].astype(F32) + norm_backward(grad_n2, normal, inverse2, row_of(ln2g_ref))
    ag[tp:, :] = jnp.zeros((tk - tp, width), BF16)
    ag[0:tp, :] = gm[...].astype(BF16)
    smallf[ne + 4 : ne + 5, :] = jnp.sum(ag[...].astype(F32), axis=0, keepdims=True)

    groups = []
    for order in chain_orders(z.bits) + [z.bits]:
        start, size, steps = 0, n, []
        for b in order:
            bit = lax.rem(me // b, 2)
            peer = me + b * (1 - 2 * bit)
            size = size // 2
            steps.append((peer, start + (1 - bit) * size, start + bit * size, size))
            start = start + bit * size
        groups.append((steps, start))
    n_main = len(groups) - 1

    def chain_of(g):
        if g < n_main:
            return chain_g.at[g], [r.at[g] for r in chain_r], chain_a.at[g], z.chunk
        return chain_small, list(small_r), small_a, z.small

    def region(ref, at, count, rows):
        return ref.at[pl.ds(pl.multiple_of(at * rows, 16), count * rows)]

    def rs_copy(g, s):
        src, bufs, _, rows = chain_of(g)
        peer, give, _, size = groups[g][0][s]
        return remote(
            region(src, give, size, rows), bufs[s], cs.at[g, s], cr.at[g, s], (peer, core)
        )

    def rs_add(g, s, at, count, dst):
        src, bufs, _, rows = chain_of(g)
        keep = groups[g][0][s][2]

        def go(i, carry):
            here = pl.ds(pl.multiple_of((at + i) * rows, 16), rows)
            there = pl.ds(pl.multiple_of((at + i - keep) * rows, 16), rows)
            dst[here, :] = (src[here, :].astype(F32) + bufs[s][there, :].astype(F32)).astype(BF16)
            return carry

        lax.fori_loop(0, count, go, 0)

    def rs_step(g, s):
        src, _, out, _ = chain_of(g)
        rs_copy(g, s).wait()
        if s + 1 < nbits:
            _, give, keep, size = groups[g][0][s + 1]
            rs_add(g, s, give, size, src)
            rs_copy(g, s + 1).start()
            rs_add(g, s, keep, size, src)
        else:
            rs_add(g, s, groups[g][1], 1, out)
            ag_copy(g, s).start()

    def ag_copy(g, s):
        _, _, out, rows = chain_of(g)
        peer, _, keep, size = groups[g][0][s]
        piece = region(out, keep, size, rows)
        return remote(piece, piece, as_.at[g, s], ar.at[g, s], (peer, core))

    def ag_step(g, s):
        _, _, out, rows = chain_of(g)
        peer, give, _, size = groups[g][0][s]
        ag_copy(g, s).wait_send()
        piece = region(out, give, size, rows)
        remote(piece, piece, as_.at[g, s], ar.at[g, s], (peer, core)).wait_recv()
        if s > 0:
            ag_copy(g, s - 1).start()

    filled = 0

    def fill(value):
        nonlocal filled
        rows = value.shape[0]
        for b in range(value.shape[1] // LANE):
            g, at = divmod(filled, z.chain_rows)
            chain_g[g, at : at + rows, :] = value[:, b * LANE : (b + 1) * LANE].astype(BF16)
            filled += rows
            if filled == (g + 1) * z.chain_rows:
                rs_copy(g, 0).start()

    if z.chain_rows < n * z.chunk:
        for g in range(n_main):
            chain_g[g, z.chain_rows :, :] = jnp.zeros((n * z.chunk - z.chain_rows, LANE), BF16)
    fill(dot(mix_t, ag[...]))

    dm[...] = dot_bt(ag[0:tp, :], wo[...]).astype(BF16)
    for p in range(z.pairs):
        lanes = slice(p * LANE, (p + 1) * LANE)
        qp, kp, vp, dp = q_s[0:tp, lanes], k_s[:, lanes], v_s[:, lanes], dm[:, lanes]
        dq, dk, dv = [], [], []
        for h in range(2):
            prob = probs[2 * p + h]
            gprob = dot_bt(dp * head_mask[h], vp)
            inner = jnp.sum(prob * gprob, axis=-1, keepdims=True)
            gs = (prob * (gprob - inner)).astype(BF16)
            dq.append(dot(gs, kp))
            dk.append(dot_at(gs, qp))
            dv.append(dot_at(prob.astype(BF16), dp))
        for c, (pair, scale) in enumerate(((dq, score_scale), (dk, score_scale), (dv, 1.0))):
            value = (jnp.where(low_lane, pair[0], pair[1]) * scale).astype(BF16)
            at = slice(c * hw + p * LANE, c * hw + (p + 1) * LANE)
            if c == 0:
                gpr[0:tp, at] = value
                gpr[tp:, at] = jnp.zeros((tk - tp, LANE), BF16)
            else:
                gpr[:, at] = value
        joined = jnp.concatenate(
            [gpr[:, c * hw + p * LANE : c * hw + (p + 1) * LANE] for c in range(3)], axis=1
        )
        fill(dot(n1t[...], joined))

    head_part = None
    for c in range(3):
        piece = dot_bt(gpr[0:tp, c * hw : (c + 1) * hw], wqkv[c])
        head_part = piece if head_part is None else head_part + piece
    gn_out[...] = head_part.astype(BF16)
    swap = remote(gn_out, gn_in, hs.at[3], hr.at[3], sib)
    swap.start()
    smallf[ne + 5 : ne + 6, 0:hw] = jnp.sum(gpr[:, 0:hw].astype(F32), axis=0, keepdims=True)
    smallf[ne + 6 : ne + 7, 0:hw] = jnp.sum(
        gpr[:, 2 * hw : 3 * hw].astype(F32), axis=0, keepdims=True
    )
    swap.wait()
    grad_n1 = gn_out[...].astype(F32) + gn_in[...].astype(F32)
    normal = normal1[...]
    smallf[ne : ne + 1, :] = jnp.sum(grad_n1 * normal, axis=0, keepdims=True)
    smallf[ne + 1 : ne + 2, :] = jnp.sum(grad_n1, axis=0, keepdims=True)
    back = gm[...] + norm_backward(grad_n1, normal, inverse1, row_of(ln1g_ref))
    o_gtok[...] = back[0:tok, :]
    used = z.small_rows * (width // LANE)
    for b in range(width // LANE):
        chain_small[b * z.small_rows : (b + 1) * z.small_rows, :] = smallf[
            :, b * LANE : (b + 1) * LANE
        ].astype(BF16)
    if used < n * z.small:
        chain_small[used:, :] = jnp.zeros((n * z.small - used, LANE), BF16)
    rs_copy(n_main, 0).start()

    a2a_forward(3)
    a2a_finish(3)
    assemble(3, y_s)
    branch = gate[0] * dot(back_one[0], y_s[...]) + gate[1] * dot(back_one[1], y_s[...])
    output = mid[...] + branch
    o_tok[...] = output[0:tok, :].astype(BF16)
    lane_id = iota((1, LANE), 1)
    x_all = xf[...]
    line = jnp.zeros((1, LANE), F32)
    for i, number in enumerate(
        (
            jnp.sum(keep_col * x_all * x_all),
            stat_attn,
            jnp.sum(keep_col * branch * branch),
            jnp.sum(keep_col * output * output),
            jnp.sum(keep_col),
        )
    ):
        line = jnp.where(lane_id == i, number, line)
    stat[me] = jnp.broadcast_to(line, (8, LANE))

    def stat_go(j, carry):
        p = lax.rem(me + j, n)
        remote(stat.at[me], stat.at[me], sts.at[p], str_.at[me], (p, core)).start()
        return carry

    lax.fori_loop(1, n, stat_go, 0)

    for s in range(nbits):
        for g in range(n_main + 1):
            rs_step(g, s)

    def stat_wait(j, carry):
        p = lax.rem(me + j, n)
        remote(stat.at[me], stat.at[me], sts.at[p], str_.at[me], (p, core)).wait_send()
        remote(stat.at[p], stat.at[p], sts.at[p], str_.at[p], (p, core)).wait_recv()
        return carry

    lax.fori_loop(1, n, stat_wait, 0)
    totals = jnp.sum(stat[...], axis=0)
    count = jnp.sum(jnp.where(iota((8, LANE), 1) == 4, totals, 0.0), axis=-1, keepdims=True)
    o_rms[...] = jnp.sqrt(totals / (count * width))

    for s in range(nbits - 1, -1, -1):
        for g in range(n_main + 1):
            ag_step(g, s)
    for g in range(n_main):
        copy = pltpu.make_async_copy(chain_a.at[g], o_red.at[g], osem.at[4 + g])
        copy.start()
        stores.append(copy)
    for b in range(width // LANE):
        o_small[:, b * LANE : (b + 1) * LANE] = small_a[
            b * z.small_rows : (b + 1) * z.small_rows, :
        ].astype(F32)
    for i in range(4):
        a2a_sent(i)
    for copy in stores:
        copy.wait()


def last_kernel(
    z,
    i_tok,
    i_gtok,
    i_x,
    i_sg,
    i_hid,
    i_gp,
    i_red,
    i_small,
    i_bei,
    i_beo,
    i_rms,
    o_tok,
    o_gtok,
    o_ln1g,
    o_ln1b,
    o_wqkv,
    o_bqv,
    o_wo,
    o_bo,
    o_ln2g,
    o_ln2b,
    o_router,
    o_win,
    o_bin,
    o_wout,
    o_bout,
    o_rms,
    x_t,
    sg,
    hid_t,
    gp,
    red,
    wqkv,
    wo,
    win,
    wout,
    tok_s,
    gtok_s,
    isem,
    osem,
):
    ne, width, hw = z.experts, z.width, z.hw
    loads = [
        pltpu.make_async_copy(i_red.at[g], red.at[g], isem.at[6 + g]) for g in range(z.chains)
    ]
    loads += [
        pltpu.make_async_copy(a, b, isem.at[i])
        for i, (a, b) in enumerate(
            (
                (i_x, x_t),
                (i_gp, gp),
                (i_hid, hid_t),
                (i_sg, sg),
                (i_tok, tok_s),
                (i_gtok, gtok_s),
            )
        )
    ]
    for copy in loads:
        copy.start()
    stores = []

    def store(src, dst, i):
        copy = pltpu.make_async_copy(src, dst, osem.at[i])
        copy.start()
        stores.append(copy)

    for ref, i in ((o_ln1g, 0), (o_ln1b, 1), (o_ln2g, 2), (o_ln2b, 3), (o_bo, 4)):
        ref[...] = i_small[ne + i : ne + i + 1, :].reshape(width)
    o_router[...] = i_small[0:ne, :]
    o_bqv[...] = i_small[ne + 5 : ne + 7, 0:hw]
    o_bin[...] = i_bei[...]
    o_bout[...] = i_beo[...]
    o_rms[...] = i_rms[0:1, 0:4].reshape(4)

    at, ready = 0, 0

    def take(rows):
        nonlocal at, ready
        g, row = divmod(at, z.chain_rows)
        if g == ready:
            loads[g].wait()
            ready += 1
        at += rows
        return red[g, row : row + rows, :].astype(F32)

    for b in range(width // LANE):
        wo[:, b * LANE : (b + 1) * LANE] = take(hw)
    store(wo, o_wo, 2)
    for p in range(z.pairs):
        for c in range(3):
            wqkv[c, :, p * LANE : (p + 1) * LANE] = take(width)
    store(wqkv, o_wqkv, 3)
    for i in range(2):
        loads[z.chains + i].wait()
    tiles = z.ff // TILE
    for t in range(tiles):
        cols = slice(t * TILE, (t + 1) * TILE)
        win[:, cols] = dot(x_t[...], gp[:, cols])
        store(win.at[:, cols], o_win.at[0, :, cols], 4 + t)
    for i in range(2, 4):
        loads[z.chains + i].wait()
    for t in range(tiles):
        rows = slice(t * TILE, (t + 1) * TILE)
        wout[rows, :] = dot(hid_t[rows, :], sg[...])
        store(wout.at[rows, :], o_wout.at[0, rows, :], 4 + tiles + t)
    for i, (src, dst) in enumerate(((tok_s, o_tok), (gtok_s, o_gtok))):
        loads[z.chains + 4 + i].wait()
        store(src, dst, i)
    for copy in stores:
        copy.wait()


def per_device(
    tokens,
    grad_out,
    valid_mask,
    routes,
    slot_index,
    ln1_gain,
    ln1_bias,
    w_qkv,
    bias_qv,
    w_attn_out,
    b_attn_out,
    ln2_gain,
    ln2_bias,
    router,
    w_expert_in,
    b_expert_in,
    w_expert_out,
    b_expert_out,
):
    tok, width = tokens.shape
    hw = w_qkv.shape[2]
    ff = w_expert_in.shape[2]
    z = Sizes(lax.axis_size("dp"), tok, width, hw, ff, router.shape[1])
    n, tp, tk = z.n, z.tp, z.tk
    nbits = len(z.bits)
    vmem = pl.BlockSpec(memory_space=pltpu.VMEM)
    any_ = pl.BlockSpec(memory_space=pl.ANY)
    shape = jax.ShapeDtypeStruct
    groups = z.chains
    V = pltpu.VMEM
    scratch = [
        V((3, width, hw), BF16),
        V((hw, width), BF16),
        V((width, ff), BF16),
        V((ff, width), BF16),
        V((tp, width), F32),
        V((tp, width), F32),
        V((tk, width), BF16),
        V((width, tk), BF16),
        V((tk, width), BF16),
        V((tk, hw), BF16),
        V((tk, hw), BF16),
        V((tk, hw), BF16),
        V((2 * z.pairs, tp, tk), F32),
        V((tk, hw), BF16),
        V((tp, width), F32),
        V((tp, width), F32),
        V((tp, width), F32),
        V((tp, width), F32),
        V((tk, width), BF16),
        V((z.slots, tk), BF16),
        V((8, tk), F32),
        V((tk, 8), F32),
        V((z.slots, width), BF16),
        V((z.slots, width), BF16),
        V((z.slots, width), BF16),
        V((z.slots, ff), F32),
        V((z.slots, ff), F32),
        V((z.slots, ff), BF16),
        V((z.slots, ff), BF16),
        V((z.slots, width), BF16),
        V((width, z.slots), BF16),
        V((ff, z.slots), BF16),
        V((z.slots, 1), F32),
        V((z.slots, 1), F32),
        V((2, z.slots, z.half), F32),
        V((2, z.slots, z.half), F32),
        V((tp, width), F32),
        V((tk, width), BF16),
        V((tp, hw), BF16),
        V((tk, 3 * hw), BF16),
        V((tp, width), BF16),
        V((tp, width), BF16),
        V((z.small_rows, width), F32),
        V((n, 8, LANE), F32),
        V((4, n, z.msg, LANE), BF16),
        V((4, n, z.msg, LANE), BF16),
        V((4, n, z.msg, LANE), BF16),
        V((groups, n * z.chunk, LANE), BF16),
        V((n * z.small, LANE), BF16),
    ]
    scratch += [V((groups, (n >> (s + 1)) * z.chunk, LANE), BF16) for s in range(nbits)]
    scratch += [V(((n >> (s + 1)) * z.small, LANE), BF16) for s in range(nbits)]
    scratch += [
        V((groups, n * z.chunk, LANE), BF16),
        V((n * z.small, LANE), BF16),
        DMA((4,)),
        DMA((4 + groups,)),
        DMA((4,)),
        DMA((4,)),
        DMA((4, n)),
        DMA((4, n)),
        DMA((4, n)),
        DMA((4, n)),
        DMA((groups + 1, nbits)),
        DMA((groups + 1, nbits)),
        DMA((groups + 1, nbits)),
        DMA((groups + 1, nbits)),
        DMA((n,)),
        DMA((n,)),
    ]
    row = lambda v: v.reshape(1, -1)
    outs = pl.pallas_call(
        functools.partial(mega_kernel, z),
        out_shape=(
            shape((tok, width), BF16),
            shape((tok, width), F32),
            shape((width, z.slots), BF16),
            shape((z.slots, width), BF16),
            shape((ff, z.slots), BF16),
            shape((z.slots, ff), BF16),
            shape((groups, n * z.chunk, LANE), BF16),
            shape((z.small_rows, width), F32),
            shape((1, ff), F32),
            shape((1, width), F32),
            shape((8, LANE), F32),
        ),
        in_specs=[vmem] * 7
        + [any_, vmem, any_, vmem, vmem, vmem, vmem, any_, vmem, any_, vmem],
        out_specs=(vmem, vmem, any_, any_, any_, any_, any_, vmem, vmem, vmem, vmem),
        scratch_shapes=scratch,
        compiler_params=pltpu.CompilerParams(
            collective_id=0, has_side_effects=True, vmem_limit_bytes=60 * 2**20
        ),
    )(
        tokens,
        grad_out,
        row(valid_mask),
        routes.T,
        slot_index.T,
        ln1_gain,
        ln1_bias,
        jnp.transpose(w_qkv, (1, 0, 2)),
        bias_qv,
        w_attn_out,
        b_attn_out,
        ln2_gain,
        ln2_bias,
        router.T,
        w_expert_in[0],
        b_expert_in,
        w_expert_out[0],
        b_expert_out,
    )
    o_tok, o_gtok, o_x, o_sg, o_hid, o_gp, o_red, o_small, o_bei, o_beo, o_rms = outs
    ne = z.experts
    vec = shape((width,), F32)
    last = pl.pallas_call(
        functools.partial(last_kernel, z),
        out_shape=(
            shape((tok, width), BF16),
            shape((tok, width), F32),
            vec,
            vec,
            shape((3, width, hw), F32),
            shape((2, hw), F32),
            shape((hw, width), F32),
            vec,
            vec,
            vec,
            shape((ne, width), F32),
            shape((1, width, ff), F32),
            shape((1, ff), F32),
            shape((1, ff, width), F32),
            shape((1, width), F32),
            shape((4,), F32),
        ),
        in_specs=[any_] * 7 + [vmem] * 4,
        out_specs=(
            [any_] * 2
            + [vmem] * 2
            + [any_, vmem, any_]
            + [vmem] * 4
            + [any_, vmem, any_, vmem, vmem]
        ),
        scratch_shapes=[
            V((width, z.slots), BF16),
            V((z.slots, width), BF16),
            V((ff, z.slots), BF16),
            V((z.slots, ff), BF16),
            V((groups, n * z.chunk, LANE), BF16),
            V((3, width, hw), F32),
            V((hw, width), F32),
            V((width, ff), F32),
            V((ff, width), F32),
            V((tok, width), BF16),
            V((tok, width), F32),
            DMA((6 + groups,)),
            DMA((4 + 2 * (ff // TILE),)),
        ],
        compiler_params=pltpu.CompilerParams(vmem_limit_bytes=60 * 2**20),
    )(o_tok, o_gtok, o_x, o_sg, o_hid, o_gp, o_red, o_small, o_bei, o_beo, o_rms)
    return (
        last[0],
        last[1],
        last[2],
        last[3],
        jnp.transpose(last[4], (1, 0, 2)),
        *last[5:10],
        last[10].T,
        *last[11:],
    )


def solution(mesh):
    return jax.shard_map(
        per_device,
        mesh=mesh,
        in_specs=(
            P("dp", None),
            P("dp", None),
            P("dp"),
            P("dp", None),
            P("dp", None),
            P(),
            P(),
            P(None, None, "tensor"),
            P(None, "tensor"),
            P("tensor", None),
            P(),
            P(),
            P(),
            P(),
            P("dp", None, "tensor"),
            P("dp", "tensor"),
            P("dp", "tensor", None),
            P("dp", None),
        ),
        out_specs=(
            P("dp", None),
            P("dp", None),
            P(),
            P(),
            P(None, None, "tensor"),
            P(None, "tensor"),
            P("tensor", None),
            P(),
            P(),
            P(),
            P(),
            P("dp", None, "tensor"),
            P("dp", "tensor"),
            P("dp", "tensor", None),
            P("dp", None),
            P(),
        ),
        check_vma=False,
    )
```

```python
import functools
import math

import jax
import jax.numpy as jnp
from jax import lax
from jax.experimental import pallas as pl
from jax.experimental.pallas import tpu as pltpu
from jax.sharding import PartitionSpec as P

HEAD = 64
SEQ = 197
LANE = 128
EPS = 1e-06
ROOT = math.sqrt(2.0 / math.pi)
CUBE = 0.044715
GROUPS = 4
SEND_ORDER = (0, 2, 1, 3)
TILE = 256
MESH = pl.DeviceIdType.MESH
F32 = jnp.float32
BF16 = jnp.bfloat16
DMA = pltpu.SemaphoreType.DMA


def up_to(value, step):
    return -(-value // step) * step


def dot(a, b):
    return lax.dot_general(a, b, (((1,), (0,)), ((), ())), preferred_element_type=F32)


def dot_bt(a, b):
    return lax.dot_general(a, b, (((1,), (1,)), ((), ())), preferred_element_type=F32)


def dot_at(a, b):
    return lax.dot_general(a, b, (((0,), (0,)), ((), ())), preferred_element_type=F32)


def row_of(ref):
    return ref[...].reshape(1, ref.shape[0])


def iota(shape, dim):
    return lax.broadcasted_iota(jnp.int32, shape, dim)


def one(cond, kind=BF16):
    return jnp.where(cond, 1.0, 0.0).astype(kind)


def split(value):
    high = value.astype(BF16)
    return high, (value - high.astype(F32)).astype(BF16)


def norm_parts(values):
    scale = 1.0 / values.shape[-1]
    center = values - jnp.sum(values, axis=-1, keepdims=True) * scale
    inverse = lax.rsqrt(jnp.sum(center * center, axis=-1, keepdims=True) * scale + EPS)
    return center * inverse, inverse


def norm_backward(incoming, normal, inverse, gain_vec):
    scale = 1.0 / incoming.shape[-1]
    scaled = incoming * gain_vec
    return inverse * (
        scaled
        - jnp.sum(scaled, axis=-1, keepdims=True) * scale
        - normal * (jnp.sum(scaled * normal, axis=-1, keepdims=True) * scale)
    )


def remote(src, dst, send_sem, recv_sem, device):
    return pltpu.make_async_remote_copy(
        src_ref=src,
        dst_ref=dst,
        send_sem=send_sem,
        recv_sem=recv_sem,
        device_id=device,
        device_id_type=MESH,
    )


class Sizes:
    def __init__(self, n, tok, width, heads_width, ff, experts):
        self.n = n
        self.tok = tok
        self.tp = up_to(tok, 16)
        self.tk = up_to(tok, LANE)
        self.width = width
        self.hw = heads_width
        self.pairs = heads_width // LANE
        self.ff = ff
        self.experts = experts
        self.cap = 2 * (3 * tok // (2 * n))
        self.main = self.cap // 16 * 16
        self.tail = self.cap - self.main
        self.half = width // 2
        self.blocks = self.half // LANE
        self.msg = self.main * self.blocks + 16
        self.per = n // GROUPS
        self.gm = self.per * self.main
        self.gt = self.per * self.tail
        self.rows = self.per * self.cap
        self.slots = n * self.cap
        self.bits = [1 << i for i in range(n.bit_length() - 1)]
        self.pack_rows = 4 * heads_width * width // LANE
        self.chains = 6
        self.chain_rows = self.pack_rows // self.chains
        self.chunk = up_to(up_to(self.chain_rows, n) // n, 16)
        self.small_rows = up_to(experts + 7, 16)
        self.small = up_to(up_to(self.small_rows * width // LANE, n) // n, 16)
        fits = 0 < self.tail * self.blocks <= 14 and self.gt % 16 == 0
        fits = fits and self.chain_rows % heads_width == 0 and self.chain_rows % width == 0
        if not fits or experts != n or (1 << len(self.bits)) != n:
            raise ValueError("unsupported sizes")


def chain_orders(bits):
    k = len(bits)
    if k < 3:
        return [bits] * 6
    order = ((0, 1, 2), (1, 2, 0), (2, 0, 1), (0, 2, 1), (1, 0, 2), (2, 1, 0))
    return [[bits[i] for i in head] + bits[3:] for head in order]


def mega_kernel(
    z,
    tokens_hbm,
    grad_out_hbm,
    valid_ref,
    routes_ref,
    slots_ref,
    ln1g_ref,
    ln1b_ref,
    wqkv_hbm,
    bqv_ref,
    wo_hbm,
    bo_ref,
    ln2g_ref,
    ln2b_ref,
    router_ref,
    win_hbm,
    bin_ref,
    wout_hbm,
    bout_ref,
    o_tok,
    o_gtok,
    o_x,
    o_sg,
    o_hid,
    o_gp,
    o_red,
    o_small,
    o_bei,
    o_beo,
    o_rms,
    tokens_ref,
    grad_out_ref,
    tok_out,
    gtok_out,
    wqkv,
    wo,
    win,
    wout,
    xf,
    normal1,
    n1,
    n1t,
    upk,
    q_s,
    k_s,
    v_s,
    probs,
    mix,
    part,
    part_in,
    mid,
    normal2,
    n2,
    onehot,
    rows8,
    cols8,
    u_s,
    x_s,
    y_s,
    gh,
    pre,
    hid,
    gp,
    sg,
    x_t,
    hid_t,
    gcol_s,
    ggv,
    half_out,
    half_in,
    half_own,
    gm,
    ag,
    dm,
    gpr,
    gn_out,
    gn_in,
    smallf,
    stat,
    s_msg,
    r_msg,
    f_msg,
    chain_g,
    chain_small,
    *rest,
):
    nbits = len(z.bits)
    chain_r = rest[:nbits]
    small_r = rest[nbits : 2 * nbits]
    chain_a, small_a, wsem, osem, hs, hr, ss, rs, fs, fr, cs, cr, as_, ar, st = rest[
        2 * nbits :
    ]
    n = z.n
    me, core = lax.axis_index("dp"), lax.axis_index("tensor")
    sib = (me, 1 - core)
    tok, tp, tk, width, hw, half = z.tok, z.tp, z.tk, z.width, z.hw, z.half
    mine = pl.multiple_of(core * half, LANE)
    other = pl.multiple_of((1 - core) * half, LANE)

    barrier = pltpu.get_barrier_semaphore()

    def greet(j, carry):
        pl.semaphore_signal(
            barrier, inc=1, device_id=(lax.rem(me + j, n), core), device_id_type=MESH
        )
        return carry

    lax.fori_loop(1, n, greet, 0)
    pl.semaphore_signal(barrier, inc=1, device_id=sib, device_id_type=MESH)

    tokens_in = [
        pltpu.make_async_copy(a, b, wsem.at[4 + i])
        for i, (a, b) in enumerate(((tokens_hbm, tokens_ref), (grad_out_hbm, grad_out_ref)))
    ]
    for copy in tokens_in[::-1]:
        copy.start()
    weights = [
        pltpu.make_async_copy(a, b, wsem.at[i])
        for i, (a, b) in enumerate(
            ((wqkv_hbm, wqkv), (wo_hbm, wo), (wout_hbm, wout), (win_hbm, win))
        )
    ]
    for copy in weights:
        copy.start()

    per = z.per
    own = me // per
    own_bits = [lax.rem(own, 2), own // 2]

    def group_at(k):
        turned = [b + t * (1 - 2 * b) for b, t in zip(own_bits, (k % 2, k // 2))]
        return turned[0] + 2 * turned[1]

    def members(ref, i, g):
        return ref.at[i, pl.ds(g * per, per)]

    def rows_of(g, first=0, count=None):
        return pl.ds(pl.multiple_of(g * z.rows + first, 16), z.rows if count is None else count)

    def a2a_send(i, k):
        g = group_at(k)
        if k == 0:
            pltpu.make_async_copy(s_msg.at[i, me], r_msg.at[i, me], rs.at[i, own]).start()

        def go(m, carry):
            p = g * per + lax.rem(me + m, per)
            remote(s_msg.at[i, p], r_msg.at[i, me], ss.at[i], rs.at[i, own], (p, core)).start()
            return carry

        lax.fori_loop(1 if k == 0 else 0, per, go, 0)

    def a2a_forward(i, k):
        g = group_at(k)
        block = members(r_msg, i, g)
        remote(block, block, ss.at[i], rs.at[i, g], sib).wait_recv()
        remote(block, members(f_msg, i, g), fs.at[i], fr.at[i, g], sib).start()

    def a2a_take(i, k):
        block = members(f_msg, i, group_at(k))
        remote(block, block, fs.at[i], fr.at[i, group_at(k)], sib).wait_recv()

    def a2a_sent(i):
        block = s_msg.at[i, pl.ds(0, n - 1)]
        remote(block, block, ss.at[i], rs.at[i, 0], sib).wait_send()
        remote(r_msg.at[i], f_msg.at[i], fs.at[i], fr.at[i, 0], sib).wait_send()

    def tail_of(i, src, g):
        rows = src[i, pl.ds(g * per, per), z.msg - 16 : z.msg, :]
        return rows.reshape(per * 16, LANE)

    def assemble(i, g, out):
        q, r = iota((z.gt, per * 16), 0), iota((z.gt, per * 16), 1)
        base = q // z.tail * 16 + q % z.tail
        for src, at in ((r_msg, mine), (f_msg, other)):
            tail = tail_of(i, src, g)
            for b in range(z.blocks):
                lanes = pl.ds(pl.multiple_of(at + b * LANE, LANE), LANE)
                if z.main:
                    rows = src[i, pl.ds(g * per, per), b * z.main : (b + 1) * z.main, :]
                    out[rows_of(g, 0, z.gm), lanes] = rows.reshape(z.gm, LANE)
                pick = one(r == base + b * z.tail)
                out[rows_of(g, z.gm, z.gt), lanes] = dot(pick, tail).astype(BF16)

    def pack(i, g, value, tail):
        q, r = iota((per * 16, z.gt), 1), iota((per * 16, z.gt), 0)
        base = q // z.tail * 16 + q % z.tail
        for b in range(z.blocks):
            lanes = slice(b * LANE, (b + 1) * LANE)
            if z.main:
                s_msg[i, pl.ds(g * per, per), b * z.main : (b + 1) * z.main, :] = value[
                    0 : z.gm, lanes
                ].reshape(per, z.main, LANE)
            piece = dot(one(r == base + b * z.tail), value[z.gm : z.rows, lanes])
            tail = piece if tail is None else tail + piece
        s_msg[i, pl.ds(g * per, per), z.msg - 16 : z.msg, :] = tail.astype(BF16).reshape(
            per, 16, LANE
        )

    gate_row = 14

    rows8[...] = jnp.full(rows8.shape, -1.0, F32)
    rows8[0:2, 0:tok] = routes_ref[...].astype(F32)
    rows8[2:4, 0:tok] = slots_ref[...].astype(F32)
    rows8[4:5, 0:tok] = valid_ref[...].astype(F32)
    table = rows8[...]
    r_row = [table[k : k + 1, :].astype(jnp.int32) for k in range(2)]
    j_row = [table[2 + k : 3 + k, :].astype(jnp.int32) for k in range(2)]
    keep_row = table[4:5, :] > 0.5

    def targets(r, j):
        sent = (r >= 0) & (j < z.cap)
        g = r // per
        m = r - g * per
        flat = jnp.where(j < z.main, m * z.main + j, z.gm + m * z.tail + (j - z.main))
        return sent, jnp.where(sent, g * z.rows + flat, -1)

    sent_row, flat_row = zip(*[targets(r, j) for r, j in zip(r_row, j_row)])
    cols8[...] = jnp.transpose(table)
    r_col = [cols8[0:tp, k : k + 1].astype(jnp.int32) for k in range(2)]
    j_col = [cols8[0:tp, 2 + k : 3 + k].astype(jnp.int32) for k in range(2)]
    keep_col = jnp.where(cols8[0:tp, 4:5] > 0.5, 1.0, 0.0)
    sent_col, flat_col = zip(*[targets(r, j) for r, j in zip(r_col, j_col)])

    slot_id = iota((z.slots, tk), 0)
    onehot[...] = one((slot_id == flat_row[0]) | (slot_id == flat_row[1]))
    tail_id = iota((per * 16, tk), 0)
    tail_row = [
        jnp.where(s & (j >= z.main), r * 16 + (j - z.main), -1000)
        for s, r, j in zip(sent_row, r_row, j_row)
    ]

    def place(src, i, g, tail):
        first = g * (per * 16)
        for b in range(z.blocks):
            lanes = pl.ds(pl.multiple_of(mine + b * LANE, LANE), LANE)
            rows = src[:, lanes]
            if z.main:
                main = dot(onehot[rows_of(g, 0, z.gm), :], rows).astype(BF16)
                s_msg[i, pl.ds(g * per, per), b * z.main : (b + 1) * z.main, :] = main.reshape(
                    per, z.main, LANE
                )
            at = b * z.tail - first
            put = one((tail_id == tail_row[0] + at) | (tail_id == tail_row[1] + at))
            piece = dot(put, rows)
            tail = piece if tail is None else tail + piece
        s_msg[i, pl.ds(g * per, per), z.msg - 16 : z.msg, :] = tail.astype(BF16).reshape(
            per, 16, LANE
        )

    upk[tok // 16 * 16 :, :] = jnp.zeros((tk - tok // 16 * 16, width), BF16)
    tokens_in[1].wait()
    upk[0:tok, :] = grad_out_ref[...]
    for g in range(GROUPS):
        place(upk, 0, g, None)

    xf[tok // 8 * 8 :, :] = jnp.zeros((tp - tok // 8 * 8, width), F32)
    tokens_in[0].wait()
    xf[0:tok, :] = tokens_ref[...].astype(F32)
    normal, inverse1 = norm_parts(xf[...])
    normal1[...] = normal
    n1[tp:, :] = jnp.zeros((tk - tp, width), BF16)
    n1[0:tp, :] = (normal * row_of(ln1g_ref) + row_of(ln1b_ref)).astype(BF16)

    pl.semaphore_wait(barrier, n)
    for k in SEND_ORDER:
        a2a_send(0, k)

    weights[0].wait()
    for c, (dst, bias) in enumerate(((q_s, bqv_ref[0:1, :]), (k_s, None), (v_s, bqv_ref[1:2, :]))):
        value = dot(n1[0:tp, :], wqkv[c])
        if bias is not None:
            value = value + bias
        dst[tp:, :] = jnp.zeros((tk - tp, hw), BF16)
        dst[0:tp, :] = value.astype(BF16)

    score_scale = 1.0 / math.sqrt(HEAD)
    low_lane = iota((1, LANE), 1) < HEAD
    head_mask = [one(low_lane), one(jnp.logical_not(low_lane))]
    for p in range(z.pairs):
        lanes = slice(p * LANE, (p + 1) * LANE)
        qp, kp, vp = q_s[0:tp, lanes], k_s[:, lanes], v_s[:, lanes]
        outs = []
        for h in range(2):
            scores = dot_bt(qp * head_mask[h], kp) * score_scale
            scores = jnp.where(keep_row, scores, -1000000000.0)
            weights_h = jnp.exp(scores - jnp.max(scores, axis=-1, keepdims=True))
            prob = weights_h / jnp.sum(weights_h, axis=-1, keepdims=True)
            probs[2 * p + h] = prob
            outs.append(dot(prob.astype(BF16), vp))
        mix[0:tp, lanes] = jnp.where(low_lane, outs[0], outs[1]).astype(BF16)
    mix[tp:, :] = jnp.zeros((tk - tp, hw), BF16)
    weights[1].wait()
    part[...] = dot(mix[0:tp, :], wo[...])
    swap = remote(part, part_in, hs.at[2, 0], hr.at[2, 0], sib)
    swap.start()
    n1t[...] = jnp.transpose(n1[...])
    swap.wait()

    attention = part[...] + part_in[...] + row_of(bo_ref)
    stat_attn = jnp.sum(keep_col * attention * attention)
    middle = xf[...] + attention
    mid[...] = middle
    normal, inverse2 = norm_parts(middle)
    normal2[...] = normal
    n2[tp:, :] = jnp.zeros((tk - tp, width), BF16)
    n2[0:tp, :] = (normal * row_of(ln2g_ref) + row_of(ln2b_ref)).astype(BF16)
    logits = dot_bt(router_ref[...], n2[...])
    expert_id = iota((z.experts, tk), 0)
    chosen = [
        jnp.sum(jnp.where(expert_id == r, logits, 0.0), axis=0, keepdims=True) for r in r_row
    ]
    top = jnp.maximum(chosen[0], chosen[1])
    raw = [jnp.exp(c - top) for c in chosen]
    total = raw[0] + raw[1]
    gate_rows = [r / total for r in raw]
    cols8[0:tk, :] = jnp.transpose(
        jnp.concatenate(gate_rows + [jnp.zeros((6, tk), F32)], axis=0)
    )
    gate = [cols8[0:tp, k : k + 1] for k in range(2)]

    slot_lane = iota((tk, LANE), 1)
    pad_col = [
        jnp.concatenate([j, jnp.full((tk - tp, 1), -1, jnp.int32)], axis=0) for j in j_col
    ]
    at_slot = [one(slot_lane == j) for j in pad_col]
    halves = [split(g) for g in gate_rows]
    for k in SEND_ORDER:
        g = group_at(k)
        number = None
        for c in range(2):
            high, low = halves[c]
            at = r_row[c] * 16 + (gate_row - g * (per * 16))
            lift = jnp.where(
                sent_row[c] & (tail_id == at), high.astype(F32), 0.0
            ) + jnp.where(sent_row[c] & (tail_id == at + 1), low.astype(F32), 0.0)
            piece = dot(lift.astype(BF16), at_slot[c])
            number = piece if number is None else number + piece
        place(n2, 1, g, number)
        a2a_send(1, k)

    for k in range(GROUPS):
        a2a_forward(0, k)
    for k in range(GROUPS):
        a2a_take(0, k)
        assemble(0, group_at(k), u_s)
    weights[2].wait()
    gh[...] = dot_bt(u_s[...], wout[...])

    weights[3].wait()
    parts = [(0, z.gm, z.main, 0)] if z.main else []
    parts += [(z.gm, z.gt, z.tail, z.main)]
    step = 16

    def activate(g):
        def go(i, carry):
            here = pl.ds(pl.multiple_of(i * step, step), step)
            rows = pl.ds(pl.multiple_of(g * z.rows + i * step, step), step)
            v = pre[here, :] + bin_ref[...]
            v2 = v * v
            s = 0.5 + 0.5 * jnp.tanh(v * (ROOT + (ROOT * CUBE) * v2))
            act = v * s
            back = s + act * (1.0 - s) * (2.0 * ROOT + (6.0 * ROOT * CUBE) * v2)
            up = gh[rows, :]
            hid[rows, :] = act.astype(BF16)
            gp[rows, :] = (gcol_s[rows, :] * up * back).astype(BF16)
            ggv[rows, :] = jnp.sum(up * act, axis=-1, keepdims=True)
            return carry

        lax.fori_loop(0, z.rows // step, go, 0)

    bias_half = bout_ref[:, pl.ds(mine, half)]

    def swap_of(j, k):
        return remote(half_out.at[j, k], half_in.at[j, k], hs.at[j, k], hr.at[j, k], sib)

    def slots_in(k):
        g = group_at(k)
        a2a_take(1, k)
        assemble(1, g, x_s)
        tail = tail_of(1, r_msg, g)
        for at, rows, each, first in parts:
            q, r = iota((rows, per * 16), 0), iota((rows, per * 16), 1)
            number = r - q // each * 16
            pick = one((number == gate_row) | (number == gate_row + 1))
            lane = iota((rows, LANE), 1) == iota((rows, LANE), 0) % each + first
            gcol_s[rows_of(g, at, rows), :] = jnp.sum(
                jnp.where(lane, dot(pick, tail), 0.0), axis=-1, keepdims=True
            )
        pre[...] = dot(x_s[rows_of(g), :], win[...])
        activate(g)
        back = gp[rows_of(g), :]
        half_out[0, k] = dot_bt(back, win[pl.ds(other, half), :]).astype(BF16)
        swap_of(0, k).start()
        half_own[k] = dot_bt(back, win[pl.ds(mine, half), :])

    def slots_back(k):
        g = group_at(k)
        gg = ggv[rows_of(g), :] + jnp.sum(
            u_s[rows_of(g), pl.ds(mine, half)].astype(F32) * bias_half, axis=-1, keepdims=True
        )
        number = None
        for at, rows, each, first in parts:
            q, r = iota((per * 16, rows), 1), iota((per * 16, rows), 0)
            lane = iota((rows, LANE), 1) == iota((rows, LANE), 0) % each + first
            high, low = split(jnp.where(lane, gg[at : at + rows, :], 0.0))
            line = r - q // each * 16
            piece = dot(one(line == gate_row), high) + dot(one(line == gate_row + 1), low)
            number = piece if number is None else number + piece
        swap_of(0, k).wait()
        pack(2, g, (half_own[k] + half_in[0, k].astype(F32)).astype(BF16), number)
        a2a_send(2, k)

    a2a_forward(1, 0)
    a2a_forward(1, 1)
    for k in range(GROUPS):
        slots_in(k)
        if k + 2 < GROUPS:
            a2a_forward(1, k + 2)
        if k > 0:
            slots_back(k - 1)
    slots_back(GROUPS - 1)

    for k in range(GROUPS):
        act = hid[rows_of(group_at(k)), :]
        half_out[1, k] = dot(act, wout[:, pl.ds(other, half)]).astype(BF16)
        swap_of(1, k).start()
        half_own[k] = dot(act, wout[:, pl.ds(mine, half)]) + bias_half
    for k in range(GROUPS):
        swap_of(1, k).wait()
        pack(3, group_at(k), (half_own[k] + half_in[1, k].astype(F32)).astype(BF16), None)

    sg[...] = (gcol_s[...] * u_s[...].astype(F32)).astype(BF16)
    x_t[...] = jnp.transpose(x_s[...])
    hid_t[...] = jnp.transpose(hid[...])
    o_beo[...] = jnp.sum(sg[...].astype(F32), axis=0, keepdims=True)
    o_bei[...] = jnp.sum(gp[...].astype(F32), axis=0, keepdims=True)
    stores = [
        pltpu.make_async_copy(a, b, osem.at[i])
        for i, (a, b) in enumerate(((x_t, o_x), (sg, o_sg), (hid_t, o_hid), (gp, o_gp)))
    ]
    for copy in stores:
        copy.start()
    mix_t = jnp.transpose(mix[...])

    flat_id = iota((tp, z.slots), 1)
    back_one = [one(flat_id == f) for f in flat_col]
    for k in range(GROUPS):
        a2a_forward(2, k)
    for k in SEND_ORDER:
        a2a_send(3, k)
    tail_lane = iota((tp, per * 16), 1)
    number = [None, None]
    for k in range(GROUPS):
        g = group_at(k)
        a2a_take(2, k)
        assemble(2, g, y_s)
        tails = [tail_of(2, r_msg, g), tail_of(2, f_msg, g)]
        for c in range(2):
            at = r_col[c] * 16 + (gate_row - g * (per * 16))
            pick = one(sent_col[c] & ((tail_lane == at) | (tail_lane == at + 1)))
            piece = dot(pick, tails[0]) + dot(pick, tails[1])
            number[c] = piece if number[c] is None else number[c] + piece
    grad_gate = [
        jnp.sum(
            jnp.where(iota((tp, LANE), 1) == j_col[c], number[c], 0.0), axis=-1, keepdims=True
        )
        for c in range(2)
    ]
    mean_gate = gate[0] * grad_gate[0] + gate[1] * grad_gate[1]
    e_pad = up_to(z.experts, LANE)
    e_lane = iota((tp, e_pad), 1)
    grad_logits = jnp.where(
        e_lane == r_col[0], gate[0] * (grad_gate[0] - mean_gate), 0.0
    ) + jnp.where(e_lane == r_col[1], gate[1] * (grad_gate[1] - mean_gate), 0.0)
    gl_high, gl_low = split(grad_logits)
    router_pad = router_ref[...]
    if e_pad > z.experts:
        router_pad = jnp.concatenate(
            [router_pad, jnp.zeros((e_pad - z.experts, width), BF16)], axis=0
        )
    grad_n2 = (
        dot(back_one[0] + back_one[1], y_s[...])
        + dot(gl_high, router_pad)
        + dot(gl_low, router_pad)
    )
    grad_router = dot_at(gl_high, n2[0:tp, :]) + dot_at(gl_low, n2[0:tp, :])
    smallf[...] = jnp.zeros(smallf.shape, F32)
    ne = z.experts
    smallf[0:ne, :] = grad_router[0:ne, :]
    normal = normal2[...]
    smallf[ne + 2 : ne + 3, :] = jnp.sum(grad_n2 * normal, axis=0, keepdims=True)
    smallf[ne + 3 : ne + 4, :] = jnp.sum(grad_n2, axis=0, keepdims=True)
    gm[...] = upk[0:tp, :].astype(F32) + norm_backward(grad_n2, normal, inverse2, row_of(ln2g_ref))
    ag[tp:, :] = jnp.zeros((tk - tp, width), BF16)
    ag[0:tp, :] = gm[...].astype(BF16)
    smallf[ne + 4 : ne + 5, :] = jnp.sum(ag[...].astype(F32), axis=0, keepdims=True)

    groups = []
    for order in chain_orders(z.bits) + [z.bits]:
        start, size, steps = 0, n, []
        for b in order:
            bit = lax.rem(me // b, 2)
            peer = me + b * (1 - 2 * bit)
            size = size // 2
            steps.append((peer, start + (1 - bit) * size, start + bit * size, size))
            start = start + bit * size
        groups.append((steps, start))
    n_main = len(groups) - 1

    def chain_of(g):
        if g < n_main:
            return chain_g.at[g], [r.at[g] for r in chain_r], chain_a.at[g], z.chunk
        return chain_small, list(small_r), small_a, z.small

    def region(ref, at, count, rows):
        return ref.at[pl.ds(pl.multiple_of(at * rows, 16), count * rows)]

    def rs_copy(g, s):
        src, bufs, _, rows = chain_of(g)
        peer, give, _, size = groups[g][0][s]
        return remote(
            region(src, give, size, rows), bufs[s], cs.at[g], cr.at[g, s], (peer, core)
        )

    def rs_add(g, s, at, count, dst):
        src, bufs, _, rows = chain_of(g)
        keep = groups[g][0][s][2]

        def go(i, carry):
            here = pl.ds(pl.multiple_of((at + i) * rows, 16), rows)
            there = pl.ds(pl.multiple_of((at + i - keep) * rows, 16), rows)
            dst[here, :] = (src[here, :].astype(F32) + bufs[s][there, :].astype(F32)).astype(BF16)
            return carry

        lax.fori_loop(0, count, go, 0)

    def rs_step(g, s):
        src, _, out, _ = chain_of(g)
        rs_copy(g, s).wait()
        if s + 1 < nbits:
            _, give, keep, size = groups[g][0][s + 1]
            rs_add(g, s, give, size, src)
            rs_copy(g, s + 1).start()
            rs_add(g, s, keep, size, src)
        else:
            rs_add(g, s, groups[g][1], 1, out)
            ag_copy(g, s).start()

    def ag_copy(g, s):
        _, _, out, rows = chain_of(g)
        peer, _, keep, size = groups[g][0][s]
        piece = region(out, keep, size, rows)
        return remote(piece, piece, as_.at[g], ar.at[g, s], (peer, core))

    def ag_step(g, s):
        _, _, out, rows = chain_of(g)
        peer, give, _, size = groups[g][0][s]
        ag_copy(g, s).wait_send()
        piece = region(out, give, size, rows)
        remote(piece, piece, as_.at[g], ar.at[g, s], (peer, core)).wait_recv()
        if s > 0:
            ag_copy(g, s - 1).start()

    filled = 0

    def fill(value):
        nonlocal filled
        rows = value.shape[0]
        for b in range(value.shape[1] // LANE):
            g, at = divmod(filled, z.chain_rows)
            chain_g[g, at : at + rows, :] = value[:, b * LANE : (b + 1) * LANE].astype(BF16)
            filled += rows
            if filled == (g + 1) * z.chain_rows:
                rs_copy(g, 0).start()

    if z.chain_rows < n * z.chunk:
        for g in range(n_main):
            chain_g[g, z.chain_rows :, :] = jnp.zeros((n * z.chunk - z.chain_rows, LANE), BF16)
    fill(dot(mix_t, ag[...]))

    dm[...] = dot_bt(ag[0:tp, :], wo[...]).astype(BF16)
    for p in range(z.pairs):
        lanes = slice(p * LANE, (p + 1) * LANE)
        qp, kp, vp, dp = q_s[0:tp, lanes], k_s[:, lanes], v_s[:, lanes], dm[:, lanes]
        dq, dk, dv = [], [], []
        for h in range(2):
            prob = probs[2 * p + h]
            gprob = dot_bt(dp * head_mask[h], vp)
            inner = jnp.sum(prob * gprob, axis=-1, keepdims=True)
            gs = (prob * (gprob - inner)).astype(BF16)
            dq.append(dot(gs, kp))
            dk.append(dot_at(gs, qp))
            dv.append(dot_at(prob.astype(BF16), dp))
        for c, (pair, scale) in enumerate(((dq, score_scale), (dk, score_scale), (dv, 1.0))):
            value = (jnp.where(low_lane, pair[0], pair[1]) * scale).astype(BF16)
            at = slice(c * hw + p * LANE, c * hw + (p + 1) * LANE)
            if c == 0:
                gpr[0:tp, at] = value
                gpr[tp:, at] = jnp.zeros((tk - tp, LANE), BF16)
            else:
                gpr[:, at] = value
        joined = jnp.concatenate(
            [gpr[:, c * hw + p * LANE : c * hw + (p + 1) * LANE] for c in range(3)], axis=1
        )
        fill(dot(n1t[...], joined))

    head_part = None
    for c in range(3):
        piece = dot_bt(gpr[0:tp, c * hw : (c + 1) * hw], wqkv[c])
        head_part = piece if head_part is None else head_part + piece
    gn_out[...] = head_part.astype(BF16)
    swap = remote(gn_out, gn_in, hs.at[2, 1], hr.at[2, 1], sib)
    swap.start()
    smallf[ne + 5 : ne + 6, 0:hw] = jnp.sum(gpr[:, 0:hw].astype(F32), axis=0, keepdims=True)
    smallf[ne + 6 : ne + 7, 0:hw] = jnp.sum(
        gpr[:, 2 * hw : 3 * hw].astype(F32), axis=0, keepdims=True
    )
    swap.wait()
    grad_n1 = gn_out[...].astype(F32) + gn_in[...].astype(F32)
    normal = normal1[...]
    smallf[ne : ne + 1, :] = jnp.sum(grad_n1 * normal, axis=0, keepdims=True)
    smallf[ne + 1 : ne + 2, :] = jnp.sum(grad_n1, axis=0, keepdims=True)
    back = gm[...] + norm_backward(grad_n1, normal, inverse1, row_of(ln1g_ref))
    gtok_out[...] = back[0:tok, :]
    copy = pltpu.make_async_copy(gtok_out, o_gtok, osem.at[4])
    copy.start()
    stores.append(copy)
    used = z.small_rows * (width // LANE)
    for b in range(width // LANE):
        chain_small[b * z.small_rows : (b + 1) * z.small_rows, :] = smallf[
            :, b * LANE : (b + 1) * LANE
        ].astype(BF16)
    if used < n * z.small:
        chain_small[used:, :] = jnp.zeros((n * z.small - used, LANE), BF16)
    rs_copy(n_main, 0).start()

    for k in range(GROUPS):
        a2a_forward(3, k)
    for k in range(GROUPS):
        a2a_take(3, k)
        assemble(3, group_at(k), y_s)
    branch = gate[0] * dot(back_one[0], y_s[...]) + gate[1] * dot(back_one[1], y_s[...])
    output = mid[...] + branch
    tok_out[...] = output[0:tok, :].astype(BF16)
    copy = pltpu.make_async_copy(tok_out, o_tok, osem.at[5])
    copy.start()
    stores.append(copy)
    lane_id = iota((1, LANE), 1)
    x_all = xf[...]
    line = jnp.zeros((1, LANE), F32)
    for i, number in enumerate(
        (
            jnp.sum(keep_col * x_all * x_all),
            stat_attn,
            jnp.sum(keep_col * branch * branch),
            jnp.sum(keep_col * output * output),
            jnp.sum(keep_col),
        )
    ):
        line = jnp.where(lane_id == i, number, line)
    stat[me] = jnp.broadcast_to(line, (8, LANE))

    def stat_go(j, carry):
        p = lax.rem(me + j, n)
        remote(stat.at[me], stat.at[me], st.at[0], st.at[1], (p, core)).start()
        return carry

    lax.fori_loop(1, n, stat_go, 0)

    for s in range(nbits):
        for g in range(n_main + 1):
            rs_step(g, s)

    block = stat.at[pl.ds(0, n - 1)]
    remote(block, block, st.at[0], st.at[1], sib).wait()
    totals = jnp.sum(stat[...], axis=0)
    count = jnp.sum(jnp.where(iota((8, LANE), 1) == 4, totals, 0.0), axis=-1, keepdims=True)
    o_rms[...] = jnp.sqrt(totals / (count * width))

    for s in range(nbits - 1, -1, -1):
        for g in range(n_main + 1):
            ag_step(g, s)
    for g in range(n_main):
        copy = pltpu.make_async_copy(chain_a.at[g], o_red.at[g], osem.at[6 + g])
        copy.start()
        stores.append(copy)
    for b in range(width // LANE):
        o_small[:, b * LANE : (b + 1) * LANE] = small_a[
            b * z.small_rows : (b + 1) * z.small_rows, :
        ].astype(F32)
    for i in range(4):
        a2a_sent(i)
    for copy in stores:
        copy.wait()


def last_kernel(
    z,
    i_tok,
    i_gtok,
    i_x,
    i_sg,
    i_hid,
    i_gp,
    i_red,
    i_small,
    i_bei,
    i_beo,
    i_rms,
    o_tok,
    o_gtok,
    o_ln1g,
    o_ln1b,
    o_wqkv,
    o_bqv,
    o_wo,
    o_bo,
    o_ln2g,
    o_ln2b,
    o_router,
    o_win,
    o_bin,
    o_wout,
    o_bout,
    o_rms,
    x_t,
    sg,
    hid_t,
    gp,
    red,
    wqkv,
    wo,
    win,
    wout,
    tok_s,
    gtok_s,
    isem,
    osem,
):
    ne, width, hw = z.experts, z.width, z.hw
    loads = [
        pltpu.make_async_copy(i_red.at[g], red.at[g], isem.at[6 + g]) for g in range(z.chains)
    ]
    loads += [
        pltpu.make_async_copy(a, b, isem.at[i])
        for i, (a, b) in enumerate(
            (
                (i_x, x_t),
                (i_gp, gp),
                (i_hid, hid_t),
                (i_sg, sg),
                (i_tok, tok_s),
                (i_gtok, gtok_s),
            )
        )
    ]
    for copy in loads:
        copy.start()
    stores = []

    def store(src, dst, i):
        copy = pltpu.make_async_copy(src, dst, osem.at[i])
        copy.start()
        stores.append(copy)

    for ref, i in ((o_ln1g, 0), (o_ln1b, 1), (o_ln2g, 2), (o_ln2b, 3), (o_bo, 4)):
        ref[...] = i_small[ne + i : ne + i + 1, :].reshape(width)
    o_router[...] = i_small[0:ne, :]
    o_bqv[...] = i_small[ne + 5 : ne + 7, 0:hw]
    o_bin[...] = i_bei[...]
    o_bout[...] = i_beo[...]
    o_rms[...] = i_rms[0:1, 0:4].reshape(4)

    at, ready = 0, 0

    def take(rows):
        nonlocal at, ready
        g, row = divmod(at, z.chain_rows)
        if g == ready:
            loads[g].wait()
            ready += 1
        at += rows
        return red[g, row : row + rows, :].astype(F32)

    for b in range(width // LANE):
        wo[:, b * LANE : (b + 1) * LANE] = take(hw)
    store(wo, o_wo, 2)
    for p in range(z.pairs):
        for c in range(3):
            wqkv[c, :, p * LANE : (p + 1) * LANE] = take(width)
    store(wqkv, o_wqkv, 3)
    for i in range(2):
        loads[z.chains + i].wait()
    tiles = z.ff // TILE
    for t in range(tiles):
        cols = slice(t * TILE, (t + 1) * TILE)
        win[:, cols] = dot(x_t[...], gp[:, cols])
        store(win.at[:, cols], o_win.at[0, :, cols], 4 + t)
    for i in range(2, 4):
        loads[z.chains + i].wait()
    for t in range(tiles):
        rows = slice(t * TILE, (t + 1) * TILE)
        wout[rows, :] = dot(hid_t[rows, :], sg[...])
        store(wout.at[rows, :], o_wout.at[0, rows, :], 4 + tiles + t)
    for i, (src, dst) in enumerate(((tok_s, o_tok), (gtok_s, o_gtok))):
        loads[z.chains + 4 + i].wait()
        store(src, dst, i)
    for copy in stores:
        copy.wait()


def per_device(
    tokens,
    grad_out,
    valid_mask,
    routes,
    slot_index,
    ln1_gain,
    ln1_bias,
    w_qkv,
    bias_qv,
    w_attn_out,
    b_attn_out,
    ln2_gain,
    ln2_bias,
    router,
    w_expert_in,
    b_expert_in,
    w_expert_out,
    b_expert_out,
):
    tok, width = tokens.shape
    hw = w_qkv.shape[2]
    ff = w_expert_in.shape[2]
    z = Sizes(lax.axis_size("dp"), tok, width, hw, ff, router.shape[1])
    n, tp, tk = z.n, z.tp, z.tk
    nbits = len(z.bits)
    vmem = pl.BlockSpec(memory_space=pltpu.VMEM)
    any_ = pl.BlockSpec(memory_space=pl.ANY)
    shape = jax.ShapeDtypeStruct
    groups = z.chains
    V = pltpu.VMEM
    scratch = [
        V((tok, width), BF16),
        V((tok, width), BF16),
        V((tok, width), BF16),
        V((tok, width), F32),
        V((3, width, hw), BF16),
        V((hw, width), BF16),
        V((width, ff), BF16),
        V((ff, width), BF16),
        V((tp, width), F32),
        V((tp, width), F32),
        V((tk, width), BF16),
        V((width, tk), BF16),
        V((tk, width), BF16),
        V((tk, hw), BF16),
        V((tk, hw), BF16),
        V((tk, hw), BF16),
        V((2 * z.pairs, tp, tk), F32),
        V((tk, hw), BF16),
        V((tp, width), F32),
        V((tp, width), F32),
        V((tp, width), F32),
        V((tp, width), F32),
        V((tk, width), BF16),
        V((z.slots, tk), BF16),
        V((8, tk), F32),
        V((tk, 8), F32),
        V((z.slots, width), BF16),
        V((z.slots, width), BF16),
        V((z.slots, width), BF16),
        V((z.slots, ff), F32),
        V((z.rows, ff), F32),
        V((z.slots, ff), BF16),
        V((z.slots, ff), BF16),
        V((z.slots, width), BF16),
        V((width, z.slots), BF16),
        V((ff, z.slots), BF16),
        V((z.slots, 1), F32),
        V((z.slots, 1), F32),
        V((2, GROUPS, z.rows, z.half), BF16),
        V((2, GROUPS, z.rows, z.half), BF16),
        V((GROUPS, z.rows, z.half), F32),
        V((tp, width), F32),
        V((tk, width), BF16),
        V((tp, hw), BF16),
        V((tk, 3 * hw), BF16),
        V((tp, width), BF16),
        V((tp, width), BF16),
        V((z.small_rows, width), F32),
        V((n, 8, LANE), F32),
        V((4, n, z.msg, LANE), BF16),
        V((4, n, z.msg, LANE), BF16),
        V((4, n, z.msg, LANE), BF16),
        V((groups, n * z.chunk, LANE), BF16),
        V((n * z.small, LANE), BF16),
    ]
    scratch += [V((groups, (n >> (s + 1)) * z.chunk, LANE), BF16) for s in range(nbits)]
    scratch += [V(((n >> (s + 1)) * z.small, LANE), BF16) for s in range(nbits)]
    scratch += [
        V((groups, n * z.chunk, LANE), BF16),
        V((n * z.small, LANE), BF16),
        DMA((6,)),
        DMA((6 + groups,)),
        DMA((3, GROUPS)),
        DMA((3, GROUPS)),
        DMA((4,)),
        DMA((4, GROUPS)),
        DMA((4,)),
        DMA((4, GROUPS)),
        DMA((groups + 1,)),
        DMA((groups + 1, nbits)),
        DMA((groups + 1,)),
        DMA((groups + 1, nbits)),
        DMA((2,)),
    ]
    row = lambda v: v.reshape(1, -1)
    outs = pl.pallas_call(
        functools.partial(mega_kernel, z),
        out_shape=(
            shape((tok, width), BF16),
            shape((tok, width), F32),
            shape((width, z.slots), BF16),
            shape((z.slots, width), BF16),
            shape((ff, z.slots), BF16),
            shape((z.slots, ff), BF16),
            shape((groups, n * z.chunk, LANE), BF16),
            shape((z.small_rows, width), F32),
            shape((1, ff), F32),
            shape((1, width), F32),
            shape((8, LANE), F32),
        ),
        in_specs=[any_] * 2
        + [vmem] * 5
        + [any_, vmem, any_, vmem, vmem, vmem, vmem, any_, vmem, any_, vmem],
        out_specs=(any_,) * 7 + (vmem,) * 4,
        scratch_shapes=scratch,
        compiler_params=pltpu.CompilerParams(
            collective_id=0, has_side_effects=True, vmem_limit_bytes=60 * 2**20
        ),
    )(
        tokens,
        grad_out,
        row(valid_mask),
        routes.T,
        slot_index.T,
        ln1_gain,
        ln1_bias,
        jnp.transpose(w_qkv, (1, 0, 2)),
        bias_qv,
        w_attn_out,
        b_attn_out,
        ln2_gain,
        ln2_bias,
        router.T,
        w_expert_in[0],
        b_expert_in,
        w_expert_out[0],
        b_expert_out,
    )
    o_tok, o_gtok, o_x, o_sg, o_hid, o_gp, o_red, o_small, o_bei, o_beo, o_rms = outs
    ne = z.experts
    vec = shape((width,), F32)
    last = pl.pallas_call(
        functools.partial(last_kernel, z),
        out_shape=(
            shape((tok, width), BF16),
            shape((tok, width), F32),
            vec,
            vec,
            shape((3, width, hw), F32),
            shape((2, hw), F32),
            shape((hw, width), F32),
            vec,
            vec,
            vec,
            shape((ne, width), F32),
            shape((1, width, ff), F32),
            shape((1, ff), F32),
            shape((1, ff, width), F32),
            shape((1, width), F32),
            shape((4,), F32),
        ),
        in_specs=[any_] * 7 + [vmem] * 4,
        out_specs=(
            [any_] * 2
            + [vmem] * 2
            + [any_, vmem, any_]
            + [vmem] * 4
            + [any_, vmem, any_, vmem, vmem]
        ),
        scratch_shapes=[
            V((width, z.slots), BF16),
            V((z.slots, width), BF16),
            V((ff, z.slots), BF16),
            V((z.slots, ff), BF16),
            V((groups, n * z.chunk, LANE), BF16),
            V((3, width, hw), F32),
            V((hw, width), F32),
            V((width, ff), F32),
            V((ff, width), F32),
            V((tok, width), BF16),
            V((tok, width), F32),
            DMA((6 + groups,)),
            DMA((4 + 2 * (ff // TILE),)),
        ],
        compiler_params=pltpu.CompilerParams(vmem_limit_bytes=60 * 2**20),
    )(o_tok, o_gtok, o_x, o_sg, o_hid, o_gp, o_red, o_small, o_bei, o_beo, o_rms)
    return (
        last[0],
        last[1],
        last[2],
        last[3],
        jnp.transpose(last[4], (1, 0, 2)),
        *last[5:10],
        last[10].T,
        *last[11:],
    )


def solution(mesh):
    return jax.shard_map(
        per_device,
        mesh=mesh,
        in_specs=(
            P("dp", None),
            P("dp", None),
            P("dp"),
            P("dp", None),
            P("dp", None),
            P(),
            P(),
            P(None, None, "tensor"),
            P(None, "tensor"),
            P("tensor", None),
            P(),
            P(),
            P(),
            P(),
            P("dp", None, "tensor"),
            P("dp", "tensor"),
            P("dp", "tensor", None),
            P("dp", None),
        ),
        out_specs=(
            P("dp", None),
            P("dp", None),
            P(),
            P(),
            P(None, None, "tensor"),
            P(None, "tensor"),
            P("tensor", None),
            P(),
            P(),
            P(),
            P(),
            P("dp", None, "tensor"),
            P("dp", "tensor"),
            P("dp", "tensor", None),
            P("dp", None),
            P(),
        ),
        check_vma=False,
    )
```

```python
import functools
import math

import jax
import jax.numpy as jnp
from jax import lax
from jax.experimental import pallas as pl
from jax.experimental.pallas import tpu as pltpu
from jax.sharding import PartitionSpec as P

HEAD = 64
SEQ = 197
LANE = 128
EPS = 1e-06
ROOT = math.sqrt(2.0 / math.pi)
CUBE = 0.044715
GROUPS = 4
LAST = 5
ORDERS = (
    (0, 1, 3, 2),
    (1, 3, 0, 2),
    (2, 0, 1, 3),
    (0, 2, 1, 3),
    (1, 0, 3, 2),
    (2, 1, 0, 3),
    (3, 0, 1, 2),
    (2, 1, 0, 3),
    (1, 0, 2, 3),
    (1, 3, 0, 2),
    (0, 1, 2, 3),
    (0, 3, 1, 2),
)
STEPS = (
    (5, 0, 0), (5, 1, 0), (5, 2, 0), (5, 4, 0), (5, 12, 0), (5, 3, 0), (5, 8, 0), (5, 5, 0),
    (5, 9, 0), (5, 10, 0), (5, 11, 0), (5, 0, 1), (5, 7, 0), (5, 6, 0), (5, 12, 1), (5, 2, 1),
    (5, 4, 1), (5, 1, 1), (5, 3, 1), (5, 8, 1), (5, 5, 1), (5, 10, 1), (5, 7, 1), (5, 9, 1),
    (5, 12, 2), (5, 6, 1), (5, 2, 2), (5, 1, 2), (5, 0, 2), (5, 3, 2), (5, 5, 2), (5, 4, 2),
    (5, 11, 1), (5, 8, 2), (5, 7, 2), (5, 12, 3), (5, 10, 2), (5, 9, 2), (5, 6, 2), (5, 2, 3),
    (5, 1, 3), (5, 0, 3), (5, 3, 3), (5, 5, 3), (5, 4, 3), (5, 11, 2), (5, 12, -4), (5, 8, 3),
    (5, 7, 3), (5, 9, 3), (5, 10, 3), (5, 6, 3), (5, 2, -4), (5, 1, -4), (5, 0, -4), (5, 3, -4),
    (5, 12, -3), (5, 5, -4), (5, 4, -4), (5, 11, 3), (5, 8, -4), (5, 7, -4), (5, 9, -4),
    (5, 10, -4), (5, 6, -4), (5, 2, -3), (5, 1, -3), (5, 5, -3), (5, 12, -2), (5, 3, -3),
    (5, 11, -4), (5, 0, -3), (5, 7, -3), (5, 4, -3), (5, 6, -3), (5, 9, -3), (5, 8, -3),
    (5, 10, -3), (5, 12, -1), (5, 2, -2), (5, 5, -2), (5, 1, -2), (5, 11, -3), (5, 3, -2),
    (5, 0, -2), (5, 9, -2), (5, 4, -2), (5, 6, -2), (5, 7, -2), (5, 8, -2), (5, 10, -2),
    (5, 11, -2), (5, 3, -1), (5, 1, -1), (5, 0, -1), (5, 2, -1), (5, 5, -1), (5, 10, -1),
    (5, 9, -1), (5, 4, -1), (5, 11, -1), (5, 8, -1), (5, 6, -1), (5, 7, -1),
)
SEND_ORDER = (0, 2, 1, 3)
TILE = 256
MESH = pl.DeviceIdType.MESH
F32 = jnp.float32
BF16 = jnp.bfloat16
DMA = pltpu.SemaphoreType.DMA


def up_to(value, step):
    return -(-value // step) * step


def dot(a, b):
    return lax.dot_general(a, b, (((1,), (0,)), ((), ())), preferred_element_type=F32)


def dot_bt(a, b):
    return lax.dot_general(a, b, (((1,), (1,)), ((), ())), preferred_element_type=F32)


def dot_at(a, b):
    return lax.dot_general(a, b, (((0,), (0,)), ((), ())), preferred_element_type=F32)


def row_of(ref):
    return ref[...].reshape(1, ref.shape[0])


def iota(shape, dim):
    return lax.broadcasted_iota(jnp.int32, shape, dim)


def one(cond, kind=BF16):
    return jnp.where(cond, 1.0, 0.0).astype(kind)


def split(value):
    high = value.astype(BF16)
    return high, (value - high.astype(F32)).astype(BF16)


def norm_parts(values):
    scale = 1.0 / values.shape[-1]
    center = values - jnp.sum(values, axis=-1, keepdims=True) * scale
    inverse = lax.rsqrt(jnp.sum(center * center, axis=-1, keepdims=True) * scale + EPS)
    return center * inverse, inverse


def norm_backward(incoming, normal, inverse, gain_vec):
    scale = 1.0 / incoming.shape[-1]
    scaled = incoming * gain_vec
    return inverse * (
        scaled
        - jnp.sum(scaled, axis=-1, keepdims=True) * scale
        - normal * (jnp.sum(scaled * normal, axis=-1, keepdims=True) * scale)
    )


def remote(src, dst, send_sem, recv_sem, device):
    return pltpu.make_async_remote_copy(
        src_ref=src,
        dst_ref=dst,
        send_sem=send_sem,
        recv_sem=recv_sem,
        device_id=device,
        device_id_type=MESH,
    )


class Sizes:
    def __init__(self, n, tok, width, heads_width, ff, experts):
        self.n = n
        self.tok = tok
        self.tp = up_to(tok, 16)
        self.tk = up_to(tok, LANE)
        self.width = width
        self.hw = heads_width
        self.pairs = heads_width // LANE
        self.ff = ff
        self.experts = experts
        self.cap = 2 * (3 * tok // (2 * n))
        self.main = self.cap // 16 * 16
        self.tail = self.cap - self.main
        self.half = width // 2
        self.blocks = self.half // LANE
        self.msg = self.main * self.blocks + 16
        self.per = n // GROUPS
        self.gm = self.per * self.main
        self.gt = self.per * self.tail
        self.rows = self.per * self.cap
        self.slots = n * self.cap
        self.bits = [1 << i for i in range(n.bit_length() - 1)]
        self.pack_rows = 4 * heads_width * width // LANE
        self.chains = 12 if n <= 16 else 6
        self.chain_rows = self.pack_rows // self.chains
        self.chunk = up_to(up_to(self.chain_rows, n) // n, 16)
        self.small_rows = up_to(experts + 7, 16)
        self.small = up_to(up_to(self.small_rows * width // LANE, n) // n, 16)
        fits = 0 < self.tail * self.blocks <= 14 and self.gt % 16 == 0
        fits = fits and self.chain_rows % heads_width == 0 and self.chain_rows % width == 0
        if not fits or experts != n or (1 << len(self.bits)) != n:
            raise ValueError("unsupported sizes")


def chain_orders(bits, chains):
    if len(bits) == 4 and chains == len(ORDERS):
        return [[bits[i] for i in order] for order in ORDERS]
    if len(bits) < 3:
        return [bits] * chains
    order = ((0, 1, 2), (1, 2, 0), (2, 0, 1), (0, 2, 1), (1, 0, 2), (2, 1, 0))
    return [[bits[i] for i in order[c % 6]] + bits[3:] for c in range(chains)]


def chain_steps(bits, chains):
    if len(bits) == 4 and chains == len(ORDERS):
        return STEPS
    steps = [(LAST, c, s) for s in range(len(bits)) for c in range(chains + 1)]
    return steps + [
        (LAST, c, -1 - s) for s in range(len(bits) - 1, -1, -1) for c in range(chains + 1)
    ]


def mega_kernel(
    z,
    tokens_hbm,
    grad_out_hbm,
    valid_hbm,
    routes_hbm,
    slots_hbm,
    ln1g_hbm,
    ln1b_hbm,
    wqkv_hbm,
    bqv_hbm,
    wo_hbm,
    bo_hbm,
    ln2g_hbm,
    ln2b_hbm,
    router_hbm,
    win_hbm,
    bin_hbm,
    wout_hbm,
    bout_hbm,
    o_tok,
    o_gtok,
    o_x,
    o_sg,
    o_hid,
    o_gp,
    o_red,
    o_small,
    o_bei,
    o_beo,
    o_rms,
    tokens_ref,
    grad_out_ref,
    valid_ref,
    routes_ref,
    slots_ref,
    ln1g_ref,
    ln1b_ref,
    bqv_ref,
    bo_ref,
    ln2g_ref,
    ln2b_ref,
    router_ref,
    bin_ref,
    bout_ref,
    tok_out,
    gtok_out,
    wqkv,
    wo,
    win,
    wout,
    xf,
    normal1,
    n1,
    n1t,
    upk,
    q_s,
    k_s,
    v_s,
    probs,
    mix,
    part,
    part_in,
    mid,
    normal2,
    n2,
    onehot,
    rows8,
    cols8,
    u_s,
    x_s,
    y_s,
    gh,
    pre,
    hid,
    gp,
    sg,
    x_t,
    hid_t,
    gcol_s,
    ggv,
    half_out,
    half_in,
    half_own,
    whole,
    win_t,
    gm,
    ag,
    dm,
    gpr,
    gn_out,
    gn_in,
    smallf,
    stat,
    s_msg,
    r_msg,
    f_msg,
    chain_g,
    chain_small,
    *rest,
):
    nbits = len(z.bits)
    chain_r = rest[:nbits]
    small_r = rest[nbits : 2 * nbits]
    chain_a, small_a, wsem, osem, hs, hr, ss, rs, fs, fr, cs, cr, as_, ar, st = rest[
        2 * nbits :
    ]
    n = z.n
    me, core = lax.axis_index("dp"), lax.axis_index("tensor")
    sib = (me, 1 - core)
    tok, tp, tk, width, hw, half = z.tok, z.tp, z.tk, z.width, z.hw, z.half
    mine = pl.multiple_of(core * half, LANE)
    other = pl.multiple_of((1 - core) * half, LANE)

    barrier = pltpu.get_barrier_semaphore()

    def greet(j, carry):
        pl.semaphore_signal(
            barrier, inc=1, device_id=(lax.rem(me + j, n), core), device_id_type=MESH
        )
        return carry

    lax.fori_loop(1, n, greet, 0)
    pl.semaphore_signal(barrier, inc=1, device_id=sib, device_id_type=MESH)

    tokens_in = [
        pltpu.make_async_copy(a, b, wsem.at[4 + i])
        for i, (a, b) in enumerate(((tokens_hbm, tokens_ref), (grad_out_hbm, grad_out_ref)))
    ]
    small_in = [
        pltpu.make_async_copy(a, b, wsem.at[6 + i])
        for i, (a, b) in enumerate(
            (
                (valid_hbm, valid_ref),
                (routes_hbm, routes_ref),
                (slots_hbm, slots_ref),
                (ln1g_hbm, ln1g_ref),
                (ln1b_hbm, ln1b_ref),
                (bqv_hbm, bqv_ref),
                (bo_hbm, bo_ref),
                (ln2g_hbm, ln2g_ref),
                (ln2b_hbm, ln2b_ref),
                (router_hbm, router_ref),
                (bin_hbm, bin_ref),
                (bout_hbm, bout_ref),
            )
        )
    ]
    for copy in small_in + tokens_in[::-1]:
        copy.start()
    weights = [
        pltpu.make_async_copy(a, b, wsem.at[i])
        for i, (a, b) in enumerate(
            ((wqkv_hbm, wqkv), (wo_hbm, wo), (wout_hbm, wout), (win_hbm, win))
        )
    ]
    for copy in weights:
        copy.start()

    per = z.per
    own = me // per
    own_bits = [lax.rem(own, 2), own // 2]

    def group_at(k):
        turned = [b + t * (1 - 2 * b) for b, t in zip(own_bits, (k % 2, k // 2))]
        return turned[0] + 2 * turned[1]

    def members(ref, i, g):
        return ref.at[i, pl.ds(g * per, per)]

    def rows_of(g, first=0, count=None):
        return pl.ds(pl.multiple_of(g * z.rows + first, 16), z.rows if count is None else count)

    def a2a_send(i, k):
        g = group_at(k)
        if k == 0:
            pltpu.make_async_copy(s_msg.at[i, me], r_msg.at[i, me], rs.at[i, own]).start()

        def go(m, carry):
            p = g * per + lax.rem(me + m, per)
            remote(s_msg.at[i, p], r_msg.at[i, me], ss.at[i], rs.at[i, own], (p, core)).start()
            return carry

        lax.fori_loop(1 if k == 0 else 0, per, go, 0)

    def a2a_forward(i, k):
        g = group_at(k)
        block = members(r_msg, i, g)
        remote(block, block, ss.at[i], rs.at[i, g], sib).wait_recv()
        remote(block, members(f_msg, i, g), fs.at[i], fr.at[i, g], sib).start()

    def a2a_take(i, k):
        block = members(f_msg, i, group_at(k))
        remote(block, block, fs.at[i], fr.at[i, group_at(k)], sib).wait_recv()

    def a2a_sent(i):
        block = s_msg.at[i, pl.ds(0, n - 1)]
        remote(block, block, ss.at[i], rs.at[i, 0], sib).wait_send()
        remote(r_msg.at[i], f_msg.at[i], fs.at[i], fr.at[i, 0], sib).wait_send()

    def tail_of(i, src, g):
        rows = src[i, pl.ds(g * per, per), z.msg - 16 : z.msg, :]
        return rows.reshape(per * 16, LANE)

    def assemble(i, g, out):
        q, r = iota((z.gt, per * 16), 0), iota((z.gt, per * 16), 1)
        base = q // z.tail * 16 + q % z.tail
        for src, at in ((r_msg, mine), (f_msg, other)):
            tail = tail_of(i, src, g)
            for b in range(z.blocks):
                lanes = pl.ds(pl.multiple_of(at + b * LANE, LANE), LANE)
                if z.main:
                    rows = src[i, pl.ds(g * per, per), b * z.main : (b + 1) * z.main, :]
                    out[rows_of(g, 0, z.gm), lanes] = rows.reshape(z.gm, LANE)
                pick = one(r == base + b * z.tail)
                out[rows_of(g, z.gm, z.gt), lanes] = dot(pick, tail).astype(BF16)

    def pack(i, g, value, tail):
        q, r = iota((per * 16, z.gt), 1), iota((per * 16, z.gt), 0)
        base = q // z.tail * 16 + q % z.tail
        for b in range(z.blocks):
            lanes = slice(b * LANE, (b + 1) * LANE)
            if z.main:
                s_msg[i, pl.ds(g * per, per), b * z.main : (b + 1) * z.main, :] = value[
                    0 : z.gm, lanes
                ].reshape(per, z.main, LANE)
            piece = dot(one(r == base + b * z.tail), value[z.gm : z.rows, lanes])
            tail = piece if tail is None else tail + piece
        s_msg[i, pl.ds(g * per, per), z.msg - 16 : z.msg, :] = tail.astype(BF16).reshape(
            per, 16, LANE
        )

    gate_row = 14

    for copy in small_in:
        copy.wait()
    rows8[...] = jnp.full(rows8.shape, -1.0, F32)
    rows8[0:2, 0:tok] = routes_ref[...].astype(F32)
    rows8[2:4, 0:tok] = slots_ref[...].astype(F32)
    rows8[4:5, 0:tok] = valid_ref[...].astype(F32)
    table = rows8[...]
    r_row = [table[k : k + 1, :].astype(jnp.int32) for k in range(2)]
    j_row = [table[2 + k : 3 + k, :].astype(jnp.int32) for k in range(2)]
    keep_row = table[4:5, :] > 0.5

    def targets(r, j):
        sent = (r >= 0) & (j < z.cap)
        g = r // per
        m = r - g * per
        flat = jnp.where(j < z.main, m * z.main + j, z.gm + m * z.tail + (j - z.main))
        return sent, jnp.where(sent, g * z.rows + flat, -1)

    sent_row, flat_row = zip(*[targets(r, j) for r, j in zip(r_row, j_row)])
    cols8[...] = jnp.transpose(table)
    r_col = [cols8[0:tp, k : k + 1].astype(jnp.int32) for k in range(2)]
    j_col = [cols8[0:tp, 2 + k : 3 + k].astype(jnp.int32) for k in range(2)]
    keep_col = jnp.where(cols8[0:tp, 4:5] > 0.5, 1.0, 0.0)
    sent_col, flat_col = zip(*[targets(r, j) for r, j in zip(r_col, j_col)])

    slot_id = iota((z.slots, tk), 0)
    onehot[...] = one((slot_id == flat_row[0]) | (slot_id == flat_row[1]))
    tail_id = iota((per * 16, tk), 0)
    tail_row = [
        jnp.where(s & (j >= z.main), r * 16 + (j - z.main), -1000)
        for s, r, j in zip(sent_row, r_row, j_row)
    ]

    def place(src, i, g, tail):
        first = g * (per * 16)
        for b in range(z.blocks):
            lanes = pl.ds(pl.multiple_of(mine + b * LANE, LANE), LANE)
            rows = src[:, lanes]
            if z.main:
                main = dot(onehot[rows_of(g, 0, z.gm), :], rows).astype(BF16)
                s_msg[i, pl.ds(g * per, per), b * z.main : (b + 1) * z.main, :] = main.reshape(
                    per, z.main, LANE
                )
            at = b * z.tail - first
            put = one((tail_id == tail_row[0] + at) | (tail_id == tail_row[1] + at))
            piece = dot(put, rows)
            tail = piece if tail is None else tail + piece
        s_msg[i, pl.ds(g * per, per), z.msg - 16 : z.msg, :] = tail.astype(BF16).reshape(
            per, 16, LANE
        )

    upk[tok // 16 * 16 :, :] = jnp.zeros((tk - tok // 16 * 16, width), BF16)
    tokens_in[1].wait()
    upk[0:tok, :] = grad_out_ref[...]
    for g in range(GROUPS):
        place(upk, 0, g, None)

    xf[tok // 8 * 8 :, :] = jnp.zeros((tp - tok // 8 * 8, width), F32)
    tokens_in[0].wait()
    xf[0:tok, :] = tokens_ref[...].astype(F32)
    normal, inverse1 = norm_parts(xf[...])
    normal1[...] = normal
    n1[tp:, :] = jnp.zeros((tk - tp, width), BF16)
    n1[0:tp, :] = (normal * row_of(ln1g_ref) + row_of(ln1b_ref)).astype(BF16)

    pl.semaphore_wait(barrier, n)
    for k in SEND_ORDER:
        a2a_send(0, k)

    weights[0].wait()
    for c, (dst, bias) in enumerate(((q_s, bqv_ref[0:1, :]), (k_s, None), (v_s, bqv_ref[1:2, :]))):
        value = dot(n1[0:tp, :], wqkv[c])
        if bias is not None:
            value = value + bias
        dst[tp:, :] = jnp.zeros((tk - tp, hw), BF16)
        dst[0:tp, :] = value.astype(BF16)

    score_scale = 1.0 / math.sqrt(HEAD)
    low_lane = iota((1, LANE), 1) < HEAD
    head_mask = [one(low_lane), one(jnp.logical_not(low_lane))]
    for p in range(z.pairs):
        lanes = slice(p * LANE, (p + 1) * LANE)
        qp, kp, vp = q_s[0:tp, lanes], k_s[:, lanes], v_s[:, lanes]
        outs = []
        for h in range(2):
            scores = dot_bt(qp * head_mask[h], kp) * score_scale
            scores = jnp.where(keep_row, scores, -1000000000.0)
            weights_h = jnp.exp(scores - jnp.max(scores, axis=-1, keepdims=True))
            prob = weights_h / jnp.sum(weights_h, axis=-1, keepdims=True)
            probs[2 * p + h] = prob
            outs.append(dot(prob.astype(BF16), vp))
        mix[0:tp, lanes] = jnp.where(low_lane, outs[0], outs[1]).astype(BF16)
    mix[tp:, :] = jnp.zeros((tk - tp, hw), BF16)
    weights[1].wait()
    part[...] = dot(mix[0:tp, :], wo[...])
    swap = remote(part, part_in, hs.at[2, 0], hr.at[2, 0], sib)
    swap.start()
    n1t[...] = jnp.transpose(n1[...])
    swap.wait()

    attention = part[...] + part_in[...] + row_of(bo_ref)
    stat_attn = jnp.sum(keep_col * attention * attention)
    middle = xf[...] + attention
    mid[...] = middle
    normal, inverse2 = norm_parts(middle)
    normal2[...] = normal
    n2[tp:, :] = jnp.zeros((tk - tp, width), BF16)
    n2[0:tp, :] = (normal * row_of(ln2g_ref) + row_of(ln2b_ref)).astype(BF16)
    logits = dot_bt(router_ref[...], n2[...])
    expert_id = iota((z.experts, tk), 0)
    chosen = [
        jnp.sum(jnp.where(expert_id == r, logits, 0.0), axis=0, keepdims=True) for r in r_row
    ]
    top = jnp.maximum(chosen[0], chosen[1])
    raw = [jnp.exp(c - top) for c in chosen]
    total = raw[0] + raw[1]
    gate_rows = [r / total for r in raw]
    cols8[0:tk, :] = jnp.transpose(
        jnp.concatenate(gate_rows + [jnp.zeros((6, tk), F32)], axis=0)
    )
    gate = [cols8[0:tp, k : k + 1] for k in range(2)]

    slot_lane = iota((tk, LANE), 1)
    pad_col = [
        jnp.concatenate([j, jnp.full((tk - tp, 1), -1, jnp.int32)], axis=0) for j in j_col
    ]
    at_slot = [one(slot_lane == j) for j in pad_col]
    halves = [split(g) for g in gate_rows]
    for k in SEND_ORDER:
        g = group_at(k)
        number = None
        for c in range(2):
            high, low = halves[c]
            at = r_row[c] * 16 + (gate_row - g * (per * 16))
            lift = jnp.where(
                sent_row[c] & (tail_id == at), high.astype(F32), 0.0
            ) + jnp.where(sent_row[c] & (tail_id == at + 1), low.astype(F32), 0.0)
            piece = dot(lift.astype(BF16), at_slot[c])
            number = piece if number is None else number + piece
        place(n2, 1, g, number)
        if k < GROUPS - 1:
            a2a_send(1, k)

    for k in range(GROUPS):
        a2a_forward(0, k)
    for k in range(GROUPS):
        a2a_take(0, k)
        assemble(0, group_at(k), u_s)
    weights[2].wait()
    gh[...] = dot_bt(u_s[...], wout[...])

    a2a_send(1, GROUPS - 1)
    weights[3].wait()
    win_t[...] = jnp.transpose(win[...])

    parts = [(0, z.gm, z.main, 0)] if z.main else []
    parts += [(z.gm, z.gt, z.tail, z.main)]
    step = 16

    def activate(g):
        def go(i, carry):
            here = pl.ds(pl.multiple_of(i * step, step), step)
            rows = pl.ds(pl.multiple_of(g * z.rows + i * step, step), step)
            gate_of = jnp.broadcast_to(gcol_s[rows, :], (step, LANE))
            total = jnp.zeros((step, LANE), F32)
            for b in range(z.ff // LANE):
                lanes = slice(b * LANE, (b + 1) * LANE)
                v = pre[here, lanes] + bin_ref[:, lanes]
                v2 = v * v
                s = 0.5 + 0.5 * jnp.tanh(v * (ROOT + (ROOT * CUBE) * v2))
                act = v * s
                back = s + act * (1.0 - s) * (2.0 * ROOT + (6.0 * ROOT * CUBE) * v2)
                up = gh[rows, lanes]
                hid[rows, lanes] = act.astype(BF16)
                gp[rows, lanes] = (gate_of * up * back).astype(BF16)
                total = total + up * act
            ggv[rows, :] = total
            return carry

        count = z.rows // step
        lax.fori_loop(0, count, go, 0, unroll=3 if count % 3 == 0 else 2)

    bias_half = bout_ref[:, pl.ds(mine, half)]

    def swap_of(j, k):
        return remote(half_out.at[j, k], half_in.at[j, k], hs.at[j, k], hr.at[j, k], sib)

    def slots_in(k):
        g = group_at(k)
        a2a_take(1, k)
        assemble(1, g, x_s)
        tail = tail_of(1, r_msg, g)
        for at, rows, each, first in parts:
            q, r = iota((rows, per * 16), 0), iota((rows, per * 16), 1)
            number = r - q // each * 16
            pick = one((number == gate_row) | (number == gate_row + 1))
            lane = iota((rows, LANE), 1) == iota((rows, LANE), 0) % each + first
            gcol_s[rows_of(g, at, rows), :] = jnp.sum(
                jnp.where(lane, dot(pick, tail), 0.0), axis=-1, keepdims=True
            )
        pre[...] = dot(x_s[rows_of(g), :], win[...])
        activate(g)
        back = gp[rows_of(g), :]
        whole[...] = dot(back, win_t[...])
        half_out[0, k] = whole[:, pl.ds(other, half)].astype(BF16)
        swap_of(0, k).start()
        half_own[k] = whole[:, pl.ds(mine, half)]

    def slots_back(k):
        g = group_at(k)
        gg = jnp.sum(ggv[rows_of(g), :], axis=-1, keepdims=True) + jnp.sum(
            u_s[rows_of(g), pl.ds(mine, half)].astype(F32) * bias_half, axis=-1, keepdims=True
        )
        number = None
        for at, rows, each, first in parts:
            q, r = iota((per * 16, rows), 1), iota((per * 16, rows), 0)
            lane = iota((rows, LANE), 1) == iota((rows, LANE), 0) % each + first
            high, low = split(jnp.where(lane, gg[at : at + rows, :], 0.0))
            line = r - q // each * 16
            piece = dot(one(line == gate_row), high) + dot(one(line == gate_row + 1), low)
            number = piece if number is None else number + piece
        swap_of(0, k).wait()
        pack(2, g, (half_own[k] + half_in[0, k].astype(F32)).astype(BF16), number)
        a2a_send(2, k)

    a2a_forward(1, 0)
    a2a_forward(1, 1)
    slots_in(0)
    slots_in(1)
    slots_back(0)
    a2a_forward(1, 2)
    slots_back(1)
    slots_in(2)
    a2a_forward(1, 3)
    slots_back(2)
    slots_in(3)
    slots_back(3)

    for k in range(GROUPS):
        act = hid[rows_of(group_at(k)), :]
        whole[...] = dot(act, wout[...])
        half_out[1, k] = whole[:, pl.ds(other, half)].astype(BF16)
        swap_of(1, k).start()
        half_own[k] = whole[:, pl.ds(mine, half)] + bias_half
    for k in range(GROUPS):
        swap_of(1, k).wait()
        pack(3, group_at(k), (half_own[k] + half_in[1, k].astype(F32)).astype(BF16), None)

    sg[...] = (gcol_s[...] * u_s[...].astype(F32)).astype(BF16)
    x_t[...] = jnp.transpose(x_s[...])
    hid_t[...] = jnp.transpose(hid[...])
    o_beo[...] = jnp.sum(sg[...].astype(F32), axis=0, keepdims=True)
    o_bei[...] = jnp.sum(gp[...].astype(F32), axis=0, keepdims=True)
    stores = [
        pltpu.make_async_copy(a, b, osem.at[i])
        for i, (a, b) in enumerate(((x_t, o_x), (sg, o_sg), (hid_t, o_hid), (gp, o_gp)))
    ]
    for copy in stores:
        copy.start()
    mix_t = jnp.transpose(mix[...])

    flat_id = iota((tp, z.slots), 1)
    back_one = [one(flat_id == f) for f in flat_col]
    for k in range(GROUPS):
        a2a_forward(2, k)
    for k in SEND_ORDER:
        a2a_send(3, k)
    tail_lane = iota((tp, per * 16), 1)
    number = [None, None]
    for k in range(GROUPS):
        g = group_at(k)
        a2a_take(2, k)
        assemble(2, g, y_s)
        tails = [tail_of(2, r_msg, g), tail_of(2, f_msg, g)]
        for c in range(2):
            at = r_col[c] * 16 + (gate_row - g * (per * 16))
            pick = one(sent_col[c] & ((tail_lane == at) | (tail_lane == at + 1)))
            piece = dot(pick, tails[0]) + dot(pick, tails[1])
            number[c] = piece if number[c] is None else number[c] + piece
    grad_gate = [
        jnp.sum(
            jnp.where(iota((tp, LANE), 1) == j_col[c], number[c], 0.0), axis=-1, keepdims=True
        )
        for c in range(2)
    ]
    mean_gate = gate[0] * grad_gate[0] + gate[1] * grad_gate[1]
    e_pad = up_to(z.experts, LANE)
    e_lane = iota((tp, e_pad), 1)
    grad_logits = jnp.where(
        e_lane == r_col[0], gate[0] * (grad_gate[0] - mean_gate), 0.0
    ) + jnp.where(e_lane == r_col[1], gate[1] * (grad_gate[1] - mean_gate), 0.0)
    gl_high, gl_low = split(grad_logits)
    router_pad = router_ref[...]
    if e_pad > z.experts:
        router_pad = jnp.concatenate(
            [router_pad, jnp.zeros((e_pad - z.experts, width), BF16)], axis=0
        )
    grad_n2 = (
        dot(back_one[0] + back_one[1], y_s[...])
        + dot(gl_high, router_pad)
        + dot(gl_low, router_pad)
    )
    grad_router = dot_at(gl_high, n2[0:tp, :]) + dot_at(gl_low, n2[0:tp, :])
    smallf[...] = jnp.zeros(smallf.shape, F32)
    ne = z.experts
    smallf[0:ne, :] = grad_router[0:ne, :]
    normal = normal2[...]
    smallf[ne + 2 : ne + 3, :] = jnp.sum(grad_n2 * normal, axis=0, keepdims=True)
    smallf[ne + 3 : ne + 4, :] = jnp.sum(grad_n2, axis=0, keepdims=True)
    gm[...] = upk[0:tp, :].astype(F32) + norm_backward(grad_n2, normal, inverse2, row_of(ln2g_ref))
    ag[tp:, :] = jnp.zeros((tk - tp, width), BF16)
    ag[0:tp, :] = gm[...].astype(BF16)
    smallf[ne + 4 : ne + 5, :] = jnp.sum(ag[...].astype(F32), axis=0, keepdims=True)

    groups = []
    for order in chain_orders(z.bits, z.chains) + [z.bits]:
        start, size, steps = 0, n, []
        for b in order:
            bit = lax.rem(me // b, 2)
            peer = me + b * (1 - 2 * bit)
            size = size // 2
            steps.append((peer, start + (1 - bit) * size, start + bit * size, size))
            start = start + bit * size
        groups.append((steps, start))
    n_main = len(groups) - 1

    def chain_of(g):
        if g < n_main:
            return chain_g.at[g], [r.at[g] for r in chain_r], chain_a.at[g], z.chunk
        return chain_small, list(small_r), small_a, z.small

    def region(ref, at, count, rows):
        return ref.at[pl.ds(pl.multiple_of(at * rows, 16), count * rows)]

    def rs_copy(g, s):
        src, bufs, _, rows = chain_of(g)
        peer, give, _, size = groups[g][0][s]
        return remote(
            region(src, give, size, rows), bufs[s], cs.at[g], cr.at[g, s], (peer, core)
        )

    def rs_add(g, s, at, count, dst):
        src, bufs, _, rows = chain_of(g)
        keep = groups[g][0][s][2]

        def go(i, carry):
            here = pl.ds(pl.multiple_of((at + i) * rows, 16), rows)
            there = pl.ds(pl.multiple_of((at + i - keep) * rows, 16), rows)
            dst[here, :] = (src[here, :].astype(F32) + bufs[s][there, :].astype(F32)).astype(BF16)
            return carry

        lax.fori_loop(0, count, go, 0, unroll=2 if count % 2 == 0 else 1)

    def rs_step(g, s):
        src, _, out, _ = chain_of(g)
        rs_copy(g, s).wait()
        if s + 1 < nbits:
            _, give, keep, size = groups[g][0][s + 1]
            rs_add(g, s, give, size, src)
            rs_copy(g, s + 1).start()
            rs_add(g, s, keep, size, src)
        else:
            rs_add(g, s, groups[g][1], 1, out)
            ag_copy(g, s).start()

    def ag_copy(g, s):
        _, _, out, rows = chain_of(g)
        peer, _, keep, size = groups[g][0][s]
        piece = region(out, keep, size, rows)
        return remote(piece, piece, as_.at[g], ar.at[g, s], (peer, core))

    def ag_step(g, s):
        _, _, out, rows = chain_of(g)
        peer, give, _, size = groups[g][0][s]
        ag_copy(g, s).wait_send()
        piece = region(out, give, size, rows)
        remote(piece, piece, as_.at[g], ar.at[g, s], (peer, core)).wait_recv()
        if s > 0:
            ag_copy(g, s - 1).start()

    waiting = list(chain_steps(z.bits, z.chains))

    def advance(place):
        while waiting and waiting[0][0] <= place:
            _, g, s = waiting.pop(0)
            if s >= 0:
                rs_step(g, s)
            else:
                ag_step(g, -1 - s)

    filled = 0

    def fill(value):
        nonlocal filled
        rows = value.shape[0]
        for b in range(value.shape[1] // LANE):
            g, at = divmod(filled, z.chain_rows)
            chain_g[g, at : at + rows, :] = value[:, b * LANE : (b + 1) * LANE].astype(BF16)
            filled += rows
            if filled == (g + 1) * z.chain_rows:
                rs_copy(g, 0).start()

    if z.chain_rows < n * z.chunk:
        for g in range(n_main):
            chain_g[g, z.chain_rows :, :] = jnp.zeros((n * z.chunk - z.chain_rows, LANE), BF16)
    fill(dot(mix_t, ag[...]))
    advance(0)

    dm[...] = dot_bt(ag[0:tp, :], wo[...]).astype(BF16)
    for p in range(z.pairs):
        lanes = slice(p * LANE, (p + 1) * LANE)
        qp, kp, vp, dp = q_s[0:tp, lanes], k_s[:, lanes], v_s[:, lanes], dm[:, lanes]
        dq, dk, dv = [], [], []
        for h in range(2):
            prob = probs[2 * p + h]
            gprob = dot_bt(dp * head_mask[h], vp)
            inner = jnp.sum(prob * gprob, axis=-1, keepdims=True)
            gs = (prob * (gprob - inner)).astype(BF16)
            dq.append(dot(gs, kp))
            dk.append(dot_at(gs, qp))
            dv.append(dot_at(prob.astype(BF16), dp))
        for c, (pair, scale) in enumerate(((dq, score_scale), (dk, score_scale), (dv, 1.0))):
            value = (jnp.where(low_lane, pair[0], pair[1]) * scale).astype(BF16)
            at = slice(c * hw + p * LANE, c * hw + (p + 1) * LANE)
            if c == 0:
                gpr[0:tp, at] = value
                gpr[tp:, at] = jnp.zeros((tk - tp, LANE), BF16)
            else:
                gpr[:, at] = value
        joined = jnp.concatenate(
            [gpr[:, c * hw + p * LANE : c * hw + (p + 1) * LANE] for c in range(3)], axis=1
        )
        fill(dot(n1t[...], joined))
        advance(1 + p)

    head_part = None
    for c in range(3):
        piece = dot_bt(gpr[0:tp, c * hw : (c + 1) * hw], wqkv[c])
        head_part = piece if head_part is None else head_part + piece
    gn_out[...] = head_part.astype(BF16)
    swap = remote(gn_out, gn_in, hs.at[2, 1], hr.at[2, 1], sib)
    swap.start()
    smallf[ne + 5 : ne + 6, 0:hw] = jnp.sum(gpr[:, 0:hw].astype(F32), axis=0, keepdims=True)
    smallf[ne + 6 : ne + 7, 0:hw] = jnp.sum(
        gpr[:, 2 * hw : 3 * hw].astype(F32), axis=0, keepdims=True
    )
    swap.wait()
    grad_n1 = gn_out[...].astype(F32) + gn_in[...].astype(F32)
    normal = normal1[...]
    smallf[ne : ne + 1, :] = jnp.sum(grad_n1 * normal, axis=0, keepdims=True)
    smallf[ne + 1 : ne + 2, :] = jnp.sum(grad_n1, axis=0, keepdims=True)
    back = gm[...] + norm_backward(grad_n1, normal, inverse1, row_of(ln1g_ref))
    gtok_out[...] = back[0:tok, :]
    copy = pltpu.make_async_copy(gtok_out, o_gtok, osem.at[4])
    copy.start()
    stores.append(copy)
    used = z.small_rows * (width // LANE)
    for b in range(width // LANE):
        chain_small[b * z.small_rows : (b + 1) * z.small_rows, :] = smallf[
            :, b * LANE : (b + 1) * LANE
        ].astype(BF16)
    if used < n * z.small:
        chain_small[used:, :] = jnp.zeros((n * z.small - used, LANE), BF16)
    rs_copy(n_main, 0).start()
    advance(1 + z.pairs)

    for k in range(GROUPS):
        a2a_forward(3, k)
    for k in range(GROUPS):
        a2a_take(3, k)
        assemble(3, group_at(k), y_s)
    branch = gate[0] * dot(back_one[0], y_s[...]) + gate[1] * dot(back_one[1], y_s[...])
    output = mid[...] + branch
    tok_out[...] = output[0:tok, :].astype(BF16)
    copy = pltpu.make_async_copy(tok_out, o_tok, osem.at[5])
    copy.start()
    stores.append(copy)
    lane_id = iota((1, LANE), 1)
    x_all = xf[...]
    line = jnp.zeros((1, LANE), F32)
    for i, number in enumerate(
        (
            jnp.sum(keep_col * x_all * x_all),
            stat_attn,
            jnp.sum(keep_col * branch * branch),
            jnp.sum(keep_col * output * output),
            jnp.sum(keep_col),
        )
    ):
        line = jnp.where(lane_id == i, number, line)
    stat[me] = jnp.broadcast_to(line, (8, LANE))

    def stat_go(j, carry):
        p = lax.rem(me + j, n)
        remote(stat.at[me], stat.at[me], st.at[0], st.at[1], (p, core)).start()
        return carry

    lax.fori_loop(1, n, stat_go, 0)

    advance(LAST)
    block = stat.at[pl.ds(0, n - 1)]
    remote(block, block, st.at[0], st.at[1], sib).wait()
    totals = jnp.sum(stat[...], axis=0)
    count = jnp.sum(jnp.where(iota((8, LANE), 1) == 4, totals, 0.0), axis=-1, keepdims=True)
    o_rms[...] = jnp.sqrt(totals / (count * width))

    for g in range(n_main):
        copy = pltpu.make_async_copy(chain_a.at[g], o_red.at[g], osem.at[6 + g])
        copy.start()
        stores.append(copy)
    for b in range(width // LANE):
        o_small[:, b * LANE : (b + 1) * LANE] = small_a[
            b * z.small_rows : (b + 1) * z.small_rows, :
        ].astype(F32)
    for i in range(4):
        a2a_sent(i)
    for copy in stores:
        copy.wait()


def last_kernel(
    z,
    i_tok,
    i_gtok,
    x_t,
    sg,
    hid_t,
    gp,
    red,
    i_small,
    i_bei,
    i_beo,
    i_rms,
    o_tok,
    o_gtok,
    o_ln1g,
    o_ln1b,
    o_wqkv,
    o_bqv,
    o_wo,
    o_bo,
    o_ln2g,
    o_ln2b,
    o_router,
    o_win,
    o_bin,
    o_wout,
    o_bout,
    o_rms,
    wqkv,
    wo,
    win,
    wout,
    osem,
):
    ne, width, hw = z.experts, z.width, z.hw
    stores = []

    def store(src, dst, i):
        copy = pltpu.make_async_copy(src, dst, osem.at[i])
        copy.start()
        stores.append(copy)

    store(i_tok, o_tok, 0)
    store(i_gtok, o_gtok, 1)
    for ref, i in ((o_ln1g, 0), (o_ln1b, 1), (o_ln2g, 2), (o_ln2b, 3), (o_bo, 4)):
        ref[...] = i_small[ne + i : ne + i + 1, :].reshape(width)
    o_router[...] = i_small[0:ne, :]
    o_bqv[...] = i_small[ne + 5 : ne + 7, 0:hw]
    o_bin[...] = i_bei[...]
    o_bout[...] = i_beo[...]
    o_rms[...] = i_rms[0:1, 0:4].reshape(4)

    at = 0

    def take(rows):
        nonlocal at
        g, row = divmod(at, z.chain_rows)
        at += rows
        return red[g, row : row + rows, :].astype(F32)

    for b in range(width // LANE):
        wo[:, b * LANE : (b + 1) * LANE] = take(hw)
    store(wo, o_wo, 2)
    for p in range(z.pairs):
        for c in range(3):
            wqkv[c, :, p * LANE : (p + 1) * LANE] = take(width)
    store(wqkv, o_wqkv, 3)
    tiles = z.ff // TILE
    for t in range(tiles):
        cols = slice(t * TILE, (t + 1) * TILE)
        win[:, cols] = dot(x_t[...], gp[:, cols])
        store(win.at[:, cols], o_win.at[0, :, cols], 4 + t)
    for t in range(tiles):
        rows = slice(t * TILE, (t + 1) * TILE)
        wout[rows, :] = dot(hid_t[rows, :], sg[...])
        store(wout.at[rows, :], o_wout.at[0, rows, :], 4 + tiles + t)
    for copy in stores:
        copy.wait()


def per_device(
    tokens,
    grad_out,
    valid_mask,
    routes,
    slot_index,
    ln1_gain,
    ln1_bias,
    w_qkv,
    bias_qv,
    w_attn_out,
    b_attn_out,
    ln2_gain,
    ln2_bias,
    router,
    w_expert_in,
    b_expert_in,
    w_expert_out,
    b_expert_out,
):
    tok, width = tokens.shape
    hw = w_qkv.shape[2]
    ff = w_expert_in.shape[2]
    z = Sizes(lax.axis_size("dp"), tok, width, hw, ff, router.shape[1])
    n, tp, tk = z.n, z.tp, z.tk
    nbits = len(z.bits)
    vmem = pl.BlockSpec(memory_space=pltpu.VMEM)
    any_ = pl.BlockSpec(memory_space=pl.ANY)
    shape = jax.ShapeDtypeStruct
    groups = z.chains
    kept = pltpu.VMEM if n <= 16 else shape
    keep = lambda a: pltpu.with_memory_space_constraint(a, pltpu.VMEM) if n <= 16 else a
    V = pltpu.VMEM
    scratch = [
        V((tok, width), BF16),
        V((tok, width), BF16),
        V((1, tok), jnp.int32),
        V((2, tok), jnp.int32),
        V((2, tok), jnp.int32),
        V((width,), F32),
        V((width,), F32),
        V((2, hw), F32),
        V((width,), F32),
        V((width,), F32),
        V((width,), F32),
        V((z.experts, width), BF16),
        V((1, ff), F32),
        V((1, width), F32),
        V((tok, width), BF16),
        V((tok, width), F32),
        V((3, width, hw), BF16),
        V((hw, width), BF16),
        V((width, ff), BF16),
        V((ff, width), BF16),
        V((tp, width), F32),
        V((tp, width), F32),
        V((tk, width), BF16),
        V((width, tk), BF16),
        V((tk, width), BF16),
        V((tk, hw), BF16),
        V((tk, hw), BF16),
        V((tk, hw), BF16),
        V((2 * z.pairs, tp, tk), F32),
        V((tk, hw), BF16),
        V((tp, width), F32),
        V((tp, width), F32),
        V((tp, width), F32),
        V((tp, width), F32),
        V((tk, width), BF16),
        V((z.slots, tk), BF16),
        V((8, tk), F32),
        V((tk, 8), F32),
        V((z.slots, width), BF16),
        V((z.slots, width), BF16),
        V((z.slots, width), BF16),
        V((z.slots, ff), F32),
        V((z.rows, ff), F32),
        V((z.slots, ff), BF16),
        V((z.slots, ff), BF16),
        V((z.slots, width), BF16),
        V((width, z.slots), BF16),
        V((ff, z.slots), BF16),
        V((z.slots, 1), F32),
        V((z.slots, LANE), F32),
        V((2, GROUPS, z.rows, z.half), BF16),
        V((2, GROUPS, z.rows, z.half), BF16),
        V((GROUPS, z.rows, z.half), F32),
        V((z.rows, width), F32),
        V((ff, width), BF16),
        V((tp, width), F32),
        V((tk, width), BF16),
        V((tp, hw), BF16),
        V((tk, 3 * hw), BF16),
        V((tp, width), BF16),
        V((tp, width), BF16),
        V((z.small_rows, width), F32),
        V((n, 8, LANE), F32),
        V((4, n, z.msg, LANE), BF16),
        V((4, n, z.msg, LANE), BF16),
        V((4, n, z.msg, LANE), BF16),
        V((groups, n * z.chunk, LANE), BF16),
        V((n * z.small, LANE), BF16),
    ]
    scratch += [V((groups, (n >> (s + 1)) * z.chunk, LANE), BF16) for s in range(nbits)]
    scratch += [V(((n >> (s + 1)) * z.small, LANE), BF16) for s in range(nbits)]
    scratch += [
        V((groups, n * z.chunk, LANE), BF16),
        V((n * z.small, LANE), BF16),
        DMA((18,)),
        DMA((6 + groups,)),
        DMA((3, GROUPS)),
        DMA((3, GROUPS)),
        DMA((4,)),
        DMA((4, GROUPS)),
        DMA((4,)),
        DMA((4, GROUPS)),
        DMA((groups + 1,)),
        DMA((groups + 1, nbits)),
        DMA((groups + 1,)),
        DMA((groups + 1, nbits)),
        DMA((2,)),
    ]
    row = lambda v: v.reshape(1, -1)
    outs = pl.pallas_call(
        functools.partial(mega_kernel, z),
        out_shape=(
            kept((tok, width), BF16),
            kept((tok, width), F32),
            kept((width, z.slots), BF16),
            kept((z.slots, width), BF16),
            kept((ff, z.slots), BF16),
            kept((z.slots, ff), BF16),
            kept((groups, n * z.chunk, LANE), BF16),
            kept((z.small_rows, width), F32),
            kept((1, ff), F32),
            kept((1, width), F32),
            kept((8, LANE), F32),
        ),
        in_specs=[any_] * 18,
        out_specs=(any_,) * 7 + (vmem,) * 4,
        scratch_shapes=scratch,
        compiler_params=pltpu.CompilerParams(
            collective_id=0,
            has_side_effects=True,
            vmem_limit_bytes=(53 if n <= 16 else 61) * 2**20,
        ),
    )(*(
        pltpu.with_memory_space_constraint(a, pltpu.HBM)
        for a in (
        tokens,
        grad_out,
        row(valid_mask),
        routes.T,
        slot_index.T,
        ln1_gain,
        ln1_bias,
        jnp.transpose(w_qkv, (1, 0, 2)),
        bias_qv,
        w_attn_out,
        b_attn_out,
        ln2_gain,
        ln2_bias,
        router.T,
        w_expert_in[0],
        b_expert_in,
        w_expert_out[0],
        b_expert_out,
        )
    ))
    ne = z.experts
    vec = shape((width,), F32)
    last = pl.pallas_call(
        functools.partial(last_kernel, z),
        out_shape=(
            shape((tok, width), BF16),
            shape((tok, width), F32),
            vec,
            vec,
            shape((3, width, hw), F32),
            shape((2, hw), F32),
            shape((hw, width), F32),
            vec,
            vec,
            vec,
            shape((ne, width), F32),
            shape((1, width, ff), F32),
            shape((1, ff), F32),
            shape((1, ff, width), F32),
            shape((1, width), F32),
            shape((4,), F32),
        ),
        in_specs=[any_] * 2 + [vmem] * 9,
        out_specs=(
            [any_] * 2
            + [vmem] * 2
            + [any_, vmem, any_]
            + [vmem] * 4
            + [any_, vmem, any_, vmem, vmem]
        ),
        scratch_shapes=[
            V((3, width, hw), F32),
            V((hw, width), F32),
            V((width, ff), F32),
            V((ff, width), F32),
            DMA((4 + 2 * (ff // TILE),)),
        ],
        compiler_params=pltpu.CompilerParams(vmem_limit_bytes=(30 if n <= 16 else 48) * 2**20),
    )(*(keep(a) for a in outs))
    return (
        last[0],
        last[1],
        last[2],
        last[3],
        jnp.transpose(last[4], (1, 0, 2)),
        *last[5:10],
        last[10].T,
        *last[11:],
    )


def solution(mesh):
    return jax.shard_map(
        per_device,
        mesh=mesh,
        in_specs=(
            P("dp", None),
            P("dp", None),
            P("dp"),
            P("dp", None),
            P("dp", None),
            P(),
            P(),
            P(None, None, "tensor"),
            P(None, "tensor"),
            P("tensor", None),
            P(),
            P(),
            P(),
            P(),
            P("dp", None, "tensor"),
            P("dp", "tensor"),
            P("dp", "tensor", None),
            P("dp", None),
        ),
        out_specs=(
            P("dp", None),
            P("dp", None),
            P(),
            P(),
            P(None, None, "tensor"),
            P(None, "tensor"),
            P("tensor", None),
            P(),
            P(),
            P(),
            P(),
            P("dp", None, "tensor"),
            P("dp", "tensor"),
            P("dp", "tensor", None),
            P("dp", None),
            P(),
        ),
        check_vma=False,
    )
```

```python
import functools
import math

import jax
import jax.numpy as jnp
from jax import lax
from jax.experimental import pallas as pl
from jax.experimental.pallas import tpu as pltpu
from jax.sharding import PartitionSpec as P

HEAD = 64
SEQ = 197
LANE = 128
EPS = 1e-06
ROOT = math.sqrt(2.0 / math.pi)
CUBE = 0.044715
GROUPS = 4
LAST = 5
ORDERS = (
    (0, 1, 3, 2),
    (1, 3, 0, 2),
    (2, 0, 1, 3),
    (0, 2, 1, 3),
    (1, 0, 3, 2),
    (2, 1, 0, 3),
    (3, 0, 1, 2),
    (2, 1, 0, 3),
    (1, 0, 2, 3),
    (1, 3, 0, 2),
    (0, 1, 2, 3),
    (0, 3, 1, 2),
)
STEPS = (
    (5, 0, 0), (5, 1, 0), (5, 2, 0), (5, 4, 0), (5, 12, 0), (5, 3, 0), (5, 8, 0), (5, 5, 0),
    (5, 9, 0), (5, 10, 0), (5, 11, 0), (5, 0, 1), (5, 7, 0), (5, 6, 0), (5, 12, 1), (5, 2, 1),
    (5, 4, 1), (5, 1, 1), (5, 3, 1), (5, 8, 1), (5, 5, 1), (5, 10, 1), (5, 7, 1), (5, 9, 1),
    (5, 12, 2), (5, 6, 1), (5, 2, 2), (5, 1, 2), (5, 0, 2), (5, 3, 2), (5, 5, 2), (5, 4, 2),
    (5, 11, 1), (5, 8, 2), (5, 7, 2), (5, 12, 3), (5, 10, 2), (5, 9, 2), (5, 6, 2), (5, 2, 3),
    (5, 1, 3), (5, 0, 3), (5, 3, 3), (5, 5, 3), (5, 4, 3), (5, 11, 2), (5, 12, -4), (5, 8, 3),
    (5, 7, 3), (5, 9, 3), (5, 10, 3), (5, 6, 3), (5, 2, -4), (5, 1, -4), (5, 0, -4), (5, 3, -4),
    (5, 12, -3), (5, 5, -4), (5, 4, -4), (5, 11, 3), (5, 8, -4), (5, 7, -4), (5, 9, -4),
    (5, 10, -4), (5, 6, -4), (5, 2, -3), (5, 1, -3), (5, 5, -3), (5, 12, -2), (5, 3, -3),
    (5, 11, -4), (5, 0, -3), (5, 7, -3), (5, 4, -3), (5, 6, -3), (5, 9, -3), (5, 8, -3),
    (5, 10, -3), (5, 12, -1), (5, 2, -2), (5, 5, -2), (5, 1, -2), (5, 11, -3), (5, 3, -2),
    (5, 0, -2), (5, 9, -2), (5, 4, -2), (5, 6, -2), (5, 7, -2), (5, 8, -2), (5, 10, -2),
    (5, 11, -2), (5, 3, -1), (5, 1, -1), (5, 0, -1), (5, 2, -1), (5, 5, -1), (5, 10, -1),
    (5, 9, -1), (5, 4, -1), (5, 11, -1), (5, 8, -1), (5, 6, -1), (5, 7, -1),
)
SEND_ORDER = (0, 2, 1, 3)
TILE = 256
MESH = pl.DeviceIdType.MESH
F32 = jnp.float32
BF16 = jnp.bfloat16
DMA = pltpu.SemaphoreType.DMA


def up_to(value, step):
    return -(-value // step) * step


def dot(a, b):
    return lax.dot_general(a, b, (((1,), (0,)), ((), ())), preferred_element_type=F32)


def dot_bt(a, b):
    return lax.dot_general(a, b, (((1,), (1,)), ((), ())), preferred_element_type=F32)


def dot_at(a, b):
    return lax.dot_general(a, b, (((0,), (0,)), ((), ())), preferred_element_type=F32)


def row_of(ref):
    return ref[...].reshape(1, ref.shape[0])


def iota(shape, dim):
    return lax.broadcasted_iota(jnp.int32, shape, dim)


def one(cond, kind=BF16):
    return jnp.where(cond, 1.0, 0.0).astype(kind)


def split(value):
    high = value.astype(BF16)
    return high, (value - high.astype(F32)).astype(BF16)


def norm_parts(values):
    scale = 1.0 / values.shape[-1]
    center = values - jnp.sum(values, axis=-1, keepdims=True) * scale
    inverse = lax.rsqrt(jnp.sum(center * center, axis=-1, keepdims=True) * scale + EPS)
    return center * inverse, inverse


def norm_backward(incoming, normal, inverse, gain_vec):
    scale = 1.0 / incoming.shape[-1]
    scaled = incoming * gain_vec
    return inverse * (
        scaled
        - jnp.sum(scaled, axis=-1, keepdims=True) * scale
        - normal * (jnp.sum(scaled * normal, axis=-1, keepdims=True) * scale)
    )


def remote(src, dst, send_sem, recv_sem, device):
    return pltpu.make_async_remote_copy(
        src_ref=src,
        dst_ref=dst,
        send_sem=send_sem,
        recv_sem=recv_sem,
        device_id=device,
        device_id_type=MESH,
    )


class Sizes:
    def __init__(self, n, tok, width, heads_width, ff, experts):
        self.n = n
        self.tok = tok
        self.tp = up_to(tok, 16)
        self.tk = up_to(tok, LANE)
        self.width = width
        self.hw = heads_width
        self.pairs = heads_width // LANE
        self.ff = ff
        self.experts = experts
        self.cap = 2 * (3 * tok // (2 * n))
        self.main = self.cap // 16 * 16
        self.tail = self.cap - self.main
        self.half = width // 2
        self.blocks = self.half // LANE
        self.msg = self.main * self.blocks + 16
        self.per = n // GROUPS
        self.gm = self.per * self.main
        self.gt = self.per * self.tail
        self.rows = self.per * self.cap
        self.slots = n * self.cap
        self.bits = [1 << i for i in range(n.bit_length() - 1)]
        self.pack_rows = 4 * heads_width * width // LANE
        self.chains = 12 if n <= 16 else 6
        self.chain_rows = self.pack_rows // self.chains
        self.chunk = up_to(up_to(self.chain_rows, n) // n, 16)
        self.small_rows = up_to(experts + 7, 16)
        self.small = up_to(up_to(self.small_rows * width // LANE, n) // n, 16)
        fits = 0 < self.tail * self.blocks <= 14 and self.gt % 16 == 0
        fits = fits and self.chain_rows % heads_width == 0 and self.chain_rows % width == 0
        if not fits or experts != n or (1 << len(self.bits)) != n:
            raise ValueError("unsupported sizes")


def chain_orders(bits, chains):
    if len(bits) == 4 and chains == len(ORDERS):
        return [[bits[i] for i in order] for order in ORDERS]
    if len(bits) < 3:
        return [bits] * chains
    order = ((0, 1, 2), (1, 2, 0), (2, 0, 1), (0, 2, 1), (1, 0, 2), (2, 1, 0))
    return [[bits[i] for i in order[c % 6]] + bits[3:] for c in range(chains)]


def chain_steps(bits, chains):
    if len(bits) == 4 and chains == len(ORDERS):
        return STEPS
    steps = [(LAST, c, s) for s in range(len(bits)) for c in range(chains + 1)]
    return steps + [
        (LAST, c, -1 - s) for s in range(len(bits) - 1, -1, -1) for c in range(chains + 1)
    ]


def mega_kernel(
    z,
    tokens_hbm,
    grad_out_hbm,
    valid_hbm,
    routes_hbm,
    slots_hbm,
    ln1g_hbm,
    ln1b_hbm,
    wqkv_hbm,
    bqv_hbm,
    wo_hbm,
    bo_hbm,
    ln2g_hbm,
    ln2b_hbm,
    router_hbm,
    win_hbm,
    bin_hbm,
    wout_hbm,
    bout_hbm,
    o_tok,
    o_gtok,
    x_t,
    sg,
    hid_t,
    gp,
    chain_a,
    o_small,
    o_bei,
    o_beo,
    o_rms,
    tokens_ref,
    grad_out_ref,
    valid_ref,
    routes_ref,
    slots_ref,
    ln1g_ref,
    ln1b_ref,
    bqv_ref,
    bo_ref,
    ln2g_ref,
    ln2b_ref,
    router_ref,
    bin_ref,
    bout_ref,
    tok_out,
    gtok_out,
    wqkv,
    wo,
    win,
    wout,
    xf,
    normal1,
    n1,
    n1t,
    upk,
    q_s,
    k_s,
    v_s,
    probs,
    mix,
    part,
    part_in,
    mid,
    normal2,
    n2,
    onehot,
    rows8,
    cols8,
    u_s,
    x_s,
    y_s,
    gh,
    pre,
    hid,
    gcol_s,
    ggv,
    half_out,
    half_in,
    half_own,
    whole,
    win_t,
    wout_t,
    gm,
    ag,
    dm,
    gpr,
    gn_out,
    gn_in,
    smallf,
    stat,
    s_msg,
    r_msg,
    f_msg,
    chain_g,
    chain_small,
    *rest,
):
    nbits = len(z.bits)
    chain_r = rest[:nbits]
    small_r = rest[nbits : 2 * nbits]
    small_a, wsem, osem, hs, hr, ss, rs, fs, fr, cs, cr, as_, ar, st = rest[
        2 * nbits :
    ]
    n = z.n
    me, core = lax.axis_index("dp"), lax.axis_index("tensor")
    sib = (me, 1 - core)
    tok, tp, tk, width, hw, half = z.tok, z.tp, z.tk, z.width, z.hw, z.half
    mine = pl.multiple_of(core * half, LANE)
    other = pl.multiple_of((1 - core) * half, LANE)

    barrier = pltpu.get_barrier_semaphore()

    def greet(j, carry):
        pl.semaphore_signal(
            barrier, inc=1, device_id=(lax.rem(me + j, n), core), device_id_type=MESH
        )
        return carry

    lax.fori_loop(1, n, greet, 0)
    pl.semaphore_signal(barrier, inc=1, device_id=sib, device_id_type=MESH)

    tokens_in = [
        pltpu.make_async_copy(a, b, wsem.at[4 + i])
        for i, (a, b) in enumerate(((tokens_hbm, tokens_ref), (grad_out_hbm, grad_out_ref)))
    ]
    small_in = [
        pltpu.make_async_copy(a, b, wsem.at[6 + i])
        for i, (a, b) in enumerate(
            (
                (valid_hbm, valid_ref),
                (routes_hbm, routes_ref),
                (slots_hbm, slots_ref),
                (ln1g_hbm, ln1g_ref),
                (ln1b_hbm, ln1b_ref),
                (bqv_hbm, bqv_ref),
                (bo_hbm, bo_ref),
                (ln2g_hbm, ln2g_ref),
                (ln2b_hbm, ln2b_ref),
                (router_hbm, router_ref),
                (bin_hbm, bin_ref),
                (bout_hbm, bout_ref),
            )
        )
    ]
    for copy in small_in + tokens_in[::-1]:
        copy.start()
    weights = [
        pltpu.make_async_copy(a, b, wsem.at[i])
        for i, (a, b) in enumerate(
            ((wqkv_hbm, wqkv), (wo_hbm, wo), (wout_hbm, wout), (win_hbm, win))
        )
    ]
    for copy in weights:
        copy.start()

    per = z.per
    own = me // per
    own_bits = [lax.rem(own, 2), own // 2]

    def group_at(k):
        turned = [b + t * (1 - 2 * b) for b, t in zip(own_bits, (k % 2, k // 2))]
        return turned[0] + 2 * turned[1]

    def members(ref, i, g):
        return ref.at[i, pl.ds(g * per, per)]

    def rows_of(g, first=0, count=None):
        return pl.ds(pl.multiple_of(g * z.rows + first, 16), z.rows if count is None else count)

    def a2a_send(i, k):
        g = group_at(k)
        if k == 0:
            pltpu.make_async_copy(s_msg.at[i, me], r_msg.at[i, me], rs.at[i, own]).start()

        def go(m, carry):
            p = g * per + lax.rem(me + m, per)
            remote(s_msg.at[i, p], r_msg.at[i, me], ss.at[i], rs.at[i, own], (p, core)).start()
            return carry

        lax.fori_loop(1 if k == 0 else 0, per, go, 0)

    def a2a_forward(i, k):
        g = group_at(k)
        block = members(r_msg, i, g)
        remote(block, block, ss.at[i], rs.at[i, g], sib).wait_recv()
        remote(block, members(f_msg, i, g), fs.at[i], fr.at[i, g], sib).start()

    def a2a_take(i, k):
        block = members(f_msg, i, group_at(k))
        remote(block, block, fs.at[i], fr.at[i, group_at(k)], sib).wait_recv()

    def a2a_sent(i):
        block = s_msg.at[i, pl.ds(0, n - 1)]
        remote(block, block, ss.at[i], rs.at[i, 0], sib).wait_send()
        remote(r_msg.at[i], f_msg.at[i], fs.at[i], fr.at[i, 0], sib).wait_send()

    def tail_of(i, src, g):
        rows = src[i, pl.ds(g * per, per), z.msg - 16 : z.msg, :]
        return rows.reshape(per * 16, LANE)

    def assemble(i, g, out):
        q, r = iota((z.gt, per * 16), 0), iota((z.gt, per * 16), 1)
        base = q // z.tail * 16 + q % z.tail
        for src, at in ((r_msg, mine), (f_msg, other)):
            tail = tail_of(i, src, g)
            for b in range(z.blocks):
                lanes = pl.ds(pl.multiple_of(at + b * LANE, LANE), LANE)
                if z.main:
                    rows = src[i, pl.ds(g * per, per), b * z.main : (b + 1) * z.main, :]
                    out[rows_of(g, 0, z.gm), lanes] = rows.reshape(z.gm, LANE)
                pick = one(r == base + b * z.tail)
                out[rows_of(g, z.gm, z.gt), lanes] = dot(pick, tail).astype(BF16)

    def pack(i, g, value, tail):
        q, r = iota((per * 16, z.gt), 1), iota((per * 16, z.gt), 0)
        base = q // z.tail * 16 + q % z.tail
        for b in range(z.blocks):
            lanes = slice(b * LANE, (b + 1) * LANE)
            if z.main:
                s_msg[i, pl.ds(g * per, per), b * z.main : (b + 1) * z.main, :] = value[
                    0 : z.gm, lanes
                ].reshape(per, z.main, LANE)
            piece = dot(one(r == base + b * z.tail), value[z.gm : z.rows, lanes])
            tail = piece if tail is None else tail + piece
        s_msg[i, pl.ds(g * per, per), z.msg - 16 : z.msg, :] = tail.astype(BF16).reshape(
            per, 16, LANE
        )

    gate_row = 14

    for copy in small_in:
        copy.wait()
    rows8[...] = jnp.full(rows8.shape, -1.0, F32)
    rows8[0:2, 0:tok] = routes_ref[...].astype(F32)
    rows8[2:4, 0:tok] = slots_ref[...].astype(F32)
    rows8[4:5, 0:tok] = valid_ref[...].astype(F32)
    table = rows8[...]
    r_row = [table[k : k + 1, :].astype(jnp.int32) for k in range(2)]
    j_row = [table[2 + k : 3 + k, :].astype(jnp.int32) for k in range(2)]
    keep_row = table[4:5, :] > 0.5

    def targets(r, j):
        sent = (r >= 0) & (j < z.cap)
        g = r // per
        m = r - g * per
        flat = jnp.where(j < z.main, m * z.main + j, z.gm + m * z.tail + (j - z.main))
        return sent, jnp.where(sent, g * z.rows + flat, -1)

    sent_row, flat_row = zip(*[targets(r, j) for r, j in zip(r_row, j_row)])
    cols8[...] = jnp.transpose(table)
    r_col = [cols8[0:tp, k : k + 1].astype(jnp.int32) for k in range(2)]
    j_col = [cols8[0:tp, 2 + k : 3 + k].astype(jnp.int32) for k in range(2)]
    keep_col = jnp.where(cols8[0:tp, 4:5] > 0.5, 1.0, 0.0)
    sent_col, flat_col = zip(*[targets(r, j) for r, j in zip(r_col, j_col)])

    slot_id = iota((z.slots, tk), 0)
    onehot[...] = one((slot_id == flat_row[0]) | (slot_id == flat_row[1]))
    tail_id = iota((per * 16, tk), 0)
    tail_row = [
        jnp.where(s & (j >= z.main), r * 16 + (j - z.main), -1000)
        for s, r, j in zip(sent_row, r_row, j_row)
    ]

    def place(src, i, g, tail):
        first = g * (per * 16)
        for b in range(z.blocks):
            lanes = pl.ds(pl.multiple_of(mine + b * LANE, LANE), LANE)
            rows = src[:, lanes]
            if z.main:
                main = dot(onehot[rows_of(g, 0, z.gm), :], rows).astype(BF16)
                s_msg[i, pl.ds(g * per, per), b * z.main : (b + 1) * z.main, :] = main.reshape(
                    per, z.main, LANE
                )
            at = b * z.tail - first
            put = one((tail_id == tail_row[0] + at) | (tail_id == tail_row[1] + at))
            piece = dot(put, rows)
            tail = piece if tail is None else tail + piece
        s_msg[i, pl.ds(g * per, per), z.msg - 16 : z.msg, :] = tail.astype(BF16).reshape(
            per, 16, LANE
        )

    upk[tok // 16 * 16 :, :] = jnp.zeros((tk - tok // 16 * 16, width), BF16)
    tokens_in[1].wait()
    upk[0:tok, :] = grad_out_ref[...]
    for g in range(GROUPS):
        place(upk, 0, g, None)

    xf[tok // 8 * 8 :, :] = jnp.zeros((tp - tok // 8 * 8, width), F32)
    tokens_in[0].wait()
    xf[0:tok, :] = tokens_ref[...].astype(F32)
    normal, inverse1 = norm_parts(xf[...])
    normal1[...] = normal
    n1[tp:, :] = jnp.zeros((tk - tp, width), BF16)
    n1[0:tp, :] = (normal * row_of(ln1g_ref) + row_of(ln1b_ref)).astype(BF16)

    pl.semaphore_wait(barrier, n)
    for k in SEND_ORDER:
        a2a_send(0, k)

    weights[0].wait()
    for c, (dst, bias) in enumerate(((q_s, bqv_ref[0:1, :]), (k_s, None), (v_s, bqv_ref[1:2, :]))):
        value = dot(n1[0:tp, :], wqkv[c])
        if bias is not None:
            value = value + bias
        dst[tp:, :] = jnp.zeros((tk - tp, hw), BF16)
        dst[0:tp, :] = value.astype(BF16)

    score_scale = 1.0 / math.sqrt(HEAD)
    low_lane = iota((1, LANE), 1) < HEAD
    head_mask = [one(low_lane), one(jnp.logical_not(low_lane))]
    for p in range(z.pairs):
        lanes = slice(p * LANE, (p + 1) * LANE)
        qp, kp, vp = q_s[0:tp, lanes], k_s[:, lanes], v_s[:, lanes]
        outs = []
        for h in range(2):
            scores = dot_bt(qp * head_mask[h], kp) * score_scale
            scores = jnp.where(keep_row, scores, -1000000000.0)
            weights_h = jnp.exp(scores - jnp.max(scores, axis=-1, keepdims=True))
            prob = weights_h / jnp.sum(weights_h, axis=-1, keepdims=True)
            probs[2 * p + h] = prob
            outs.append(dot(prob.astype(BF16), vp))
        mix[0:tp, lanes] = jnp.where(low_lane, outs[0], outs[1]).astype(BF16)
    mix[tp:, :] = jnp.zeros((tk - tp, hw), BF16)
    weights[1].wait()
    part[...] = dot(mix[0:tp, :], wo[...])
    swap = remote(part, part_in, hs.at[2, 0], hr.at[2, 0], sib)
    swap.start()
    n1t[...] = jnp.transpose(n1[...])
    swap.wait()

    attention = part[...] + part_in[...] + row_of(bo_ref)
    stat_attn = jnp.sum(keep_col * attention * attention)
    middle = xf[...] + attention
    mid[...] = middle
    normal, inverse2 = norm_parts(middle)
    normal2[...] = normal
    n2[tp:, :] = jnp.zeros((tk - tp, width), BF16)
    n2[0:tp, :] = (normal * row_of(ln2g_ref) + row_of(ln2b_ref)).astype(BF16)
    logits = dot_bt(router_ref[...], n2[...])
    expert_id = iota((z.experts, tk), 0)
    chosen = [
        jnp.sum(jnp.where(expert_id == r, logits, 0.0), axis=0, keepdims=True) for r in r_row
    ]
    top = jnp.maximum(chosen[0], chosen[1])
    raw = [jnp.exp(c - top) for c in chosen]
    total = raw[0] + raw[1]
    gate_rows = [r / total for r in raw]
    cols8[0:tk, :] = jnp.transpose(
        jnp.concatenate(gate_rows + [jnp.zeros((6, tk), F32)], axis=0)
    )
    gate = [cols8[0:tp, k : k + 1] for k in range(2)]

    slot_lane = iota((tk, LANE), 1)
    pad_col = [
        jnp.concatenate([j, jnp.full((tk - tp, 1), -1, jnp.int32)], axis=0) for j in j_col
    ]
    at_slot = [one(slot_lane == j) for j in pad_col]
    halves = [split(g) for g in gate_rows]
    for k in SEND_ORDER:
        g = group_at(k)
        number = None
        for c in range(2):
            high, low = halves[c]
            at = r_row[c] * 16 + (gate_row - g * (per * 16))
            lift = jnp.where(
                sent_row[c] & (tail_id == at), high.astype(F32), 0.0
            ) + jnp.where(sent_row[c] & (tail_id == at + 1), low.astype(F32), 0.0)
            piece = dot(lift.astype(BF16), at_slot[c])
            number = piece if number is None else number + piece
        place(n2, 1, g, number)
        if k < GROUPS - 1:
            a2a_send(1, k)

    def upstream(k):
        g = group_at(k)
        a2a_take(0, k)
        assemble(0, g, u_s)
        gh[rows_of(g), :] = dot(u_s[rows_of(g), :], wout_t[...])

    weights[2].wait()
    wout_t[...] = jnp.transpose(wout[...])
    a2a_forward(0, 0)
    a2a_forward(0, 1)
    weights[3].wait()
    win_t[...] = jnp.transpose(win[...])
    upstream(0)
    upstream(1)
    a2a_forward(0, 2)
    a2a_forward(0, 3)
    a2a_send(1, 3)
    a2a_forward(1, 0)
    upstream(2)
    upstream(3)

    parts = [(0, z.gm, z.main, 0)] if z.main else []
    parts += [(z.gm, z.gt, z.tail, z.main)]
    step = 16

    def activate(g):
        def go(i, carry):
            here = pl.ds(pl.multiple_of(i * step, step), step)
            rows = pl.ds(pl.multiple_of(g * z.rows + i * step, step), step)
            gate_of = jnp.broadcast_to(gcol_s[rows, :], (step, LANE))
            total = jnp.zeros((step, LANE), F32)
            for b in range(z.ff // LANE):
                lanes = slice(b * LANE, (b + 1) * LANE)
                v = pre[here, lanes] + bin_ref[:, lanes]
                v2 = v * v
                s = 0.5 + 0.5 * jnp.tanh(v * (ROOT + (ROOT * CUBE) * v2))
                act = v * s
                back = s + act * (1.0 - s) * (2.0 * ROOT + (6.0 * ROOT * CUBE) * v2)
                up = gh[rows, lanes]
                hid[rows, lanes] = act.astype(BF16)
                gp[rows, lanes] = (gate_of * up * back).astype(BF16)
                total = total + up * act
            ggv[rows, :] = total
            return carry

        count = z.rows // step
        lax.fori_loop(0, count, go, 0, unroll=3 if count % 3 == 0 else 2)

    bias_half = bout_ref[:, pl.ds(mine, half)]

    def swap_of(j, k):
        return remote(half_out.at[j, k], half_in.at[j, k], hs.at[j, k], hr.at[j, k], sib)

    def slots_in(k):
        g = group_at(k)
        a2a_take(1, k)
        assemble(1, g, x_s)
        tail = tail_of(1, r_msg, g)
        for at, rows, each, first in parts:
            q, r = iota((rows, per * 16), 0), iota((rows, per * 16), 1)
            number = r - q // each * 16
            pick = one((number == gate_row) | (number == gate_row + 1))
            lane = iota((rows, LANE), 1) == iota((rows, LANE), 0) % each + first
            gcol_s[rows_of(g, at, rows), :] = jnp.sum(
                jnp.where(lane, dot(pick, tail), 0.0), axis=-1, keepdims=True
            )
        pre[...] = dot(x_s[rows_of(g), :], win[...])
        activate(g)
        back = gp[rows_of(g), :]
        whole[...] = dot(back, win_t[...])
        half_out[0, k] = whole[:, pl.ds(other, half)].astype(BF16)
        swap_of(0, k).start()
        half_own[k] = whole[:, pl.ds(mine, half)]

    def slots_back(k):
        g = group_at(k)
        gg = jnp.sum(ggv[rows_of(g), :], axis=-1, keepdims=True) + jnp.sum(
            u_s[rows_of(g), pl.ds(mine, half)].astype(F32) * bias_half, axis=-1, keepdims=True
        )
        number = None
        for at, rows, each, first in parts:
            q, r = iota((per * 16, rows), 1), iota((per * 16, rows), 0)
            lane = iota((rows, LANE), 1) == iota((rows, LANE), 0) % each + first
            high, low = split(jnp.where(lane, gg[at : at + rows, :], 0.0))
            line = r - q // each * 16
            piece = dot(one(line == gate_row), high) + dot(one(line == gate_row + 1), low)
            number = piece if number is None else number + piece
        swap_of(0, k).wait()
        pack(2, g, (half_own[k] + half_in[0, k].astype(F32)).astype(BF16), number)
        a2a_send(2, k)

    a2a_forward(1, 1)
    slots_in(0)
    slots_in(1)
    slots_back(0)
    a2a_forward(1, 2)
    slots_back(1)
    slots_in(2)
    a2a_forward(1, 3)
    slots_back(2)
    slots_in(3)
    slots_back(3)

    for k in range(GROUPS):
        act = hid[rows_of(group_at(k)), :]
        whole[...] = dot(act, wout[...])
        half_out[1, k] = whole[:, pl.ds(other, half)].astype(BF16)
        swap_of(1, k).start()
        half_own[k] = whole[:, pl.ds(mine, half)] + bias_half
    for k in range(GROUPS):
        swap_of(1, k).wait()
        pack(3, group_at(k), (half_own[k] + half_in[1, k].astype(F32)).astype(BF16), None)

    sg[...] = (gcol_s[...] * u_s[...].astype(F32)).astype(BF16)
    x_t[...] = jnp.transpose(x_s[...])
    hid_t[...] = jnp.transpose(hid[...])
    o_beo[...] = jnp.sum(sg[...].astype(F32), axis=0, keepdims=True)
    o_bei[...] = jnp.sum(gp[...].astype(F32), axis=0, keepdims=True)
    stores = []
    mix_t = jnp.transpose(mix[...])

    flat_id = iota((tp, z.slots), 1)
    back_one = [one(flat_id == f) for f in flat_col]
    for k in range(GROUPS):
        a2a_forward(2, k)
    for k in SEND_ORDER:
        a2a_send(3, k)
    tail_lane = iota((tp, per * 16), 1)
    number = [None, None]
    for k in range(GROUPS):
        g = group_at(k)
        a2a_take(2, k)
        assemble(2, g, y_s)
        tails = [tail_of(2, r_msg, g), tail_of(2, f_msg, g)]
        for c in range(2):
            at = r_col[c] * 16 + (gate_row - g * (per * 16))
            pick = one(sent_col[c] & ((tail_lane == at) | (tail_lane == at + 1)))
            piece = dot(pick, tails[0]) + dot(pick, tails[1])
            number[c] = piece if number[c] is None else number[c] + piece
    grad_gate = [
        jnp.sum(
            jnp.where(iota((tp, LANE), 1) == j_col[c], number[c], 0.0), axis=-1, keepdims=True
        )
        for c in range(2)
    ]
    mean_gate = gate[0] * grad_gate[0] + gate[1] * grad_gate[1]
    e_pad = up_to(z.experts, LANE)
    e_lane = iota((tp, e_pad), 1)
    grad_logits = jnp.where(
        e_lane == r_col[0], gate[0] * (grad_gate[0] - mean_gate), 0.0
    ) + jnp.where(e_lane == r_col[1], gate[1] * (grad_gate[1] - mean_gate), 0.0)
    gl_high, gl_low = split(grad_logits)
    router_pad = router_ref[...]
    if e_pad > z.experts:
        router_pad = jnp.concatenate(
            [router_pad, jnp.zeros((e_pad - z.experts, width), BF16)], axis=0
        )
    grad_n2 = (
        dot(back_one[0] + back_one[1], y_s[...])
        + dot(gl_high, router_pad)
        + dot(gl_low, router_pad)
    )
    grad_router = dot_at(gl_high, n2[0:tp, :]) + dot_at(gl_low, n2[0:tp, :])
    smallf[...] = jnp.zeros(smallf.shape, F32)
    ne = z.experts
    smallf[0:ne, :] = grad_router[0:ne, :]
    normal = normal2[...]
    smallf[ne + 2 : ne + 3, :] = jnp.sum(grad_n2 * normal, axis=0, keepdims=True)
    smallf[ne + 3 : ne + 4, :] = jnp.sum(grad_n2, axis=0, keepdims=True)
    gm[...] = upk[0:tp, :].astype(F32) + norm_backward(grad_n2, normal, inverse2, row_of(ln2g_ref))
    ag[tp:, :] = jnp.zeros((tk - tp, width), BF16)
    ag[0:tp, :] = gm[...].astype(BF16)
    smallf[ne + 4 : ne + 5, :] = jnp.sum(ag[...].astype(F32), axis=0, keepdims=True)

    groups = []
    for order in chain_orders(z.bits, z.chains) + [z.bits]:
        start, size, steps = 0, n, []
        for b in order:
            bit = lax.rem(me // b, 2)
            peer = me + b * (1 - 2 * bit)
            size = size // 2
            steps.append((peer, start + (1 - bit) * size, start + bit * size, size))
            start = start + bit * size
        groups.append((steps, start))
    n_main = len(groups) - 1

    def chain_of(g):
        if g < n_main:
            return chain_g.at[g], [r.at[g] for r in chain_r], chain_a.at[g], z.chunk
        return chain_small, list(small_r), small_a, z.small

    def region(ref, at, count, rows):
        return ref.at[pl.ds(pl.multiple_of(at * rows, 16), count * rows)]

    def rs_copy(g, s):
        src, bufs, _, rows = chain_of(g)
        peer, give, _, size = groups[g][0][s]
        return remote(
            region(src, give, size, rows), bufs[s], cs.at[g], cr.at[g, s], (peer, core)
        )

    def rs_add(g, s, at, count, dst):
        src, bufs, _, rows = chain_of(g)
        keep = groups[g][0][s][2]

        def go(i, carry):
            here = pl.ds(pl.multiple_of((at + i) * rows, 16), rows)
            there = pl.ds(pl.multiple_of((at + i - keep) * rows, 16), rows)
            dst[here, :] = (src[here, :].astype(F32) + bufs[s][there, :].astype(F32)).astype(BF16)
            return carry

        lax.fori_loop(0, count, go, 0, unroll=2 if count % 2 == 0 else 1)

    def rs_step(g, s):
        src, _, out, _ = chain_of(g)
        rs_copy(g, s).wait()
        if s + 1 < nbits:
            _, give, keep, size = groups[g][0][s + 1]
            rs_add(g, s, give, size, src)
            rs_copy(g, s + 1).start()
            rs_add(g, s, keep, size, src)
        else:
            rs_add(g, s, groups[g][1], 1, out)
            ag_copy(g, s).start()

    def ag_copy(g, s):
        _, _, out, rows = chain_of(g)
        peer, _, keep, size = groups[g][0][s]
        piece = region(out, keep, size, rows)
        return remote(piece, piece, as_.at[g], ar.at[g, s], (peer, core))

    def ag_step(g, s):
        _, _, out, rows = chain_of(g)
        peer, give, _, size = groups[g][0][s]
        ag_copy(g, s).wait_send()
        piece = region(out, give, size, rows)
        remote(piece, piece, as_.at[g], ar.at[g, s], (peer, core)).wait_recv()
        if s > 0:
            ag_copy(g, s - 1).start()

    waiting = list(chain_steps(z.bits, z.chains))

    def advance(place):
        while waiting and waiting[0][0] <= place:
            _, g, s = waiting.pop(0)
            if s >= 0:
                rs_step(g, s)
            else:
                ag_step(g, -1 - s)

    filled = 0

    def fill(value):
        nonlocal filled
        rows = value.shape[0]
        for b in range(value.shape[1] // LANE):
            g, at = divmod(filled, z.chain_rows)
            chain_g[g, at : at + rows, :] = value[:, b * LANE : (b + 1) * LANE].astype(BF16)
            filled += rows
            if filled == (g + 1) * z.chain_rows:
                rs_copy(g, 0).start()

    if z.chain_rows < n * z.chunk:
        for g in range(n_main):
            chain_g[g, z.chain_rows :, :] = jnp.zeros((n * z.chunk - z.chain_rows, LANE), BF16)
    fill(dot(mix_t, ag[...]))
    advance(0)

    dm[...] = dot_bt(ag[0:tp, :], wo[...]).astype(BF16)
    for p in range(z.pairs):
        lanes = slice(p * LANE, (p + 1) * LANE)
        qp, kp, vp, dp = q_s[0:tp, lanes], k_s[:, lanes], v_s[:, lanes], dm[:, lanes]
        dq, dk, dv = [], [], []
        for h in range(2):
            prob = probs[2 * p + h]
            gprob = dot_bt(dp * head_mask[h], vp)
            inner = jnp.sum(prob * gprob, axis=-1, keepdims=True)
            gs = (prob * (gprob - inner)).astype(BF16)
            dq.append(dot(gs, kp))
            dk.append(dot_at(gs, qp))
            dv.append(dot_at(prob.astype(BF16), dp))
        for c, (pair, scale) in enumerate(((dq, score_scale), (dk, score_scale), (dv, 1.0))):
            value = (jnp.where(low_lane, pair[0], pair[1]) * scale).astype(BF16)
            at = slice(c * hw + p * LANE, c * hw + (p + 1) * LANE)
            if c == 0:
                gpr[0:tp, at] = value
                gpr[tp:, at] = jnp.zeros((tk - tp, LANE), BF16)
            else:
                gpr[:, at] = value
        joined = jnp.concatenate(
            [gpr[:, c * hw + p * LANE : c * hw + (p + 1) * LANE] for c in range(3)], axis=1
        )
        fill(dot(n1t[...], joined))
        advance(1 + p)

    head_part = None
    for c in range(3):
        piece = dot_bt(gpr[0:tp, c * hw : (c + 1) * hw], wqkv[c])
        head_part = piece if head_part is None else head_part + piece
    gn_out[...] = head_part.astype(BF16)
    swap = remote(gn_out, gn_in, hs.at[2, 1], hr.at[2, 1], sib)
    swap.start()
    smallf[ne + 5 : ne + 6, 0:hw] = jnp.sum(gpr[:, 0:hw].astype(F32), axis=0, keepdims=True)
    smallf[ne + 6 : ne + 7, 0:hw] = jnp.sum(
        gpr[:, 2 * hw : 3 * hw].astype(F32), axis=0, keepdims=True
    )
    swap.wait()
    grad_n1 = gn_out[...].astype(F32) + gn_in[...].astype(F32)
    normal = normal1[...]
    smallf[ne : ne + 1, :] = jnp.sum(grad_n1 * normal, axis=0, keepdims=True)
    smallf[ne + 1 : ne + 2, :] = jnp.sum(grad_n1, axis=0, keepdims=True)
    back = gm[...] + norm_backward(grad_n1, normal, inverse1, row_of(ln1g_ref))
    gtok_out[...] = back[0:tok, :]
    copy = pltpu.make_async_copy(gtok_out, o_gtok, osem.at[0])
    copy.start()
    stores.append(copy)
    used = z.small_rows * (width // LANE)
    for b in range(width // LANE):
        chain_small[b * z.small_rows : (b + 1) * z.small_rows, :] = smallf[
            :, b * LANE : (b + 1) * LANE
        ].astype(BF16)
    if used < n * z.small:
        chain_small[used:, :] = jnp.zeros((n * z.small - used, LANE), BF16)
    rs_copy(n_main, 0).start()
    advance(1 + z.pairs)

    for k in range(GROUPS):
        a2a_forward(3, k)
    for k in range(GROUPS):
        a2a_take(3, k)
        assemble(3, group_at(k), y_s)
    branch = gate[0] * dot(back_one[0], y_s[...]) + gate[1] * dot(back_one[1], y_s[...])
    output = mid[...] + branch
    tok_out[...] = output[0:tok, :].astype(BF16)
    copy = pltpu.make_async_copy(tok_out, o_tok, osem.at[1])
    copy.start()
    stores.append(copy)
    lane_id = iota((1, LANE), 1)
    x_all = xf[...]
    line = jnp.zeros((1, LANE), F32)
    for i, number in enumerate(
        (
            jnp.sum(keep_col * x_all * x_all),
            stat_attn,
            jnp.sum(keep_col * branch * branch),
            jnp.sum(keep_col * output * output),
            jnp.sum(keep_col),
        )
    ):
        line = jnp.where(lane_id == i, number, line)
    stat[me] = jnp.broadcast_to(line, (8, LANE))

    def stat_go(j, carry):
        p = lax.rem(me + j, n)
        remote(stat.at[me], stat.at[me], st.at[0], st.at[1], (p, core)).start()
        return carry

    lax.fori_loop(1, n, stat_go, 0)

    advance(LAST)
    block = stat.at[pl.ds(0, n - 1)]
    remote(block, block, st.at[0], st.at[1], sib).wait()
    totals = jnp.sum(stat[...], axis=0)
    count = jnp.sum(jnp.where(iota((8, LANE), 1) == 4, totals, 0.0), axis=-1, keepdims=True)
    o_rms[...] = jnp.sqrt(totals / (count * width))

    for b in range(width // LANE):
        o_small[:, b * LANE : (b + 1) * LANE] = small_a[
            b * z.small_rows : (b + 1) * z.small_rows, :
        ].astype(F32)
    for i in range(4):
        a2a_sent(i)
    for copy in stores:
        copy.wait()


def last_kernel(
    z,
    i_tok,
    i_gtok,
    x_t,
    sg,
    hid_t,
    gp,
    red,
    i_small,
    i_bei,
    i_beo,
    i_rms,
    o_tok,
    o_gtok,
    o_ln1g,
    o_ln1b,
    o_wqkv,
    o_bqv,
    o_wo,
    o_bo,
    o_ln2g,
    o_ln2b,
    o_router,
    o_win,
    o_bin,
    o_wout,
    o_bout,
    o_rms,
    wqkv,
    wo,
    win,
    wout,
    osem,
):
    ne, width, hw = z.experts, z.width, z.hw
    stores = []

    def store(src, dst, i):
        copy = pltpu.make_async_copy(src, dst, osem.at[i])
        copy.start()
        stores.append(copy)

    store(i_tok, o_tok, 0)
    store(i_gtok, o_gtok, 1)
    for ref, i in ((o_ln1g, 0), (o_ln1b, 1), (o_ln2g, 2), (o_ln2b, 3), (o_bo, 4)):
        ref[...] = i_small[ne + i : ne + i + 1, :].reshape(width)
    o_router[...] = i_small[0:ne, :]
    o_bqv[...] = i_small[ne + 5 : ne + 7, 0:hw]
    o_bin[...] = i_bei[...]
    o_bout[...] = i_beo[...]
    o_rms[...] = i_rms[0:1, 0:4].reshape(4)

    at = 0

    def take(rows):
        nonlocal at
        g, row = divmod(at, z.chain_rows)
        at += rows
        return red[g, row : row + rows, :].astype(F32)

    for b in range(width // LANE):
        wo[:, b * LANE : (b + 1) * LANE] = take(hw)
    store(wo, o_wo, 2)
    for p in range(z.pairs):
        for c in range(3):
            wqkv[c, :, p * LANE : (p + 1) * LANE] = take(width)
    store(wqkv, o_wqkv, 3)
    tiles = z.ff // TILE
    for t in range(tiles):
        cols = slice(t * TILE, (t + 1) * TILE)
        win[:, cols] = dot(x_t[...], gp[:, cols])
        store(win.at[:, cols], o_win.at[0, :, cols], 4 + t)
    for t in range(tiles):
        rows = slice(t * TILE, (t + 1) * TILE)
        wout[rows, :] = dot(hid_t[rows, :], sg[...])
        store(wout.at[rows, :], o_wout.at[0, rows, :], 4 + tiles + t)
    for copy in stores:
        copy.wait()


def per_device(
    tokens,
    grad_out,
    valid_mask,
    routes,
    slot_index,
    ln1_gain,
    ln1_bias,
    w_qkv,
    bias_qv,
    w_attn_out,
    b_attn_out,
    ln2_gain,
    ln2_bias,
    router,
    w_expert_in,
    b_expert_in,
    w_expert_out,
    b_expert_out,
):
    tok, width = tokens.shape
    hw = w_qkv.shape[2]
    ff = w_expert_in.shape[2]
    z = Sizes(lax.axis_size("dp"), tok, width, hw, ff, router.shape[1])
    n, tp, tk = z.n, z.tp, z.tk
    nbits = len(z.bits)
    vmem = pl.BlockSpec(memory_space=pltpu.VMEM)
    any_ = pl.BlockSpec(memory_space=pl.ANY)
    shape = jax.ShapeDtypeStruct
    groups = z.chains
    kept = pltpu.VMEM if n <= 16 else shape
    keep = lambda a: pltpu.with_memory_space_constraint(a, pltpu.VMEM) if n <= 16 else a
    V = pltpu.VMEM
    scratch = [
        V((tok, width), BF16),
        V((tok, width), BF16),
        V((1, tok), jnp.int32),
        V((2, tok), jnp.int32),
        V((2, tok), jnp.int32),
        V((width,), F32),
        V((width,), F32),
        V((2, hw), F32),
        V((width,), F32),
        V((width,), F32),
        V((width,), F32),
        V((z.experts, width), BF16),
        V((1, ff), F32),
        V((1, width), F32),
        V((tok, width), BF16),
        V((tok, width), F32),
        V((3, width, hw), BF16),
        V((hw, width), BF16),
        V((width, ff), BF16),
        V((ff, width), BF16),
        V((tp, width), F32),
        V((tp, width), F32),
        V((tk, width), BF16),
        V((width, tk), BF16),
        V((tk, width), BF16),
        V((tk, hw), BF16),
        V((tk, hw), BF16),
        V((tk, hw), BF16),
        V((2 * z.pairs, tp, tk), F32),
        V((tk, hw), BF16),
        V((tp, width), F32),
        V((tp, width), F32),
        V((tp, width), F32),
        V((tp, width), F32),
        V((tk, width), BF16),
        V((z.slots, tk), BF16),
        V((8, tk), F32),
        V((tk, 8), F32),
        V((z.slots, width), BF16),
        V((z.slots, width), BF16),
        V((z.slots, width), BF16),
        V((z.slots, ff), F32),
        V((z.rows, ff), F32),
        V((z.slots, ff), BF16),
        V((z.slots, 1), F32),
        V((z.slots, LANE), F32),
        V((2, GROUPS, z.rows, z.half), BF16),
        V((2, GROUPS, z.rows, z.half), BF16),
        V((GROUPS, z.rows, z.half), F32),
        V((z.rows, width), F32),
        V((ff, width), BF16),
        V((width, ff), BF16),
        V((tp, width), F32),
        V((tk, width), BF16),
        V((tp, hw), BF16),
        V((tk, 3 * hw), BF16),
        V((tp, width), BF16),
        V((tp, width), BF16),
        V((z.small_rows, width), F32),
        V((n, 8, LANE), F32),
        V((4, n, z.msg, LANE), BF16),
        V((4, n, z.msg, LANE), BF16),
        V((4, n, z.msg, LANE), BF16),
        V((groups, n * z.chunk, LANE), BF16),
        V((n * z.small, LANE), BF16),
    ]
    scratch += [V((groups, (n >> (s + 1)) * z.chunk, LANE), BF16) for s in range(nbits)]
    scratch += [V(((n >> (s + 1)) * z.small, LANE), BF16) for s in range(nbits)]
    scratch += [
        V((n * z.small, LANE), BF16),
        DMA((18,)),
        DMA((2,)),
        DMA((3, GROUPS)),
        DMA((3, GROUPS)),
        DMA((4,)),
        DMA((4, GROUPS)),
        DMA((4,)),
        DMA((4, GROUPS)),
        DMA((groups + 1,)),
        DMA((groups + 1, nbits)),
        DMA((groups + 1,)),
        DMA((groups + 1, nbits)),
        DMA((2,)),
    ]
    row = lambda v: v.reshape(1, -1)
    outs = pl.pallas_call(
        functools.partial(mega_kernel, z),
        out_shape=(
            kept((tok, width), BF16),
            kept((tok, width), F32),
            kept((width, z.slots), BF16),
            kept((z.slots, width), BF16),
            kept((ff, z.slots), BF16),
            kept((z.slots, ff), BF16),
            kept((groups, n * z.chunk, LANE), BF16),
            kept((z.small_rows, width), F32),
            kept((1, ff), F32),
            kept((1, width), F32),
            kept((8, LANE), F32),
        ),
        in_specs=[any_] * 18,
        out_specs=(any_,) * 2 + (vmem,) * 9,
        scratch_shapes=scratch,
        compiler_params=pltpu.CompilerParams(
            collective_id=0,
            has_side_effects=True,
            vmem_limit_bytes=(54 if n <= 16 else 61) * 2**20,
        ),
    )(*(
        pltpu.with_memory_space_constraint(a, pltpu.HBM)
        for a in (
        tokens,
        grad_out,
        row(valid_mask),
        routes.T,
        slot_index.T,
        ln1_gain,
        ln1_bias,
        jnp.transpose(w_qkv, (1, 0, 2)),
        bias_qv,
        w_attn_out,
        b_attn_out,
        ln2_gain,
        ln2_bias,
        router.T,
        w_expert_in[0],
        b_expert_in,
        w_expert_out[0],
        b_expert_out,
        )
    ))
    ne = z.experts
    vec = shape((width,), F32)
    last = pl.pallas_call(
        functools.partial(last_kernel, z),
        out_shape=(
            shape((tok, width), BF16),
            shape((tok, width), F32),
            vec,
            vec,
            shape((3, width, hw), F32),
            shape((2, hw), F32),
            shape((hw, width), F32),
            vec,
            vec,
            vec,
            shape((ne, width), F32),
            shape((1, width, ff), F32),
            shape((1, ff), F32),
            shape((1, ff, width), F32),
            shape((1, width), F32),
            shape((4,), F32),
        ),
        in_specs=[any_] * 2 + [vmem] * 9,
        out_specs=(
            [any_] * 2
            + [vmem] * 2
            + [any_, vmem, any_]
            + [vmem] * 4
            + [any_, vmem, any_, vmem, vmem]
        ),
        scratch_shapes=[
            V((3, width, hw), F32),
            V((hw, width), F32),
            V((width, ff), F32),
            V((ff, width), F32),
            DMA((4 + 2 * (ff // TILE),)),
        ],
        compiler_params=pltpu.CompilerParams(vmem_limit_bytes=(30 if n <= 16 else 48) * 2**20),
    )(*(keep(a) for a in outs))
    return (
        last[0],
        last[1],
        last[2],
        last[3],
        jnp.transpose(last[4], (1, 0, 2)),
        *last[5:10],
        last[10].T,
        *last[11:],
    )


def solution(mesh):
    return jax.shard_map(
        per_device,
        mesh=mesh,
        in_specs=(
            P("dp", None),
            P("dp", None),
            P("dp"),
            P("dp", None),
            P("dp", None),
            P(),
            P(),
            P(None, None, "tensor"),
            P(None, "tensor"),
            P("tensor", None),
            P(),
            P(),
            P(),
            P(),
            P("dp", None, "tensor"),
            P("dp", "tensor"),
            P("dp", "tensor", None),
            P("dp", None),
        ),
        out_specs=(
            P("dp", None),
            P("dp", None),
            P(),
            P(),
            P(None, None, "tensor"),
            P(None, "tensor"),
            P("tensor", None),
            P(),
            P(),
            P(),
            P(),
            P("dp", None, "tensor"),
            P("dp", "tensor"),
            P("dp", "tensor", None),
            P("dp", None),
            P(),
        ),
        check_vma=False,
    )
```

```python
import functools
import math

import jax
import jax.numpy as jnp
from jax import lax
from jax.experimental import pallas as pl
from jax.experimental.pallas import tpu as pltpu
from jax.sharding import PartitionSpec as P

HEAD = 64
SEQ = 197
LANE = 128
EPS = 1e-06
ROOT = math.sqrt(2.0 / math.pi)
CUBE = 0.044715
GROUPS = 4
QUAD = 4
LAST = 5
CHAINS = (
    (2, 0, 1, 3),
    (2, 0, 1, 3),
    (3, 1, 0, 2),
)
UNITS = (
    (3, 2),
    (2, 3),
    (3, 2),
)
PIECES = (
    (0, 1, 2, 3),
    (1, 2, 0, 3),
    (2, 0, 3, 1),
    (1, 2, 0, 3),
    (0, 1, 3, 2),
    (1, 3, 0, 2),
    (0, 1, 2, 3),
    (1, 3, 0, 2),
    (0, 2, 3, 1),
)
STEPS = (
    (4, 3, 9), (5, 4, 9), (5, 5, 9), (5, 0, 0), (5, 1, 0), (5, 2, 0), (5, 6, 0), (5, 3, 0),
    (5, 4, 0), (5, 0, 1), (5, 6, 1), (5, 1, 1), (5, 2, 1), (5, 5, 0), (5, 3, 1), (5, 6, 2),
    (5, 0, 2), (5, 4, 1), (5, 1, 2), (5, 2, 2), (5, 5, -4), (5, 3, -4), (5, 4, -4), (5, 6, 3),
    (5, 5, 1), (5, 0, 3), (5, 7, -4), (5, 8, -4), (5, 6, -4), (5, 1, 3), (5, 2, 3), (5, 4, -3),
    (5, 12, -4), (5, 11, -4), (5, 10, -4), (5, 9, -4), (5, 5, -3), (5, 3, -3), (5, 0, -4),
    (5, 8, -3), (5, 6, -3), (5, 1, -4), (5, 12, -3), (5, 2, -4), (5, 10, -3), (5, 7, -3),
    (5, 5, -2), (5, 11, -3), (5, 0, -3), (5, 3, -2), (5, 9, -3), (5, 2, -3), (5, 12, -2),
    (5, 1, -3), (5, 4, -2), (5, 7, -2), (5, 9, -2), (5, 8, -2), (5, 6, -2), (5, 0, -2),
    (5, 2, -2), (5, 10, -2), (5, 11, -2), (5, 12, -1), (5, 5, -1), (5, 1, -2), (5, 4, -1),
    (5, 3, -1), (5, 0, -1), (5, 2, -1), (5, 7, -1), (5, 8, -1), (5, 6, -1), (5, 9, -1),
    (5, 10, -1), (5, 1, -1), (5, 11, -1),
)
SEND_ORDER = (0, 2, 1, 3)
TILE = 256
MESH = pl.DeviceIdType.MESH
F32 = jnp.float32
BF16 = jnp.bfloat16
DMA = pltpu.SemaphoreType.DMA


def up_to(value, step):
    return -(-value // step) * step


def dot(a, b):
    return lax.dot_general(a, b, (((1,), (0,)), ((), ())), preferred_element_type=F32)


def dot_bt(a, b):
    return lax.dot_general(a, b, (((1,), (1,)), ((), ())), preferred_element_type=F32)


def dot_at(a, b):
    return lax.dot_general(a, b, (((0,), (0,)), ((), ())), preferred_element_type=F32)


def row_of(ref):
    return ref[...].reshape(1, ref.shape[0])


def iota(shape, dim):
    return lax.broadcasted_iota(jnp.int32, shape, dim)


def one(cond, kind=BF16):
    return jnp.where(cond, 1.0, 0.0).astype(kind)


def split(value):
    high = value.astype(BF16)
    return high, (value - high.astype(F32)).astype(BF16)


def norm_parts(values):
    scale = 1.0 / values.shape[-1]
    center = values - jnp.sum(values, axis=-1, keepdims=True) * scale
    inverse = lax.rsqrt(jnp.sum(center * center, axis=-1, keepdims=True) * scale + EPS)
    return center * inverse, inverse


def norm_backward(incoming, normal, inverse, gain_vec):
    scale = 1.0 / incoming.shape[-1]
    scaled = incoming * gain_vec
    return inverse * (
        scaled
        - jnp.sum(scaled, axis=-1, keepdims=True) * scale
        - normal * (jnp.sum(scaled * normal, axis=-1, keepdims=True) * scale)
    )


def remote(src, dst, send_sem, recv_sem, device):
    return pltpu.make_async_remote_copy(
        src_ref=src,
        dst_ref=dst,
        send_sem=send_sem,
        recv_sem=recv_sem,
        device_id=device,
        device_id_type=MESH,
    )


class Sizes:
    def __init__(self, n, tok, width, heads_width, ff, experts):
        self.n = n
        self.tok = tok
        self.tp = up_to(tok, 16)
        self.tk = up_to(tok, LANE)
        self.width = width
        self.hw = heads_width
        self.pairs = heads_width // LANE
        self.ff = ff
        self.experts = experts
        self.cap = 2 * (3 * tok // (2 * n))
        self.main = self.cap // 16 * 16
        self.tail = self.cap - self.main
        self.half = width // 2
        self.blocks = self.half // LANE
        self.msg = self.main * self.blocks + 16
        self.per = n // GROUPS
        self.gm = self.per * self.main
        self.gt = self.per * self.tail
        self.rows = self.per * self.cap
        self.slots = n * self.cap
        self.bits = [1 << i for i in range(n.bit_length() - 1)]
        self.chain_rows = heads_width * width // LANE // 3
        self.chunk = up_to(up_to(self.chain_rows, n) // n, 16)
        self.share = 3 * LANE // QUAD
        self.unit_rows = self.share * width // LANE
        self.unit = up_to(up_to(self.unit_rows, n // QUAD) // (n // QUAD), 16)
        self.cuts = 3 if self.unit % 48 == 0 else 1
        self.cut = self.unit // self.cuts
        self.small_rows = up_to(experts + 7, 16)
        self.small = up_to(up_to(self.small_rows * width // LANE, n) // n, 16)
        fits = 0 < self.tail * self.blocks <= 14 and self.gt % 16 == 0
        fits = fits and self.chain_rows % heads_width == 0 and len(self.bits) > 2
        if not fits or experts != n or (1 << len(self.bits)) != n:
            raise ValueError("unsupported sizes")


def sum_plan(bits, pairs, cuts):
    if len(bits) == 4 and pairs == 3 and cuts == 3:
        take = lambda orders: [[bits[i] for i in order] for order in orders]
        halve = take(CHAINS) + take(UNITS) + [bits]
        return halve, take(CHAINS) + take(PIECES) + [bits], STEPS
    rolled = [bits[i:3] + bits[:i] + bits[3:] for i in range(3)]
    halve = rolled + [bits[2:]] * pairs + [bits]
    double = rolled + [rolled[i % 3] for i in range(pairs * cuts)] + [bits]
    steps = [(LAST, 3 + p, 9) for p in range(pairs)]
    for s in range(len(bits)):
        steps += [(LAST, g, s) for g, order in enumerate(halve) if s < len(order)]
    for s in range(len(bits) - 1, -1, -1):
        steps += [(LAST, g, -1 - s) for g in range(len(double))]
    return halve, double, steps


def mega_kernel(
    z,
    tokens_hbm,
    grad_out_hbm,
    valid_hbm,
    routes_hbm,
    slots_hbm,
    ln1g_hbm,
    ln1b_hbm,
    wqkv_hbm,
    bqv_hbm,
    wo_hbm,
    bo_hbm,
    ln2g_hbm,
    ln2b_hbm,
    router_hbm,
    win_hbm,
    bin_hbm,
    wout_hbm,
    bout_hbm,
    o_tok,
    o_gtok,
    x_t,
    sg,
    hid_t,
    gp,
    red_w,
    red_u,
    o_small,
    o_bei,
    o_beo,
    o_rms,
    tokens_ref,
    grad_out_ref,
    valid_ref,
    routes_ref,
    slots_ref,
    ln1g_ref,
    ln1b_ref,
    bqv_ref,
    bo_ref,
    ln2g_ref,
    ln2b_ref,
    router_ref,
    bin_ref,
    bout_ref,
    tok_out,
    gtok_out,
    wqkv,
    wo,
    win,
    wout,
    xf,
    normal1,
    n1,
    n1q,
    q_t,
    k_t,
    dm_t,
    gpt,
    gq,
    upk,
    q_s,
    k_s,
    v_s,
    probs,
    mix,
    part,
    part_in,
    mid,
    normal2,
    n2,
    onehot,
    rows8,
    cols8,
    u_s,
    x_s,
    y_s,
    gh,
    pre,
    hid,
    gcol_s,
    ggv,
    half_out,
    half_in,
    half_own,
    whole,
    win_t,
    wout_t,
    gm,
    ag,
    dm,
    gn_out,
    gn_in,
    smallf,
    stat,
    s_msg,
    r_msg,
    f_msg,
    sum_w,
    sum_u,
    sum_s,
    *rest,
):
    nbits = len(z.bits)
    from_w = rest[:nbits]
    from_s = rest[nbits : 2 * nbits]
    from_u = rest[2 * nbits : 3 * nbits - 2]
    red_s, wsem, osem, hs, hr, ss, rs, fs, fr, cs, cr, as_, ar, st, qs, us, ur = rest[
        3 * nbits - 2 :
    ]
    n = z.n
    me, core = lax.axis_index("dp"), lax.axis_index("tensor")
    sib = (me, 1 - core)
    tok, tp, tk, width, hw, half = z.tok, z.tp, z.tk, z.width, z.hw, z.half
    mine = pl.multiple_of(core * half, LANE)
    other = pl.multiple_of((1 - core) * half, LANE)

    barrier = pltpu.get_barrier_semaphore()

    def greet(j, carry):
        pl.semaphore_signal(
            barrier, inc=1, device_id=(lax.rem(me + j, n), core), device_id_type=MESH
        )
        return carry

    lax.fori_loop(1, n, greet, 0)
    pl.semaphore_signal(barrier, inc=1, device_id=sib, device_id_type=MESH)

    tokens_in = [
        pltpu.make_async_copy(a, b, wsem.at[4 + i])
        for i, (a, b) in enumerate(((tokens_hbm, tokens_ref), (grad_out_hbm, grad_out_ref)))
    ]
    small_in = [
        pltpu.make_async_copy(a, b, wsem.at[6 + i])
        for i, (a, b) in enumerate(
            (
                (valid_hbm, valid_ref),
                (routes_hbm, routes_ref),
                (slots_hbm, slots_ref),
                (ln1g_hbm, ln1g_ref),
                (ln1b_hbm, ln1b_ref),
                (bqv_hbm, bqv_ref),
                (bo_hbm, bo_ref),
                (ln2g_hbm, ln2g_ref),
                (ln2b_hbm, ln2b_ref),
                (router_hbm, router_ref),
                (bin_hbm, bin_ref),
                (bout_hbm, bout_ref),
            )
        )
    ]
    for copy in small_in + tokens_in[::-1]:
        copy.start()
    weights = [
        pltpu.make_async_copy(a, b, wsem.at[i])
        for i, (a, b) in enumerate(
            ((wqkv_hbm, wqkv), (wo_hbm, wo), (wout_hbm, wout), (win_hbm, win))
        )
    ]
    for copy in weights:
        copy.start()

    per = z.per
    own = me // per
    own_bits = [lax.rem(own, 2), own // 2]

    def group_at(k):
        turned = [b + t * (1 - 2 * b) for b, t in zip(own_bits, (k % 2, k // 2))]
        return turned[0] + 2 * turned[1]

    def members(ref, i, g):
        return ref.at[i, pl.ds(g * per, per)]

    def rows_of(g, first=0, count=None):
        return pl.ds(pl.multiple_of(g * z.rows + first, 16), z.rows if count is None else count)

    def a2a_send(i, k):
        g = group_at(k)
        if k == 0:
            pltpu.make_async_copy(s_msg.at[i, me], r_msg.at[i, me], rs.at[i, own]).start()

        def go(m, carry):
            p = g * per + lax.rem(me + m, per)
            remote(s_msg.at[i, p], r_msg.at[i, me], ss.at[i], rs.at[i, own], (p, core)).start()
            return carry

        lax.fori_loop(1 if k == 0 else 0, per, go, 0)

    def a2a_forward(i, k):
        g = group_at(k)
        block = members(r_msg, i, g)
        remote(block, block, ss.at[i], rs.at[i, g], sib).wait_recv()
        remote(block, members(f_msg, i, g), fs.at[i], fr.at[i, g], sib).start()

    def a2a_take(i, k):
        block = members(f_msg, i, group_at(k))
        remote(block, block, fs.at[i], fr.at[i, group_at(k)], sib).wait_recv()

    def a2a_sent(i):
        block = s_msg.at[i, pl.ds(0, n - 1)]
        remote(block, block, ss.at[i], rs.at[i, 0], sib).wait_send()
        remote(r_msg.at[i], f_msg.at[i], fs.at[i], fr.at[i, 0], sib).wait_send()

    def tail_of(i, src, g):
        rows = src[i, pl.ds(g * per, per), z.msg - 16 : z.msg, :]
        return rows.reshape(per * 16, LANE)

    def assemble(i, g, out):
        q, r = iota((z.gt, per * 16), 0), iota((z.gt, per * 16), 1)
        base = q // z.tail * 16 + q % z.tail
        for src, at in ((r_msg, mine), (f_msg, other)):
            tail = tail_of(i, src, g)
            for b in range(z.blocks):
                lanes = pl.ds(pl.multiple_of(at + b * LANE, LANE), LANE)
                if z.main:
                    rows = src[i, pl.ds(g * per, per), b * z.main : (b + 1) * z.main, :]
                    out[rows_of(g, 0, z.gm), lanes] = rows.reshape(z.gm, LANE)
                pick = one(r == base + b * z.tail)
                out[rows_of(g, z.gm, z.gt), lanes] = dot(pick, tail).astype(BF16)

    def pack(i, g, value, tail):
        q, r = iota((per * 16, z.gt), 1), iota((per * 16, z.gt), 0)
        base = q // z.tail * 16 + q % z.tail
        for b in range(z.blocks):
            lanes = slice(b * LANE, (b + 1) * LANE)
            if z.main:
                s_msg[i, pl.ds(g * per, per), b * z.main : (b + 1) * z.main, :] = value[
                    0 : z.gm, lanes
                ].reshape(per, z.main, LANE)
            piece = dot(one(r == base + b * z.tail), value[z.gm : z.rows, lanes])
            tail = piece if tail is None else tail + piece
        s_msg[i, pl.ds(g * per, per), z.msg - 16 : z.msg, :] = tail.astype(BF16).reshape(
            per, 16, LANE
        )

    quad_bits = [lax.rem(me, 2), lax.rem(me // 2, 2)]

    def in_quad(q):
        turned = [b + t * (1 - 2 * b) for b, t in zip(quad_bits, (q % 2, q // 2))]
        return turned[0] + 2 * turned[1]

    def norm_send():
        for q in range(1, QUAD):
            piece = n1q.at[lax.rem(me, QUAD), core, pl.ds(0, tp)]
            peer = me - lax.rem(me, QUAD) + in_quad(q)
            remote(piece, piece, qs.at[0], qs.at[1], (peer, core)).start()

    def norm_forward():
        block = n1q.at[pl.ds(0, QUAD - 1), 0, pl.ds(0, tp)]
        remote(block, block, qs.at[0], qs.at[1], sib).wait()
        for q in range(1, QUAD):
            piece = n1q.at[in_quad(q), core, pl.ds(0, tp)]
            remote(piece, piece, qs.at[2], qs.at[3], sib).start()

    def norm_take():
        block = n1q.at[pl.ds(0, QUAD - 1), 0, pl.ds(0, tp)]
        remote(block, block, qs.at[2], qs.at[3], sib).wait()

    gate_row = 14

    for copy in small_in:
        copy.wait()
    rows8[...] = jnp.full(rows8.shape, -1.0, F32)
    rows8[0:2, 0:tok] = routes_ref[...].astype(F32)
    rows8[2:4, 0:tok] = slots_ref[...].astype(F32)
    rows8[4:5, 0:tok] = valid_ref[...].astype(F32)
    table = rows8[...]
    r_row = [table[k : k + 1, :].astype(jnp.int32) for k in range(2)]
    j_row = [table[2 + k : 3 + k, :].astype(jnp.int32) for k in range(2)]
    keep_row = table[4:5, :] > 0.5

    def targets(r, j):
        sent = (r >= 0) & (j < z.cap)
        g = r // per
        m = r - g * per
        flat = jnp.where(j < z.main, m * z.main + j, z.gm + m * z.tail + (j - z.main))
        return sent, jnp.where(sent, g * z.rows + flat, -1)

    sent_row, flat_row = zip(*[targets(r, j) for r, j in zip(r_row, j_row)])
    cols8[...] = jnp.transpose(table)
    r_col = [cols8[0:tp, k : k + 1].astype(jnp.int32) for k in range(2)]
    j_col = [cols8[0:tp, 2 + k : 3 + k].astype(jnp.int32) for k in range(2)]
    keep_col = jnp.where(cols8[0:tp, 4:5] > 0.5, 1.0, 0.0)
    sent_col, flat_col = zip(*[targets(r, j) for r, j in zip(r_col, j_col)])

    slot_id = iota((z.slots, tk), 0)
    onehot[...] = one((slot_id == flat_row[0]) | (slot_id == flat_row[1]))
    tail_id = iota((per * 16, tk), 0)
    tail_row = [
        jnp.where(s & (j >= z.main), r * 16 + (j - z.main), -1000)
        for s, r, j in zip(sent_row, r_row, j_row)
    ]

    def place(src, i, g, tail):
        first = g * (per * 16)
        for b in range(z.blocks):
            lanes = pl.ds(pl.multiple_of(mine + b * LANE, LANE), LANE)
            rows = src[:, lanes]
            if z.main:
                main = dot(onehot[rows_of(g, 0, z.gm), :], rows).astype(BF16)
                s_msg[i, pl.ds(g * per, per), b * z.main : (b + 1) * z.main, :] = main.reshape(
                    per, z.main, LANE
                )
            at = b * z.tail - first
            put = one((tail_id == tail_row[0] + at) | (tail_id == tail_row[1] + at))
            piece = dot(put, rows)
            tail = piece if tail is None else tail + piece
        s_msg[i, pl.ds(g * per, per), z.msg - 16 : z.msg, :] = tail.astype(BF16).reshape(
            per, 16, LANE
        )

    upk[tok // 16 * 16 :, :] = jnp.zeros((tk - tok // 16 * 16, width), BF16)
    tokens_in[1].wait()
    upk[0:tok, :] = grad_out_ref[...]
    for g in range(GROUPS):
        place(upk, 0, g, None)

    xf[tok // 8 * 8 :, :] = jnp.zeros((tp - tok // 8 * 8, width), F32)
    tokens_in[0].wait()
    xf[0:tok, :] = tokens_ref[...].astype(F32)
    normal, inverse1 = norm_parts(xf[...])
    normal1[...] = normal
    n1[tp:, :] = jnp.zeros((tk - tp, width), BF16)
    n1[0:tp, :] = (normal * row_of(ln1g_ref) + row_of(ln1b_ref)).astype(BF16)
    place_in = lax.rem(me, QUAD)
    for h in range(2):
        n1q[place_in, h] = n1[:, h * half : (h + 1) * half]
        for m in range(QUAD):
            n1q[m, h, tp:, :] = jnp.zeros((tk - tp, half), BF16)

    pl.semaphore_wait(barrier, n)
    for k in SEND_ORDER:
        a2a_send(0, k)

    weights[0].wait()
    for c, (dst, bias) in enumerate(((q_s, bqv_ref[0:1, :]), (k_s, None), (v_s, bqv_ref[1:2, :]))):
        value = dot(n1[0:tp, :], wqkv[c])
        if bias is not None:
            value = value + bias
        dst[tp:, :] = jnp.zeros((tk - tp, hw), BF16)
        dst[0:tp, :] = value.astype(BF16)

    score_scale = 1.0 / math.sqrt(HEAD)
    low_lane = iota((1, LANE), 1) < HEAD
    head_mask = [one(low_lane), one(jnp.logical_not(low_lane))]
    for p in range(z.pairs):
        lanes = slice(p * LANE, (p + 1) * LANE)
        qp, kp, vp = q_s[0:tp, lanes], k_s[:, lanes], v_s[:, lanes]
        outs = []
        for h in range(2):
            scores = dot_bt(qp * head_mask[h], kp) * score_scale
            scores = jnp.where(keep_row, scores, -1000000000.0)
            weights_h = jnp.exp(scores - jnp.max(scores, axis=-1, keepdims=True))
            prob = weights_h / jnp.sum(weights_h, axis=-1, keepdims=True)
            probs[2 * p + h] = prob
            outs.append(dot(prob.astype(BF16), vp))
        mix[0:tp, lanes] = jnp.where(low_lane, outs[0], outs[1]).astype(BF16)
    mix[tp:, :] = jnp.zeros((tk - tp, hw), BF16)
    weights[1].wait()
    part[...] = dot(mix[0:tp, :], wo[...])
    swap = remote(part, part_in, hs.at[2, 0], hr.at[2, 0], sib)
    swap.start()
    for p in range(z.pairs):
        lanes = slice(p * LANE, (p + 1) * LANE)
        q_t[p] = jnp.transpose(q_s[:, lanes])
        k_t[p] = jnp.transpose(k_s[:, lanes])
    swap.wait()

    attention = part[...] + part_in[...] + row_of(bo_ref)
    stat_attn = jnp.sum(keep_col * attention * attention)
    middle = xf[...] + attention
    mid[...] = middle
    normal, inverse2 = norm_parts(middle)
    normal2[...] = normal
    n2[tp:, :] = jnp.zeros((tk - tp, width), BF16)
    n2[0:tp, :] = (normal * row_of(ln2g_ref) + row_of(ln2b_ref)).astype(BF16)
    logits = dot_bt(router_ref[...], n2[...])
    expert_id = iota((z.experts, tk), 0)
    chosen = [
        jnp.sum(jnp.where(expert_id == r, logits, 0.0), axis=0, keepdims=True) for r in r_row
    ]
    top = jnp.maximum(chosen[0], chosen[1])
    raw = [jnp.exp(c - top) for c in chosen]
    total = raw[0] + raw[1]
    gate_rows = [r / total for r in raw]
    cols8[0:tk, :] = jnp.transpose(
        jnp.concatenate(gate_rows + [jnp.zeros((6, tk), F32)], axis=0)
    )
    gate = [cols8[0:tp, k : k + 1] for k in range(2)]

    slot_lane = iota((tk, LANE), 1)
    pad_col = [
        jnp.concatenate([j, jnp.full((tk - tp, 1), -1, jnp.int32)], axis=0) for j in j_col
    ]
    at_slot = [one(slot_lane == j) for j in pad_col]
    halves = [split(g) for g in gate_rows]
    for k in SEND_ORDER:
        g = group_at(k)
        number = None
        for c in range(2):
            high, low = halves[c]
            at = r_row[c] * 16 + (gate_row - g * (per * 16))
            lift = jnp.where(
                sent_row[c] & (tail_id == at), high.astype(F32), 0.0
            ) + jnp.where(sent_row[c] & (tail_id == at + 1), low.astype(F32), 0.0)
            piece = dot(lift.astype(BF16), at_slot[c])
            number = piece if number is None else number + piece
        place(n2, 1, g, number)
        if k < GROUPS - 1:
            a2a_send(1, k)

    def upstream(k):
        g = group_at(k)
        a2a_take(0, k)
        assemble(0, g, u_s)
        gh[rows_of(g), :] = dot(u_s[rows_of(g), :], wout_t[...])

    weights[2].wait()
    wout_t[...] = jnp.transpose(wout[...])
    a2a_forward(0, 0)
    a2a_forward(0, 1)
    weights[3].wait()
    win_t[...] = jnp.transpose(win[...])
    upstream(0)
    upstream(1)
    a2a_forward(0, 2)
    a2a_forward(0, 3)
    a2a_send(1, 3)
    norm_send()
    a2a_forward(1, 0)
    upstream(2)
    upstream(3)

    parts = [(0, z.gm, z.main, 0)] if z.main else []
    parts += [(z.gm, z.gt, z.tail, z.main)]
    step = 16

    def activate(g):
        def go(i, carry):
            here = pl.ds(pl.multiple_of(i * step, step), step)
            rows = pl.ds(pl.multiple_of(g * z.rows + i * step, step), step)
            gate_of = jnp.broadcast_to(gcol_s[rows, :], (step, LANE))
            total = jnp.zeros((step, LANE), F32)
            for b in range(z.ff // LANE):
                lanes = slice(b * LANE, (b + 1) * LANE)
                v = pre[here, lanes] + bin_ref[:, lanes]
                v2 = v * v
                s = 0.5 + 0.5 * jnp.tanh(v * (ROOT + (ROOT * CUBE) * v2))
                act = v * s
                back = s + act * (1.0 - s) * (2.0 * ROOT + (6.0 * ROOT * CUBE) * v2)
                up = gh[rows, lanes]
                hid[rows, lanes] = act.astype(BF16)
                gp[rows, lanes] = (gate_of * up * back).astype(BF16)
                total = total + up * act
            ggv[rows, :] = total
            return carry

        count = z.rows // step
        lax.fori_loop(0, count, go, 0, unroll=3 if count % 3 == 0 else 2)

    bias_half = bout_ref[:, pl.ds(mine, half)]

    def swap_of(j, k):
        return remote(half_out.at[j, k], half_in.at[j, k], hs.at[j, k], hr.at[j, k], sib)

    def slots_in(k):
        g = group_at(k)
        a2a_take(1, k)
        assemble(1, g, x_s)
        tail = tail_of(1, r_msg, g)
        for at, rows, each, first in parts:
            q, r = iota((rows, per * 16), 0), iota((rows, per * 16), 1)
            number = r - q // each * 16
            pick = one((number == gate_row) | (number == gate_row + 1))
            lane = iota((rows, LANE), 1) == iota((rows, LANE), 0) % each + first
            gcol_s[rows_of(g, at, rows), :] = jnp.sum(
                jnp.where(lane, dot(pick, tail), 0.0), axis=-1, keepdims=True
            )
        pre[...] = dot(x_s[rows_of(g), :], win[...])
        activate(g)
        back = gp[rows_of(g), :]
        whole[...] = dot(back, win_t[...])
        half_out[0, k] = whole[:, pl.ds(other, half)].astype(BF16)
        swap_of(0, k).start()
        half_own[k] = whole[:, pl.ds(mine, half)]

    def slots_back(k):
        g = group_at(k)
        gg = jnp.sum(ggv[rows_of(g), :], axis=-1, keepdims=True) + jnp.sum(
            u_s[rows_of(g), pl.ds(mine, half)].astype(F32) * bias_half, axis=-1, keepdims=True
        )
        number = None
        for at, rows, each, first in parts:
            q, r = iota((per * 16, rows), 1), iota((per * 16, rows), 0)
            lane = iota((rows, LANE), 1) == iota((rows, LANE), 0) % each + first
            high, low = split(jnp.where(lane, gg[at : at + rows, :], 0.0))
            line = r - q // each * 16
            piece = dot(one(line == gate_row), high) + dot(one(line == gate_row + 1), low)
            number = piece if number is None else number + piece
        swap_of(0, k).wait()
        pack(2, g, (half_own[k] + half_in[0, k].astype(F32)).astype(BF16), number)
        a2a_send(2, k)

    a2a_forward(1, 1)
    slots_in(0)
    slots_in(1)
    slots_back(0)
    a2a_forward(1, 2)
    slots_back(1)
    slots_in(2)
    a2a_forward(1, 3)
    slots_back(2)
    slots_in(3)
    slots_back(3)

    for k in range(GROUPS):
        act = hid[rows_of(group_at(k)), :]
        whole[...] = dot(act, wout[...])
        half_out[1, k] = whole[:, pl.ds(other, half)].astype(BF16)
        swap_of(1, k).start()
        half_own[k] = whole[:, pl.ds(mine, half)] + bias_half
    for k in range(GROUPS):
        swap_of(1, k).wait()
        pack(3, group_at(k), (half_own[k] + half_in[1, k].astype(F32)).astype(BF16), None)

    sg[...] = (gcol_s[...] * u_s[...].astype(F32)).astype(BF16)
    x_t[...] = jnp.transpose(x_s[...])
    hid_t[...] = jnp.transpose(hid[...])
    o_beo[...] = jnp.sum(sg[...].astype(F32), axis=0, keepdims=True)
    o_bei[...] = jnp.sum(gp[...].astype(F32), axis=0, keepdims=True)
    stores = []
    mix_t = jnp.transpose(mix[...])
    norm_forward()

    flat_id = iota((tp, z.slots), 1)
    back_one = [one(flat_id == f) for f in flat_col]
    for k in range(GROUPS):
        a2a_forward(2, k)
    for k in SEND_ORDER:
        a2a_send(3, k)
    tail_lane = iota((tp, per * 16), 1)
    number = [None, None]
    for k in range(GROUPS):
        g = group_at(k)
        a2a_take(2, k)
        assemble(2, g, y_s)
        tails = [tail_of(2, r_msg, g), tail_of(2, f_msg, g)]
        for c in range(2):
            at = r_col[c] * 16 + (gate_row - g * (per * 16))
            pick = one(sent_col[c] & ((tail_lane == at) | (tail_lane == at + 1)))
            piece = dot(pick, tails[0]) + dot(pick, tails[1])
            number[c] = piece if number[c] is None else number[c] + piece
    grad_gate = [
        jnp.sum(
            jnp.where(iota((tp, LANE), 1) == j_col[c], number[c], 0.0), axis=-1, keepdims=True
        )
        for c in range(2)
    ]
    mean_gate = gate[0] * grad_gate[0] + gate[1] * grad_gate[1]
    e_pad = up_to(z.experts, LANE)
    e_lane = iota((tp, e_pad), 1)
    grad_logits = jnp.where(
        e_lane == r_col[0], gate[0] * (grad_gate[0] - mean_gate), 0.0
    ) + jnp.where(e_lane == r_col[1], gate[1] * (grad_gate[1] - mean_gate), 0.0)
    gl_high, gl_low = split(grad_logits)
    router_pad = router_ref[...]
    if e_pad > z.experts:
        router_pad = jnp.concatenate(
            [router_pad, jnp.zeros((e_pad - z.experts, width), BF16)], axis=0
        )
    grad_n2 = (
        dot(back_one[0] + back_one[1], y_s[...])
        + dot(gl_high, router_pad)
        + dot(gl_low, router_pad)
    )
    grad_router = dot_at(gl_high, n2[0:tp, :]) + dot_at(gl_low, n2[0:tp, :])
    smallf[...] = jnp.zeros(smallf.shape, F32)
    ne = z.experts
    smallf[0:ne, :] = grad_router[0:ne, :]
    normal = normal2[...]
    smallf[ne + 2 : ne + 3, :] = jnp.sum(grad_n2 * normal, axis=0, keepdims=True)
    smallf[ne + 3 : ne + 4, :] = jnp.sum(grad_n2, axis=0, keepdims=True)
    gm[...] = upk[0:tp, :].astype(F32) + norm_backward(grad_n2, normal, inverse2, row_of(ln2g_ref))
    ag[tp:, :] = jnp.zeros((tk - tp, width), BF16)
    ag[0:tp, :] = gm[...].astype(BF16)
    smallf[ne + 4 : ne + 5, :] = jnp.sum(ag[...].astype(F32), axis=0, keepdims=True)

    halve, double, waiting = sum_plan(z.bits, z.pairs, z.cuts)
    waiting = list(waiting)
    n_main, n_cut = len(halve) - 1, len(double) - 1

    def walk(order):
        start, size, steps = 0, 1 << len(order), []
        for b in order:
            bit = lax.rem(me // b, 2)
            peer = me + b * (1 - 2 * bit)
            size = size // 2
            steps.append((peer, start + (1 - bit) * size, start + bit * size, size))
            start = start + bit * size
        return steps, start

    halving, doubling = [walk(order) for order in halve], [walk(order) for order in double]

    def sum_of(g):
        if g < 3:
            return sum_w.at[g], [r.at[g] for r in from_w], z.chunk, [g]
        if g < n_main:
            pieces = [3 + (g - 3) * z.cuts + i for i in range(z.cuts)]
            return sum_u.at[g - 3], [r.at[g - 3] for r in from_u], z.unit, pieces
        return sum_s, list(from_s), z.small, [n_cut]

    def piece_of(i):
        if i < 3:
            return red_w.at[i], z.chunk
        if i < n_cut:
            return red_u.at[i - 3], z.cut
        return red_s, z.small

    def region(ref, at, count, rows):
        return ref.at[pl.ds(pl.multiple_of(at * rows, 16), count * rows)]

    def rs_copy(g, s):
        src, bufs, rows, _ = sum_of(g)
        peer, give, _, size = halving[g][0][s]
        return remote(
            region(src, give, size, rows), bufs[s], cs.at[g], cr.at[g, s], (peer, core)
        )

    def rs_add(g, s, at, count):
        src, bufs, rows, _ = sum_of(g)
        keep = halving[g][0][s][2]

        def go(i, carry):
            here = pl.ds(pl.multiple_of((at + i) * rows, 16), rows)
            there = pl.ds(pl.multiple_of((at + i - keep) * rows, 16), rows)
            src[here, :] = (src[here, :].astype(F32) + bufs[s][there, :].astype(F32)).astype(BF16)
            return carry

        lax.fori_loop(0, count, go, 0, unroll=2 if count % 2 == 0 else 1)

    def rs_step(g, s):
        src, bufs, rows, pieces = sum_of(g)
        steps, last = halving[g]
        rs_copy(g, s).wait()
        if s + 1 < len(steps):
            _, give, keep, size = steps[s + 1]
            rs_add(g, s, give, size)
            rs_copy(g, s + 1).start()
            rs_add(g, s, keep, size)
            return
        first = 0
        for i in pieces:
            out, count = piece_of(i)
            here = pl.ds(pl.multiple_of(last * rows + first, 16), count)
            goal = pl.ds(pl.multiple_of(doubling[i][1] * count, 16), count)
            out[goal, :] = (
                src[here, :].astype(F32) + bufs[s][first : first + count, :].astype(F32)
            ).astype(BF16)
            ag_copy(i, nbits - 1).start()
            first += count

    def ag_copy(g, s):
        out, rows = piece_of(g)
        peer, _, keep, size = doubling[g][0][s]
        piece = region(out, keep, size, rows)
        return remote(piece, piece, as_.at[g], ar.at[g, s], (peer, core))

    def ag_step(g, s):
        out, rows = piece_of(g)
        peer, give, _, size = doubling[g][0][s]
        ag_copy(g, s).wait_send()
        piece = region(out, give, size, rows)
        remote(piece, piece, as_.at[g], ar.at[g, s], (peer, core)).wait_recv()
        if s > 0:
            ag_copy(g, s - 1).start()

    def share_of(p, m):
        return gpt.at[p, pl.ds(pl.multiple_of(m * z.share, 16), z.share)]

    def quad_send(p):
        here = lax.rem(me, QUAD)
        for q in range(1, QUAD):
            m = in_quad(q)
            remote(
                share_of(p, m), gq.at[p, here], us.at[p], ur.at[p], (me - here + m, core)
            ).start()
        gq[p, here] = gpt[p, pl.ds(pl.multiple_of(here * z.share, 16), z.share), :]

    def quad_step(p):
        block = gq.at[p, pl.ds(0, QUAD - 1)]
        remote(block, block, us.at[p], ur.at[p], sib).wait()
        left = jnp.concatenate([gq[p, m] for m in range(QUAD)], axis=1)
        row = 0
        for h in range(2):
            value = dot(left, n1q[:, h].reshape(QUAD * tk, half)).astype(BF16)
            for b in range(z.blocks):
                sum_u[p, row : row + z.share, :] = value[:, b * LANE : (b + 1) * LANE]
                row += z.share
        if z.unit_rows < n // QUAD * z.unit:
            sum_u[p, z.unit_rows :, :] = jnp.zeros((n // QUAD * z.unit - z.unit_rows, LANE), BF16)
        rs_copy(3 + p, 0).start()

    def advance(place):
        while waiting and waiting[0][0] <= place:
            _, g, s = waiting.pop(0)
            if s == 9:
                quad_step(g - 3)
            elif s >= 0:
                rs_step(g, s)
            else:
                ag_step(g, -1 - s)

    grad_wo = dot(mix_t, ag[...])
    each = z.chain_rows // hw
    for g in range(3):
        for i in range(each):
            b = g * each + i
            sum_w[g, i * hw : (i + 1) * hw, :] = grad_wo[:, b * LANE : (b + 1) * LANE].astype(BF16)
        if z.chain_rows < n * z.chunk:
            sum_w[g, z.chain_rows :, :] = jnp.zeros((n * z.chunk - z.chain_rows, LANE), BF16)
        rs_copy(g, 0).start()
    norm_take()
    advance(0)

    dm[...] = dot_bt(ag[0:tp, :], wo[...]).astype(BF16)
    dm_t[...] = dot_bt(wo[...], ag[...]).astype(BF16)
    ones = jnp.ones((8, tk), BF16)
    for p in range(z.pairs):
        lanes = slice(p * LANE, (p + 1) * LANE)
        vp, dp = v_s[:, lanes], dm[:, lanes]
        dq, dk, dv = [], [], []
        for h in range(2):
            rows = slice(h * HEAD, (h + 1) * HEAD)
            prob = probs[2 * p + h]
            gprob = dot_bt(dp * head_mask[h], vp)
            inner = jnp.sum(prob * gprob, axis=-1, keepdims=True)
            gs = (prob * (gprob - inner)).astype(BF16)
            dq.append(dot_bt(k_t[p, rows, :], gs))
            dk.append(dot(q_t[p, rows, 0:tp], gs))
            dv.append(
                dot(dm_t[p * LANE + h * HEAD : p * LANE + (h + 1) * HEAD, 0:tp], prob.astype(BF16))
            )
        for c, (pair, scale) in enumerate(((dq, score_scale), (dk, score_scale), (dv, 1.0))):
            value = (jnp.concatenate(pair, axis=0) * scale).astype(BF16)
            at = slice(c * LANE, (c + 1) * LANE)
            if c == 0:
                gpt[p, at, LANE:] = jnp.zeros((LANE, tk - LANE), BF16)
                gpt[p, at, 0:tp] = value
            else:
                gpt[p, at, :] = value
        quad_send(p)
        line = dot_bt(ones, gpt[p])
        smallf[ne + 5 : ne + 6, lanes] = line[0:1, 0:LANE]
        smallf[ne + 6 : ne + 7, lanes] = line[0:1, 2 * LANE : 3 * LANE]
        advance(1 + p)

    head_part = None
    for c in range(3):
        joined = jnp.concatenate(
            [gpt[p, c * LANE : (c + 1) * LANE, :] for p in range(z.pairs)], axis=0
        )
        piece = dot(wqkv[c], joined)
        head_part = piece if head_part is None else head_part + piece
    gn_out[...] = jnp.transpose(head_part.astype(BF16))[0:tp, :]
    swap = remote(gn_out, gn_in, hs.at[2, 1], hr.at[2, 1], sib)
    swap.start()
    swap.wait()
    grad_n1 = gn_out[...].astype(F32) + gn_in[...].astype(F32)
    normal = normal1[...]
    smallf[ne : ne + 1, :] = jnp.sum(grad_n1 * normal, axis=0, keepdims=True)
    smallf[ne + 1 : ne + 2, :] = jnp.sum(grad_n1, axis=0, keepdims=True)
    back = gm[...] + norm_backward(grad_n1, normal, inverse1, row_of(ln1g_ref))
    gtok_out[...] = back[0:tok, :]
    copy = pltpu.make_async_copy(gtok_out, o_gtok, osem.at[0])
    copy.start()
    stores.append(copy)
    used = z.small_rows * (width // LANE)
    for b in range(width // LANE):
        sum_s[b * z.small_rows : (b + 1) * z.small_rows, :] = smallf[
            :, b * LANE : (b + 1) * LANE
        ].astype(BF16)
    if used < n * z.small:
        sum_s[used:, :] = jnp.zeros((n * z.small - used, LANE), BF16)
    rs_copy(n_main, 0).start()
    advance(1 + z.pairs)

    for k in range(GROUPS):
        a2a_forward(3, k)
    for k in range(GROUPS):
        a2a_take(3, k)
        assemble(3, group_at(k), y_s)
    branch = gate[0] * dot(back_one[0], y_s[...]) + gate[1] * dot(back_one[1], y_s[...])
    output = mid[...] + branch
    tok_out[...] = output[0:tok, :].astype(BF16)
    copy = pltpu.make_async_copy(tok_out, o_tok, osem.at[1])
    copy.start()
    stores.append(copy)
    lane_id = iota((1, LANE), 1)
    x_all = xf[...]
    line = jnp.zeros((1, LANE), F32)
    for i, number in enumerate(
        (
            jnp.sum(keep_col * x_all * x_all),
            stat_attn,
            jnp.sum(keep_col * branch * branch),
            jnp.sum(keep_col * output * output),
            jnp.sum(keep_col),
        )
    ):
        line = jnp.where(lane_id == i, number, line)
    stat[me] = jnp.broadcast_to(line, (8, LANE))

    def stat_go(j, carry):
        p = lax.rem(me + j, n)
        remote(stat.at[me], stat.at[me], st.at[0], st.at[1], (p, core)).start()
        return carry

    lax.fori_loop(1, n, stat_go, 0)

    advance(LAST)
    block = stat.at[pl.ds(0, n - 1)]
    remote(block, block, st.at[0], st.at[1], sib).wait()
    totals = jnp.sum(stat[...], axis=0)
    count = jnp.sum(jnp.where(iota((8, LANE), 1) == 4, totals, 0.0), axis=-1, keepdims=True)
    o_rms[...] = jnp.sqrt(totals / (count * width))

    for b in range(width // LANE):
        o_small[:, b * LANE : (b + 1) * LANE] = red_s[
            b * z.small_rows : (b + 1) * z.small_rows, :
        ].astype(F32)
    for i in range(4):
        a2a_sent(i)
    for copy in stores:
        copy.wait()


def last_kernel(
    z,
    i_tok,
    i_gtok,
    x_t,
    sg,
    hid_t,
    gp,
    red_w,
    red_u,
    i_small,
    i_bei,
    i_beo,
    i_rms,
    o_tok,
    o_gtok,
    o_ln1g,
    o_ln1b,
    o_wqkv,
    o_bqv,
    o_wo,
    o_bo,
    o_ln2g,
    o_ln2b,
    o_router,
    o_win,
    o_bin,
    o_wout,
    o_bout,
    o_rms,
    wqkv,
    wo,
    win,
    wout,
    back_t,
    osem,
):
    ne, width, hw = z.experts, z.width, z.hw
    stores = []

    def store(src, dst, i):
        copy = pltpu.make_async_copy(src, dst, osem.at[i])
        copy.start()
        stores.append(copy)

    store(i_tok, o_tok, 0)
    store(i_gtok, o_gtok, 1)
    for ref, i in ((o_ln1g, 0), (o_ln1b, 1), (o_ln2g, 2), (o_ln2b, 3), (o_bo, 4)):
        ref[...] = i_small[ne + i : ne + i + 1, :].reshape(width)
    o_router[...] = i_small[0:ne, :]
    o_bqv[...] = i_small[ne + 5 : ne + 7, 0:hw]
    o_bin[...] = i_bei[...]
    o_bout[...] = i_beo[...]
    o_rms[...] = i_rms[0:1, 0:4].reshape(4)

    each = z.chain_rows // hw
    for b in range(width // LANE):
        rows = slice(b % each * hw, (b % each + 1) * hw)
        wo[:, b * LANE : (b + 1) * LANE] = red_w[b // each, rows, :].astype(F32)
    store(wo, o_wo, 2)
    tiles = z.ff // TILE
    for t in range(tiles):
        cols = slice(t * TILE, (t + 1) * TILE)
        win[:, cols] = dot(x_t[...], gp[:, cols])
        store(win.at[:, cols], o_win.at[0, :, cols], 4 + t)
    halve, double, _ = sum_plan(z.bits, z.pairs, z.cuts)
    nbits = len(z.bits)
    piece = math.gcd(z.cut, z.share)
    for p in range(z.pairs):
        for i in range(z.cuts * z.n):
            i, c = divmod(i, z.n)
            order = double[3 + p * z.cuts + i]
            device = sum(b for k, b in enumerate(order) if c >> (nbits - 1 - k) & 1)
            q = 0
            for b in halve[3 + p]:
                q = 2 * q + (device // b) % 2
            for t in range(0, z.cut, piece):
                row = q * z.unit + i * z.cut + t
                if row < z.unit_rows:
                    b, j = divmod(row, z.share)
                    goal = device % QUAD * z.share + j
                    back_t[goal : goal + piece, b * LANE : (b + 1) * LANE] = red_u[
                        p * z.cuts + i, c * z.cut + t : c * z.cut + t + piece, :
                    ]
        for c in range(3):
            value = jnp.transpose(back_t[c * LANE : (c + 1) * LANE, :])
            wqkv[c, :, p * LANE : (p + 1) * LANE] = value.astype(F32)
    store(wqkv, o_wqkv, 3)
    for t in range(tiles):
        rows = slice(t * TILE, (t + 1) * TILE)
        wout[rows, :] = dot(hid_t[rows, :], sg[...])
        store(wout.at[rows, :], o_wout.at[0, rows, :], 4 + tiles + t)
    for copy in stores:
        copy.wait()


def per_device(
    tokens,
    grad_out,
    valid_mask,
    routes,
    slot_index,
    ln1_gain,
    ln1_bias,
    w_qkv,
    bias_qv,
    w_attn_out,
    b_attn_out,
    ln2_gain,
    ln2_bias,
    router,
    w_expert_in,
    b_expert_in,
    w_expert_out,
    b_expert_out,
):
    tok, width = tokens.shape
    hw = w_qkv.shape[2]
    ff = w_expert_in.shape[2]
    z = Sizes(lax.axis_size("dp"), tok, width, hw, ff, router.shape[1])
    n, tp, tk = z.n, z.tp, z.tk
    nbits = len(z.bits)
    vmem = pl.BlockSpec(memory_space=pltpu.VMEM)
    any_ = pl.BlockSpec(memory_space=pl.ANY)
    shape = jax.ShapeDtypeStruct
    groups = 4 + z.pairs
    pieces = 4 + z.pairs * z.cuts
    kept = pltpu.VMEM if n <= 16 else shape
    keep = lambda a: pltpu.with_memory_space_constraint(a, pltpu.VMEM) if n <= 16 else a
    V = pltpu.VMEM
    scratch = [
        V((tok, width), BF16),
        V((tok, width), BF16),
        V((1, tok), jnp.int32),
        V((2, tok), jnp.int32),
        V((2, tok), jnp.int32),
        V((width,), F32),
        V((width,), F32),
        V((2, hw), F32),
        V((width,), F32),
        V((width,), F32),
        V((width,), F32),
        V((z.experts, width), BF16),
        V((1, ff), F32),
        V((1, width), F32),
        V((tok, width), BF16),
        V((tok, width), F32),
        V((3, width, hw), BF16),
        V((hw, width), BF16),
        V((width, ff), BF16),
        V((ff, width), BF16),
        V((tp, width), F32),
        V((tp, width), F32),
        V((tk, width), BF16),
        V((QUAD, 2, tk, z.half), BF16),
        V((z.pairs, LANE, tk), BF16),
        V((z.pairs, LANE, tk), BF16),
        V((hw, tk), BF16),
        V((z.pairs, 3 * LANE, tk), BF16),
        V((z.pairs, QUAD, z.share, tk), BF16),
        V((tk, width), BF16),
        V((tk, hw), BF16),
        V((tk, hw), BF16),
        V((tk, hw), BF16),
        V((2 * z.pairs, tp, tk), F32),
        V((tk, hw), BF16),
        V((tp, width), F32),
        V((tp, width), F32),
        V((tp, width), F32),
        V((tp, width), F32),
        V((tk, width), BF16),
        V((z.slots, tk), BF16),
        V((8, tk), F32),
        V((tk, 8), F32),
        V((z.slots, width), BF16),
        V((z.slots, width), BF16),
        V((z.slots, width), BF16),
        V((z.slots, ff), F32),
        V((z.rows, ff), F32),
        V((z.slots, ff), BF16),
        V((z.slots, 1), F32),
        V((z.slots, LANE), F32),
        V((2, GROUPS, z.rows, z.half), BF16),
        V((2, GROUPS, z.rows, z.half), BF16),
        V((GROUPS, z.rows, z.half), F32),
        V((z.rows, width), F32),
        V((ff, width), BF16),
        V((width, ff), BF16),
        V((tp, width), F32),
        V((tk, width), BF16),
        V((tp, hw), BF16),
        V((tp, width), BF16),
        V((tp, width), BF16),
        V((z.small_rows, width), F32),
        V((n, 8, LANE), F32),
        V((4, n, z.msg, LANE), BF16),
        V((4, n, z.msg, LANE), BF16),
        V((4, n, z.msg, LANE), BF16),
        V((3, n * z.chunk, LANE), BF16),
        V((z.pairs, n // QUAD * z.unit, LANE), BF16),
        V((n * z.small, LANE), BF16),
    ]
    scratch += [V((3, (n >> (s + 1)) * z.chunk, LANE), BF16) for s in range(nbits)]
    scratch += [V(((n >> (s + 1)) * z.small, LANE), BF16) for s in range(nbits)]
    scratch += [
        V((z.pairs, (n // QUAD >> (s + 1)) * z.unit, LANE), BF16) for s in range(nbits - 2)
    ]
    scratch += [
        V((n * z.small, LANE), BF16),
        DMA((18,)),
        DMA((2,)),
        DMA((3, GROUPS)),
        DMA((3, GROUPS)),
        DMA((4,)),
        DMA((4, GROUPS)),
        DMA((4,)),
        DMA((4, GROUPS)),
        DMA((groups,)),
        DMA((groups, nbits)),
        DMA((pieces,)),
        DMA((pieces, nbits)),
        DMA((2,)),
        DMA((4,)),
        DMA((z.pairs,)),
        DMA((z.pairs,)),
    ]
    row = lambda v: v.reshape(1, -1)
    outs = pl.pallas_call(
        functools.partial(mega_kernel, z),
        out_shape=(
            kept((tok, width), BF16),
            kept((tok, width), F32),
            kept((width, z.slots), BF16),
            kept((z.slots, width), BF16),
            kept((ff, z.slots), BF16),
            kept((z.slots, ff), BF16),
            kept((3, n * z.chunk, LANE), BF16),
            kept((z.pairs * z.cuts, n * z.cut, LANE), BF16),
            kept((z.small_rows, width), F32),
            kept((1, ff), F32),
            kept((1, width), F32),
            kept((8, LANE), F32),
        ),
        in_specs=[any_] * 18,
        out_specs=(any_,) * 2 + (vmem,) * 10,
        scratch_shapes=scratch,
        compiler_params=pltpu.CompilerParams(
            collective_id=0,
            has_side_effects=True,
            vmem_limit_bytes=(54 if n <= 16 else 61) * 2**20,
        ),
    )(*(
        pltpu.with_memory_space_constraint(a, pltpu.HBM)
        for a in (
        tokens,
        grad_out,
        row(valid_mask),
        routes.T,
        slot_index.T,
        ln1_gain,
        ln1_bias,
        jnp.transpose(w_qkv, (1, 0, 2)),
        bias_qv,
        w_attn_out,
        b_attn_out,
        ln2_gain,
        ln2_bias,
        router.T,
        w_expert_in[0],
        b_expert_in,
        w_expert_out[0],
        b_expert_out,
        )
    ))
    ne = z.experts
    vec = shape((width,), F32)
    last = pl.pallas_call(
        functools.partial(last_kernel, z),
        out_shape=(
            shape((tok, width), BF16),
            shape((tok, width), F32),
            vec,
            vec,
            shape((3, width, hw), F32),
            shape((2, hw), F32),
            shape((hw, width), F32),
            vec,
            vec,
            vec,
            shape((ne, width), F32),
            shape((1, width, ff), F32),
            shape((1, ff), F32),
            shape((1, ff, width), F32),
            shape((1, width), F32),
            shape((4,), F32),
        ),
        in_specs=[any_] * 2 + [vmem] * 10,
        out_specs=(
            [any_] * 2
            + [vmem] * 2
            + [any_, vmem, any_]
            + [vmem] * 4
            + [any_, vmem, any_, vmem, vmem]
        ),
        scratch_shapes=[
            V((3, width, hw), F32),
            V((hw, width), F32),
            V((width, ff), F32),
            V((ff, width), F32),
            V((3 * LANE, width), BF16),
            DMA((4 + 2 * (ff // TILE),)),
        ],
        compiler_params=pltpu.CompilerParams(vmem_limit_bytes=(30 if n <= 16 else 48) * 2**20),
    )(*(keep(a) for a in outs))
    return (
        last[0],
        last[1],
        last[2],
        last[3],
        jnp.transpose(last[4], (1, 0, 2)),
        *last[5:10],
        last[10].T,
        *last[11:],
    )


def solution(mesh):
    return jax.shard_map(
        per_device,
        mesh=mesh,
        in_specs=(
            P("dp", None),
            P("dp", None),
            P("dp"),
            P("dp", None),
            P("dp", None),
            P(),
            P(),
            P(None, None, "tensor"),
            P(None, "tensor"),
            P("tensor", None),
            P(),
            P(),
            P(),
            P(),
            P("dp", None, "tensor"),
            P("dp", "tensor"),
            P("dp", "tensor", None),
            P("dp", None),
        ),
        out_specs=(
            P("dp", None),
            P("dp", None),
            P(),
            P(),
            P(None, None, "tensor"),
            P(None, "tensor"),
            P("tensor", None),
            P(),
            P(),
            P(),
            P(),
            P("dp", None, "tensor"),
            P("dp", "tensor"),
            P("dp", "tensor", None),
            P("dp", None),
            P(),
        ),
        check_vma=False,
    )
```

```python
import functools
import math

import jax
import jax.numpy as jnp
from jax import lax
from jax.experimental import pallas as pl
from jax.experimental.pallas import tpu as pltpu
from jax.sharding import PartitionSpec as P

HEAD = 64
SEQ = 197
LANE = 128
EPS = 1e-06
ROOT = math.sqrt(2.0 / math.pi)
CUBE = 0.044715
GROUPS = 4
QUAD = 4
LAST = 5
CHAINS = (
    (2, 0, 1, 3),
    (2, 0, 1, 3),
    (3, 1, 0, 2),
)
UNITS = (
    (3, 2),
    (2, 3),
    (3, 2),
)
PIECES = (
    (0, 1, 2, 3),
    (1, 2, 0, 3),
    (2, 0, 3, 1),
    (1, 2, 0, 3),
    (0, 1, 3, 2),
    (1, 3, 0, 2),
    (0, 1, 2, 3),
    (1, 3, 0, 2),
    (0, 2, 3, 1),
)
STEPS = (
    (4, 3, 9), (5, 4, 9), (5, 5, 9), (5, 0, 0), (5, 1, 0), (5, 2, 0), (5, 6, 0), (5, 3, 0),
    (5, 4, 0), (5, 0, 1), (5, 6, 1), (5, 1, 1), (5, 2, 1), (5, 5, 0), (5, 3, 1), (5, 6, 2),
    (5, 0, 2), (5, 4, 1), (5, 1, 2), (5, 2, 2), (5, 5, -4), (5, 3, -4), (5, 4, -4), (5, 6, 3),
    (5, 5, 1), (5, 0, 3), (5, 7, -4), (5, 8, -4), (5, 6, -4), (5, 1, 3), (5, 2, 3), (5, 4, -3),
    (5, 12, -4), (5, 11, -4), (5, 10, -4), (5, 9, -4), (5, 5, -3), (5, 3, -3), (5, 0, -4),
    (5, 8, -3), (5, 6, -3), (5, 1, -4), (5, 12, -3), (5, 2, -4), (5, 10, -3), (5, 7, -3),
    (5, 5, -2), (5, 11, -3), (5, 0, -3), (5, 3, -2), (5, 9, -3), (5, 2, -3), (5, 12, -2),
    (5, 1, -3), (5, 4, -2), (5, 7, -2), (5, 9, -2), (5, 8, -2), (5, 6, -2), (5, 0, -2),
    (5, 2, -2), (5, 10, -2), (5, 11, -2), (5, 12, -1), (5, 5, -1), (5, 1, -2), (5, 4, -1),
    (5, 3, -1), (5, 0, -1), (5, 2, -1), (5, 7, -1), (5, 8, -1), (5, 6, -1), (5, 9, -1),
    (5, 10, -1), (5, 1, -1), (5, 11, -1),
)
SEND_ORDER = (0, 2, 1, 3)
TILE = 256
MESH = pl.DeviceIdType.MESH
F32 = jnp.float32
BF16 = jnp.bfloat16
DMA = pltpu.SemaphoreType.DMA


def up_to(value, step):
    return -(-value // step) * step


def dot(a, b):
    return lax.dot_general(a, b, (((1,), (0,)), ((), ())), preferred_element_type=F32)


def dot_bt(a, b):
    return lax.dot_general(a, b, (((1,), (1,)), ((), ())), preferred_element_type=F32)


def dot_at(a, b):
    return lax.dot_general(a, b, (((0,), (0,)), ((), ())), preferred_element_type=F32)


def row_of(ref):
    return ref[...].reshape(1, ref.shape[0])


def iota(shape, dim):
    return lax.broadcasted_iota(jnp.int32, shape, dim)


def one(cond, kind=BF16):
    return jnp.where(cond, 1.0, 0.0).astype(kind)


def split(value):
    high = value.astype(BF16)
    return high, (value - high.astype(F32)).astype(BF16)


def norm_parts(values):
    scale = 1.0 / values.shape[-1]
    center = values - jnp.sum(values, axis=-1, keepdims=True) * scale
    inverse = lax.rsqrt(jnp.sum(center * center, axis=-1, keepdims=True) * scale + EPS)
    return center * inverse, inverse


def norm_backward(incoming, normal, inverse, gain_vec):
    scale = 1.0 / incoming.shape[-1]
    scaled = incoming * gain_vec
    return inverse * (
        scaled
        - jnp.sum(scaled, axis=-1, keepdims=True) * scale
        - normal * (jnp.sum(scaled * normal, axis=-1, keepdims=True) * scale)
    )


def remote(src, dst, send_sem, recv_sem, device):
    return pltpu.make_async_remote_copy(
        src_ref=src,
        dst_ref=dst,
        send_sem=send_sem,
        recv_sem=recv_sem,
        device_id=device,
        device_id_type=MESH,
    )


class Sizes:
    def __init__(self, n, tok, width, heads_width, ff, experts):
        self.n = n
        self.tok = tok
        self.tp = up_to(tok, 16)
        self.tk = up_to(tok, LANE)
        self.width = width
        self.hw = heads_width
        self.pairs = heads_width // LANE
        self.ff = ff
        self.experts = experts
        self.cap = 2 * (3 * tok // (2 * n))
        self.main = self.cap // 16 * 16
        self.tail = self.cap - self.main
        self.half = width // 2
        self.blocks = self.half // LANE
        self.msg = self.main * self.blocks + 16
        self.per = n // GROUPS
        self.gm = self.per * self.main
        self.gt = self.per * self.tail
        self.rows = self.per * self.cap
        self.slots = n * self.cap
        self.bits = [1 << i for i in range(n.bit_length() - 1)]
        self.chain_rows = heads_width * width // LANE // 3
        self.chunk = up_to(up_to(self.chain_rows, n) // n, 16)
        self.share = 3 * LANE // QUAD
        self.unit_rows = self.share * width // LANE
        self.unit = up_to(up_to(self.unit_rows, n // QUAD) // (n // QUAD), 16)
        self.cuts = 3 if self.unit % 48 == 0 else 1
        self.cut = self.unit // self.cuts
        self.small_rows = up_to(experts + 7, 16)
        self.small = up_to(up_to(self.small_rows * width // LANE, n) // n, 16)
        fits = 0 < self.tail * self.blocks <= 14 and self.gt % 16 == 0
        fits = fits and self.chain_rows % heads_width == 0 and len(self.bits) > 2
        if not fits or experts != n or (1 << len(self.bits)) != n:
            raise ValueError("unsupported sizes")


def sum_plan(bits, pairs, cuts):
    if len(bits) == 4 and pairs == 3 and cuts == 3:
        take = lambda orders: [[bits[i] for i in order] for order in orders]
        halve = take(CHAINS) + take(UNITS) + [bits]
        return halve, take(CHAINS) + take(PIECES) + [bits], STEPS
    rolled = [bits[i:3] + bits[:i] + bits[3:] for i in range(3)]
    halve = rolled + [bits[2:]] * pairs + [bits]
    double = rolled + [rolled[i % 3] for i in range(pairs * cuts)] + [bits]
    steps = [(LAST, 3 + p, 9) for p in range(pairs)]
    for s in range(len(bits)):
        steps += [(LAST, g, s) for g, order in enumerate(halve) if s < len(order)]
    for s in range(len(bits) - 1, -1, -1):
        steps += [(LAST, g, -1 - s) for g in range(len(double))]
    return halve, double, steps


def mega_kernel(
    z,
    tokens_hbm,
    grad_out_hbm,
    valid_hbm,
    routes_hbm,
    slots_hbm,
    ln1g_hbm,
    ln1b_hbm,
    wqkv_hbm,
    bqv_hbm,
    wo_hbm,
    bo_hbm,
    ln2g_hbm,
    ln2b_hbm,
    router_hbm,
    win_hbm,
    bin_hbm,
    wout_hbm,
    bout_hbm,
    o_tok,
    o_gtok,
    x_t,
    sg,
    hid_t,
    gp,
    red_w,
    red_u,
    o_small,
    o_bei,
    o_beo,
    o_rms,
    tokens_ref,
    grad_out_ref,
    valid_ref,
    routes_ref,
    slots_ref,
    ln1g_ref,
    ln1b_ref,
    bqv_ref,
    bo_ref,
    ln2g_ref,
    ln2b_ref,
    router_ref,
    bin_ref,
    bout_ref,
    tok_out,
    gtok_out,
    wqkv,
    wo,
    win,
    wout,
    xf,
    normal1,
    n1,
    n1q,
    q_t,
    k_t,
    dm_t,
    gpt,
    gq,
    upk,
    q_s,
    k_s,
    v_s,
    probs,
    mix,
    part,
    part_in,
    mid,
    normal2,
    n2,
    onehot,
    rows8,
    cols8,
    u_s,
    x_s,
    y_s,
    gh,
    pre,
    hid,
    gcol_s,
    ggv,
    half_out,
    half_in,
    half_own,
    whole,
    win_t,
    wout_t,
    gm,
    ag,
    dm,
    gn_out,
    gn_in,
    smallf,
    stat,
    s_msg,
    r_msg,
    f_msg,
    sum_w,
    sum_u,
    sum_s,
    *rest,
):
    nbits = len(z.bits)
    from_w = rest[:nbits]
    from_s = rest[nbits : 2 * nbits]
    from_u = rest[2 * nbits : 3 * nbits - 2]
    red_s, wsem, osem, hs, hr, ss, rs, fs, fr, cs, cr, as_, ar, st, qs, us, ur = rest[
        3 * nbits - 2 :
    ]
    n = z.n
    me, core = lax.axis_index("dp"), lax.axis_index("tensor")
    sib = (me, 1 - core)
    tok, tp, tk, width, hw, half = z.tok, z.tp, z.tk, z.width, z.hw, z.half
    mine = pl.multiple_of(core * half, LANE)
    other = pl.multiple_of((1 - core) * half, LANE)

    barrier = pltpu.get_barrier_semaphore()

    def greet(j, carry):
        pl.semaphore_signal(
            barrier, inc=1, device_id=(lax.rem(me + j, n), core), device_id_type=MESH
        )
        return carry

    lax.fori_loop(1, n, greet, 0)
    pl.semaphore_signal(barrier, inc=1, device_id=sib, device_id_type=MESH)

    tokens_in = [
        pltpu.make_async_copy(a, b, wsem.at[4 + i])
        for i, (a, b) in enumerate(((tokens_hbm, tokens_ref), (grad_out_hbm, grad_out_ref)))
    ]
    small_in = [
        pltpu.make_async_copy(a, b, wsem.at[6 + i])
        for i, (a, b) in enumerate(
            (
                (valid_hbm, valid_ref),
                (routes_hbm, routes_ref),
                (slots_hbm, slots_ref),
                (ln1g_hbm, ln1g_ref),
                (ln1b_hbm, ln1b_ref),
                (bqv_hbm, bqv_ref),
                (bo_hbm, bo_ref),
                (ln2g_hbm, ln2g_ref),
                (ln2b_hbm, ln2b_ref),
                (router_hbm, router_ref),
                (bin_hbm, bin_ref),
                (bout_hbm, bout_ref),
            )
        )
    ]
    for copy in small_in + tokens_in[::-1]:
        copy.start()
    weights = [
        pltpu.make_async_copy(a, b, wsem.at[i])
        for i, (a, b) in enumerate(
            ((wqkv_hbm, wqkv), (wo_hbm, wo), (wout_hbm, wout), (win_hbm, win))
        )
    ]
    for copy in weights:
        copy.start()

    per = z.per
    own = me // per
    own_bits = [lax.rem(own, 2), own // 2]

    def group_at(k):
        turned = [b + t * (1 - 2 * b) for b, t in zip(own_bits, (k % 2, k // 2))]
        return turned[0] + 2 * turned[1]

    def members(ref, i, g):
        return ref.at[i, pl.ds(g * per, per)]

    def rows_of(g, first=0, count=None):
        return pl.ds(pl.multiple_of(g * z.rows + first, 16), z.rows if count is None else count)

    def a2a_send(i, k):
        g = group_at(k)
        if k == 0:
            pltpu.make_async_copy(s_msg.at[i, me], r_msg.at[i, me], rs.at[i, own]).start()

        def go(m, carry):
            p = g * per + lax.rem(me + m, per)
            remote(s_msg.at[i, p], r_msg.at[i, me], ss.at[i], rs.at[i, own], (p, core)).start()
            return carry

        lax.fori_loop(1 if k == 0 else 0, per, go, 0)

    def a2a_forward(i, k):
        g = group_at(k)
        block = members(r_msg, i, g)
        remote(block, block, ss.at[i], rs.at[i, g], sib).wait_recv()
        remote(block, members(f_msg, i, g), fs.at[i], fr.at[i, g], sib).start()

    def a2a_take(i, k):
        block = members(f_msg, i, group_at(k))
        remote(block, block, fs.at[i], fr.at[i, group_at(k)], sib).wait_recv()

    def a2a_sent(i):
        block = s_msg.at[i, pl.ds(0, n - 1)]
        remote(block, block, ss.at[i], rs.at[i, 0], sib).wait_send()
        remote(r_msg.at[i], f_msg.at[i], fs.at[i], fr.at[i, 0], sib).wait_send()

    def tail_of(i, src, g):
        rows = src[i, pl.ds(g * per, per), z.msg - 16 : z.msg, :]
        return rows.reshape(per * 16, LANE)

    def assemble(i, g, out):
        q, r = iota((z.gt, per * 16), 0), iota((z.gt, per * 16), 1)
        base = q // z.tail * 16 + q % z.tail
        for src, at in ((r_msg, mine), (f_msg, other)):
            tail = tail_of(i, src, g)
            for b in range(z.blocks):
                lanes = pl.ds(pl.multiple_of(at + b * LANE, LANE), LANE)
                if z.main:
                    rows = src[i, pl.ds(g * per, per), b * z.main : (b + 1) * z.main, :]
                    out[rows_of(g, 0, z.gm), lanes] = rows.reshape(z.gm, LANE)
                pick = one(r == base + b * z.tail)
                out[rows_of(g, z.gm, z.gt), lanes] = dot(pick, tail).astype(BF16)

    def pack(i, g, value, tail):
        q, r = iota((per * 16, z.gt), 1), iota((per * 16, z.gt), 0)
        base = q // z.tail * 16 + q % z.tail
        for b in range(z.blocks):
            lanes = slice(b * LANE, (b + 1) * LANE)
            if z.main:
                s_msg[i, pl.ds(g * per, per), b * z.main : (b + 1) * z.main, :] = value[
                    0 : z.gm, lanes
                ].reshape(per, z.main, LANE)
            piece = dot(one(r == base + b * z.tail), value[z.gm : z.rows, lanes])
            tail = piece if tail is None else tail + piece
        s_msg[i, pl.ds(g * per, per), z.msg - 16 : z.msg, :] = tail.astype(BF16).reshape(
            per, 16, LANE
        )

    quad_bits = [lax.rem(me, 2), lax.rem(me // 2, 2)]

    def in_quad(q):
        turned = [b + t * (1 - 2 * b) for b, t in zip(quad_bits, (q % 2, q // 2))]
        return turned[0] + 2 * turned[1]

    def norm_send():
        for q in range(1, QUAD):
            piece = n1q.at[lax.rem(me, QUAD), core, pl.ds(0, tp)]
            peer = me - lax.rem(me, QUAD) + in_quad(q)
            remote(piece, piece, qs.at[0], qs.at[1], (peer, core)).start()

    def norm_forward():
        block = n1q.at[pl.ds(0, QUAD - 1), 0, pl.ds(0, tp)]
        remote(block, block, qs.at[0], qs.at[1], sib).wait()
        for q in range(1, QUAD):
            piece = n1q.at[in_quad(q), core, pl.ds(0, tp)]
            remote(piece, piece, qs.at[2], qs.at[3], sib).start()

    def norm_take():
        block = n1q.at[pl.ds(0, QUAD - 1), 0, pl.ds(0, tp)]
        remote(block, block, qs.at[2], qs.at[3], sib).wait()

    gate_row = 14

    for copy in small_in:
        copy.wait()
    rows8[...] = jnp.full(rows8.shape, -1.0, F32)
    rows8[0:2, 0:tok] = routes_ref[...].astype(F32)
    rows8[2:4, 0:tok] = slots_ref[...].astype(F32)
    rows8[4:5, 0:tok] = valid_ref[...].astype(F32)
    table = rows8[...]
    r_row = [table[k : k + 1, :].astype(jnp.int32) for k in range(2)]
    j_row = [table[2 + k : 3 + k, :].astype(jnp.int32) for k in range(2)]
    keep_row = table[4:5, :] > 0.5

    def targets(r, j):
        sent = (r >= 0) & (j < z.cap)
        g = r // per
        m = r - g * per
        flat = jnp.where(j < z.main, m * z.main + j, z.gm + m * z.tail + (j - z.main))
        return sent, jnp.where(sent, g * z.rows + flat, -1)

    sent_row, flat_row = zip(*[targets(r, j) for r, j in zip(r_row, j_row)])
    cols8[...] = jnp.transpose(table)
    r_col = [cols8[0:tp, k : k + 1].astype(jnp.int32) for k in range(2)]
    j_col = [cols8[0:tp, 2 + k : 3 + k].astype(jnp.int32) for k in range(2)]
    keep_col = jnp.where(cols8[0:tp, 4:5] > 0.5, 1.0, 0.0)
    sent_col, flat_col = zip(*[targets(r, j) for r, j in zip(r_col, j_col)])

    slot_id = iota((z.slots, tk), 0)
    onehot[...] = one((slot_id == flat_row[0]) | (slot_id == flat_row[1]))
    tail_id = iota((per * 16, tk), 0)
    tail_row = [
        jnp.where(s & (j >= z.main), r * 16 + (j - z.main), -1000)
        for s, r, j in zip(sent_row, r_row, j_row)
    ]

    def place(src, i, g, tail):
        first = g * (per * 16)
        for b in range(z.blocks):
            lanes = pl.ds(pl.multiple_of(mine + b * LANE, LANE), LANE)
            rows = src[:, lanes]
            if z.main:
                main = dot(onehot[rows_of(g, 0, z.gm), :], rows).astype(BF16)
                s_msg[i, pl.ds(g * per, per), b * z.main : (b + 1) * z.main, :] = main.reshape(
                    per, z.main, LANE
                )
            at = b * z.tail - first
            put = one((tail_id == tail_row[0] + at) | (tail_id == tail_row[1] + at))
            piece = dot(put, rows)
            tail = piece if tail is None else tail + piece
        s_msg[i, pl.ds(g * per, per), z.msg - 16 : z.msg, :] = tail.astype(BF16).reshape(
            per, 16, LANE
        )

    upk[tok // 16 * 16 :, :] = jnp.zeros((tk - tok // 16 * 16, width), BF16)
    tokens_in[1].wait()
    upk[0:tok, :] = grad_out_ref[...]
    for g in range(GROUPS):
        place(upk, 0, g, None)

    xf[tok // 8 * 8 :, :] = jnp.zeros((tp - tok // 8 * 8, width), F32)
    tokens_in[0].wait()
    xf[0:tok, :] = tokens_ref[...].astype(F32)
    normal, inverse1 = norm_parts(xf[...])
    normal1[...] = normal
    n1[tp:, :] = jnp.zeros((tk - tp, width), BF16)
    n1[0:tp, :] = (normal * row_of(ln1g_ref) + row_of(ln1b_ref)).astype(BF16)
    place_in = lax.rem(me, QUAD)
    for h in range(2):
        n1q[place_in, h] = n1[:, h * half : (h + 1) * half]
        for m in range(QUAD):
            n1q[m, h, tp:, :] = jnp.zeros((tk - tp, half), BF16)

    pl.semaphore_wait(barrier, n)
    for k in SEND_ORDER:
        a2a_send(0, k)

    weights[0].wait()
    for c, (dst, bias) in enumerate(((q_s, bqv_ref[0:1, :]), (k_s, None), (v_s, bqv_ref[1:2, :]))):
        value = dot(n1[0:tp, :], wqkv[c])
        if bias is not None:
            value = value + bias
        dst[tp:, :] = jnp.zeros((tk - tp, hw), BF16)
        dst[0:tp, :] = value.astype(BF16)

    score_scale = 1.0 / math.sqrt(HEAD)
    low_lane = iota((1, LANE), 1) < HEAD
    head_mask = [one(low_lane), one(jnp.logical_not(low_lane))]
    for p in range(z.pairs):
        lanes = slice(p * LANE, (p + 1) * LANE)
        qp, kp, vp = q_s[0:tp, lanes], k_s[:, lanes], v_s[:, lanes]
        outs = []
        for h in range(2):
            scores = dot_bt(qp * head_mask[h], kp) * score_scale
            scores = jnp.where(keep_row, scores, -1000000000.0)
            weights_h = jnp.exp(scores - jnp.max(scores, axis=-1, keepdims=True))
            prob = weights_h / jnp.sum(weights_h, axis=-1, keepdims=True)
            probs[2 * p + h] = prob
            outs.append(dot(prob.astype(BF16), vp))
        mix[0:tp, lanes] = jnp.where(low_lane, outs[0], outs[1]).astype(BF16)
    mix[tp:, :] = jnp.zeros((tk - tp, hw), BF16)
    weights[1].wait()
    part[...] = dot(mix[0:tp, :], wo[...])
    swap = remote(part, part_in, hs.at[2, 0], hr.at[2, 0], sib)
    swap.start()
    for p in range(z.pairs):
        lanes = slice(p * LANE, (p + 1) * LANE)
        q_t[p] = jnp.transpose(q_s[:, lanes])
        k_t[p] = jnp.transpose(k_s[:, lanes])
    swap.wait()

    strips = [slice(r, r + 16) for r in range(0, tp, 16)]
    n2[tp:, :] = jnp.zeros((tk - tp, width), BF16)
    inverses, squares = [], jnp.zeros((16, width), F32)
    for strip in strips:
        attention = part[strip, :] + part_in[strip, :] + row_of(bo_ref)
        squares = squares + keep_col[strip, :] * attention * attention
        middle = xf[strip, :] + attention
        mid[strip, :] = middle
        normal, inverse = norm_parts(middle)
        inverses.append(inverse)
        normal2[strip, :] = normal
        n2[strip, :] = (normal * row_of(ln2g_ref) + row_of(ln2b_ref)).astype(BF16)
    stat_attn = jnp.sum(squares)
    logits = dot_bt(router_ref[...], n2[...])
    expert_id = iota((z.experts, tk), 0)
    chosen = [
        jnp.sum(jnp.where(expert_id == r, logits, 0.0), axis=0, keepdims=True) for r in r_row
    ]
    top = jnp.maximum(chosen[0], chosen[1])
    raw = [jnp.exp(c - top) for c in chosen]
    total = raw[0] + raw[1]
    gate_rows = [r / total for r in raw]
    cols8[0:tk, :] = jnp.transpose(
        jnp.concatenate(gate_rows + [jnp.zeros((6, tk), F32)], axis=0)
    )
    gate = [cols8[0:tp, k : k + 1] for k in range(2)]

    slot_lane = iota((tk, LANE), 1)
    pad_col = [
        jnp.concatenate([j, jnp.full((tk - tp, 1), -1, jnp.int32)], axis=0) for j in j_col
    ]
    at_slot = [one(slot_lane == j) for j in pad_col]
    halves = [split(g) for g in gate_rows]
    for k in SEND_ORDER:
        g = group_at(k)
        number = None
        for c in range(2):
            high, low = halves[c]
            at = r_row[c] * 16 + (gate_row - g * (per * 16))
            lift = jnp.where(
                sent_row[c] & (tail_id == at), high.astype(F32), 0.0
            ) + jnp.where(sent_row[c] & (tail_id == at + 1), low.astype(F32), 0.0)
            piece = dot(lift.astype(BF16), at_slot[c])
            number = piece if number is None else number + piece
        place(n2, 1, g, number)
        if k < GROUPS - 1:
            a2a_send(1, k)

    def upstream(k):
        g = group_at(k)
        a2a_take(0, k)
        assemble(0, g, u_s)
        gh[rows_of(g), :] = dot(u_s[rows_of(g), :], wout_t[...])

    weights[2].wait()
    wout_t[...] = jnp.transpose(wout[...])
    a2a_forward(0, 0)
    a2a_forward(0, 1)
    weights[3].wait()
    win_t[...] = jnp.transpose(win[...])
    upstream(0)
    upstream(1)
    a2a_forward(0, 2)
    a2a_forward(0, 3)
    a2a_send(1, 3)
    norm_send()
    a2a_forward(1, 0)
    upstream(2)
    upstream(3)

    parts = [(0, z.gm, z.main, 0)] if z.main else []
    parts += [(z.gm, z.gt, z.tail, z.main)]
    step = 16

    def activate(g):
        def go(i, carry):
            here = pl.ds(pl.multiple_of(i * step, step), step)
            rows = pl.ds(pl.multiple_of(g * z.rows + i * step, step), step)
            gate_of = jnp.broadcast_to(gcol_s[rows, :], (step, LANE))
            total = jnp.zeros((step, LANE), F32)
            for b in range(z.ff // LANE):
                lanes = slice(b * LANE, (b + 1) * LANE)
                v = pre[here, lanes] + bin_ref[:, lanes]
                v2 = v * v
                s = 0.5 + 0.5 * jnp.tanh(v * (ROOT + (ROOT * CUBE) * v2))
                act = v * s
                back = s + act * (1.0 - s) * (2.0 * ROOT + (6.0 * ROOT * CUBE) * v2)
                up = gh[rows, lanes]
                hid[rows, lanes] = act.astype(BF16)
                gp[rows, lanes] = (gate_of * up * back).astype(BF16)
                total = total + up * act
            ggv[rows, :] = total
            return carry

        count = z.rows // step
        lax.fori_loop(0, count, go, 0, unroll=3 if count % 3 == 0 else 2)

    bias_half = bout_ref[:, pl.ds(mine, half)]

    def swap_of(j, k):
        return remote(half_out.at[j, k], half_in.at[j, k], hs.at[j, k], hr.at[j, k], sib)

    def slots_in(k):
        g = group_at(k)
        a2a_take(1, k)
        assemble(1, g, x_s)
        tail = tail_of(1, r_msg, g)
        for at, rows, each, first in parts:
            q, r = iota((rows, per * 16), 0), iota((rows, per * 16), 1)
            number = r - q // each * 16
            pick = one((number == gate_row) | (number == gate_row + 1))
            lane = iota((rows, LANE), 1) == iota((rows, LANE), 0) % each + first
            gcol_s[rows_of(g, at, rows), :] = jnp.sum(
                jnp.where(lane, dot(pick, tail), 0.0), axis=-1, keepdims=True
            )
        pre[...] = dot(x_s[rows_of(g), :], win[...])
        activate(g)
        back = gp[rows_of(g), :]
        whole[...] = dot(back, win_t[...])
        half_out[0, k] = whole[:, pl.ds(other, half)].astype(BF16)
        swap_of(0, k).start()
        half_own[k] = whole[:, pl.ds(mine, half)]

    def slots_back(k):
        g = group_at(k)
        gg = jnp.sum(ggv[rows_of(g), :], axis=-1, keepdims=True) + jnp.sum(
            u_s[rows_of(g), pl.ds(mine, half)].astype(F32) * bias_half, axis=-1, keepdims=True
        )
        number = None
        for at, rows, each, first in parts:
            q, r = iota((per * 16, rows), 1), iota((per * 16, rows), 0)
            lane = iota((rows, LANE), 1) == iota((rows, LANE), 0) % each + first
            high, low = split(jnp.where(lane, gg[at : at + rows, :], 0.0))
            line = r - q // each * 16
            piece = dot(one(line == gate_row), high) + dot(one(line == gate_row + 1), low)
            number = piece if number is None else number + piece
        swap_of(0, k).wait()
        pack(2, g, (half_own[k] + half_in[0, k].astype(F32)).astype(BF16), number)
        a2a_send(2, k)

    a2a_forward(1, 1)
    slots_in(0)
    slots_in(1)
    slots_back(0)
    a2a_forward(1, 2)
    slots_back(1)
    slots_in(2)
    a2a_forward(1, 3)
    slots_back(2)
    slots_in(3)
    slots_back(3)

    for k in range(GROUPS):
        act = hid[rows_of(group_at(k)), :]
        whole[...] = dot(act, wout[...])
        half_out[1, k] = whole[:, pl.ds(other, half)].astype(BF16)
        swap_of(1, k).start()
        half_own[k] = whole[:, pl.ds(mine, half)] + bias_half
    for k in range(GROUPS):
        swap_of(1, k).wait()
        pack(3, group_at(k), (half_own[k] + half_in[1, k].astype(F32)).astype(BF16), None)

    sg[...] = (gcol_s[...] * u_s[...].astype(F32)).astype(BF16)
    x_t[...] = jnp.transpose(x_s[...])
    hid_t[...] = jnp.transpose(hid[...])
    o_beo[...] = jnp.sum(sg[...].astype(F32), axis=0, keepdims=True)
    o_bei[...] = jnp.sum(gp[...].astype(F32), axis=0, keepdims=True)
    stores = []
    mix_t = jnp.transpose(mix[...])
    norm_forward()

    flat_id = iota((tp, z.slots), 1)
    back_one = [one(flat_id == f) for f in flat_col]
    for k in range(GROUPS):
        a2a_forward(2, k)
    for k in SEND_ORDER:
        a2a_send(3, k)
    tail_lane = iota((tp, per * 16), 1)
    number = [None, None]
    for k in range(GROUPS):
        g = group_at(k)
        a2a_take(2, k)
        assemble(2, g, y_s)
        tails = [tail_of(2, r_msg, g), tail_of(2, f_msg, g)]
        for c in range(2):
            at = r_col[c] * 16 + (gate_row - g * (per * 16))
            pick = one(sent_col[c] & ((tail_lane == at) | (tail_lane == at + 1)))
            piece = dot(pick, tails[0]) + dot(pick, tails[1])
            number[c] = piece if number[c] is None else number[c] + piece
    grad_gate = [
        jnp.sum(
            jnp.where(iota((tp, LANE), 1) == j_col[c], number[c], 0.0), axis=-1, keepdims=True
        )
        for c in range(2)
    ]
    mean_gate = gate[0] * grad_gate[0] + gate[1] * grad_gate[1]
    e_pad = up_to(z.experts, LANE)
    e_lane = iota((tp, e_pad), 1)
    grad_logits = jnp.where(
        e_lane == r_col[0], gate[0] * (grad_gate[0] - mean_gate), 0.0
    ) + jnp.where(e_lane == r_col[1], gate[1] * (grad_gate[1] - mean_gate), 0.0)
    gl_high, gl_low = split(grad_logits)
    router_pad = router_ref[...]
    if e_pad > z.experts:
        router_pad = jnp.concatenate(
            [router_pad, jnp.zeros((e_pad - z.experts, width), BF16)], axis=0
        )
    grad_n2 = (
        dot(back_one[0] + back_one[1], y_s[...])
        + dot(gl_high, router_pad)
        + dot(gl_low, router_pad)
    )
    grad_router = dot_at(gl_high, n2[0:tp, :]) + dot_at(gl_low, n2[0:tp, :])
    smallf[...] = jnp.zeros(smallf.shape, F32)
    ne = z.experts
    smallf[0:ne, :] = grad_router[0:ne, :]
    gains, shifts, lows = [jnp.zeros((16, width), F32) for _ in range(3)]
    for strip, inverse in zip(strips, inverses):
        part_grad, normal = grad_n2[strip, :], normal2[strip, :]
        gains, shifts = gains + part_grad * normal, shifts + part_grad
        value = upk[strip, :].astype(F32) + norm_backward(
            part_grad, normal, inverse, row_of(ln2g_ref)
        )
        gm[strip, :] = value
        low = value.astype(BF16)
        ag[strip, :] = low
        lows = lows + low.astype(F32)
    for i, sums in ((2, gains), (3, shifts), (4, lows)):
        smallf[ne + i : ne + i + 1, :] = jnp.sum(sums, axis=0, keepdims=True)
    ag[tp:, :] = jnp.zeros((tk - tp, width), BF16)

    halve, double, waiting = sum_plan(z.bits, z.pairs, z.cuts)
    waiting = list(waiting)
    n_main, n_cut = len(halve) - 1, len(double) - 1

    def walk(order):
        start, size, steps = 0, 1 << len(order), []
        for b in order:
            bit = lax.rem(me // b, 2)
            peer = me + b * (1 - 2 * bit)
            size = size // 2
            steps.append((peer, start + (1 - bit) * size, start + bit * size, size))
            start = start + bit * size
        return steps, start

    halving, doubling = [walk(order) for order in halve], [walk(order) for order in double]

    def sum_of(g):
        if g < 3:
            return sum_w.at[g], [r.at[g] for r in from_w], z.chunk, [g]
        if g < n_main:
            pieces = [3 + (g - 3) * z.cuts + i for i in range(z.cuts)]
            return sum_u.at[g - 3], [r.at[g - 3] for r in from_u], z.unit, pieces
        return sum_s, list(from_s), z.small, [n_cut]

    def piece_of(i):
        if i < 3:
            return red_w.at[i], z.chunk
        if i < n_cut:
            return red_u.at[i - 3], z.cut
        return red_s, z.small

    def region(ref, at, count, rows):
        return ref.at[pl.ds(pl.multiple_of(at * rows, 16), count * rows)]

    def rs_copy(g, s):
        src, bufs, rows, _ = sum_of(g)
        peer, give, _, size = halving[g][0][s]
        return remote(
            region(src, give, size, rows), bufs[s], cs.at[g], cr.at[g, s], (peer, core)
        )

    def rs_add(g, s, at, count):
        src, bufs, rows, _ = sum_of(g)
        keep = halving[g][0][s][2]

        def go(i, carry):
            here = pl.ds(pl.multiple_of((at + i) * rows, 16), rows)
            there = pl.ds(pl.multiple_of((at + i - keep) * rows, 16), rows)
            src[here, :] = (src[here, :].astype(F32) + bufs[s][there, :].astype(F32)).astype(BF16)
            return carry

        lax.fori_loop(0, count, go, 0, unroll=2 if count % 2 == 0 else 1)

    def rs_step(g, s):
        src, bufs, rows, pieces = sum_of(g)
        steps, last = halving[g]
        rs_copy(g, s).wait()
        if s + 1 < len(steps):
            _, give, keep, size = steps[s + 1]
            rs_add(g, s, give, size)
            rs_copy(g, s + 1).start()
            rs_add(g, s, keep, size)
            return
        first = 0
        for i in pieces:
            out, count = piece_of(i)
            here = pl.ds(pl.multiple_of(last * rows + first, 16), count)
            goal = pl.ds(pl.multiple_of(doubling[i][1] * count, 16), count)
            out[goal, :] = (
                src[here, :].astype(F32) + bufs[s][first : first + count, :].astype(F32)
            ).astype(BF16)
            ag_copy(i, nbits - 1).start()
            first += count

    def ag_copy(g, s):
        out, rows = piece_of(g)
        peer, _, keep, size = doubling[g][0][s]
        piece = region(out, keep, size, rows)
        return remote(piece, piece, as_.at[g], ar.at[g, s], (peer, core))

    def ag_step(g, s):
        out, rows = piece_of(g)
        peer, give, _, size = doubling[g][0][s]
        ag_copy(g, s).wait_send()
        piece = region(out, give, size, rows)
        remote(piece, piece, as_.at[g], ar.at[g, s], (peer, core)).wait_recv()
        if s > 0:
            ag_copy(g, s - 1).start()

    def share_of(p, m):
        return gpt.at[p, pl.ds(pl.multiple_of(m * z.share, 16), z.share)]

    def quad_send(p):
        here = lax.rem(me, QUAD)
        for q in range(1, QUAD):
            m = in_quad(q)
            remote(
                share_of(p, m), gq.at[p, here], us.at[p], ur.at[p], (me - here + m, core)
            ).start()
        gq[p, here] = gpt[p, pl.ds(pl.multiple_of(here * z.share, 16), z.share), :]

    def quad_step(p):
        block = gq.at[p, pl.ds(0, QUAD - 1)]
        remote(block, block, us.at[p], ur.at[p], sib).wait()
        left = jnp.concatenate([gq[p, m] for m in range(QUAD)], axis=1)
        row = 0
        for h in range(2):
            value = dot(left, n1q[:, h].reshape(QUAD * tk, half)).astype(BF16)
            for b in range(z.blocks):
                sum_u[p, row : row + z.share, :] = value[:, b * LANE : (b + 1) * LANE]
                row += z.share
        if z.unit_rows < n // QUAD * z.unit:
            sum_u[p, z.unit_rows :, :] = jnp.zeros((n // QUAD * z.unit - z.unit_rows, LANE), BF16)
        rs_copy(3 + p, 0).start()

    def advance(place):
        while waiting and waiting[0][0] <= place:
            _, g, s = waiting.pop(0)
            if s == 9:
                quad_step(g - 3)
            elif s >= 0:
                rs_step(g, s)
            else:
                ag_step(g, -1 - s)

    grad_wo = dot(mix_t, ag[...])
    each = z.chain_rows // hw
    for g in range(3):
        for i in range(each):
            b = g * each + i
            sum_w[g, i * hw : (i + 1) * hw, :] = grad_wo[:, b * LANE : (b + 1) * LANE].astype(BF16)
        if z.chain_rows < n * z.chunk:
            sum_w[g, z.chain_rows :, :] = jnp.zeros((n * z.chunk - z.chain_rows, LANE), BF16)
        rs_copy(g, 0).start()
    norm_take()
    advance(0)

    dm[...] = dot_bt(ag[0:tp, :], wo[...]).astype(BF16)
    dm_t[...] = dot_bt(wo[...], ag[...]).astype(BF16)
    ones = jnp.ones((8, tk), BF16)
    for p in range(z.pairs):
        lanes = slice(p * LANE, (p + 1) * LANE)
        vp, dp = v_s[:, lanes], dm[:, lanes]
        dq, dk, dv = [], [], []
        for h in range(2):
            rows = slice(h * HEAD, (h + 1) * HEAD)
            prob = probs[2 * p + h]
            gprob = dot_bt(dp * head_mask[h], vp)
            inner = jnp.sum(prob * gprob, axis=-1, keepdims=True)
            gs = (prob * (gprob - inner)).astype(BF16)
            dq.append(dot_bt(k_t[p, rows, :], gs))
            dk.append(dot(q_t[p, rows, 0:tp], gs))
            dv.append(
                dot(dm_t[p * LANE + h * HEAD : p * LANE + (h + 1) * HEAD, 0:tp], prob.astype(BF16))
            )
        for c, (pair, scale) in enumerate(((dq, score_scale), (dk, score_scale), (dv, 1.0))):
            value = (jnp.concatenate(pair, axis=0) * scale).astype(BF16)
            at = slice(c * LANE, (c + 1) * LANE)
            if c == 0:
                gpt[p, at, LANE:] = jnp.zeros((LANE, tk - LANE), BF16)
                gpt[p, at, 0:tp] = value
            else:
                gpt[p, at, :] = value
        quad_send(p)
        line = dot_bt(ones, gpt[p])
        smallf[ne + 5 : ne + 6, lanes] = line[0:1, 0:LANE]
        smallf[ne + 6 : ne + 7, lanes] = line[0:1, 2 * LANE : 3 * LANE]
        advance(1 + p)

    head_part = None
    for c in range(3):
        joined = jnp.concatenate(
            [gpt[p, c * LANE : (c + 1) * LANE, :] for p in range(z.pairs)], axis=0
        )
        piece = dot(wqkv[c], joined)
        head_part = piece if head_part is None else head_part + piece
    gn_out[...] = jnp.transpose(head_part.astype(BF16))[0:tp, :]
    swap = remote(gn_out, gn_in, hs.at[2, 1], hr.at[2, 1], sib)
    swap.start()
    swap.wait()
    grad_n1 = gn_out[...].astype(F32) + gn_in[...].astype(F32)
    normal = normal1[...]
    smallf[ne : ne + 1, :] = jnp.sum(grad_n1 * normal, axis=0, keepdims=True)
    smallf[ne + 1 : ne + 2, :] = jnp.sum(grad_n1, axis=0, keepdims=True)
    back = gm[...] + norm_backward(grad_n1, normal, inverse1, row_of(ln1g_ref))
    gtok_out[...] = back[0:tok, :]
    copy = pltpu.make_async_copy(gtok_out, o_gtok, osem.at[0])
    copy.start()
    stores.append(copy)
    used = z.small_rows * (width // LANE)
    for b in range(width // LANE):
        sum_s[b * z.small_rows : (b + 1) * z.small_rows, :] = smallf[
            :, b * LANE : (b + 1) * LANE
        ].astype(BF16)
    if used < n * z.small:
        sum_s[used:, :] = jnp.zeros((n * z.small - used, LANE), BF16)
    rs_copy(n_main, 0).start()
    advance(1 + z.pairs)

    for k in range(GROUPS):
        a2a_forward(3, k)
    for k in range(GROUPS):
        a2a_take(3, k)
        assemble(3, group_at(k), y_s)
    branch = gate[0] * dot(back_one[0], y_s[...]) + gate[1] * dot(back_one[1], y_s[...])
    output = mid[...] + branch
    tok_out[...] = output[0:tok, :].astype(BF16)
    copy = pltpu.make_async_copy(tok_out, o_tok, osem.at[1])
    copy.start()
    stores.append(copy)
    lane_id = iota((1, LANE), 1)
    x_all = xf[...]
    line = jnp.zeros((1, LANE), F32)
    for i, number in enumerate(
        (
            jnp.sum(keep_col * x_all * x_all),
            stat_attn,
            jnp.sum(keep_col * branch * branch),
            jnp.sum(keep_col * output * output),
            jnp.sum(keep_col),
        )
    ):
        line = jnp.where(lane_id == i, number, line)
    stat[me] = jnp.broadcast_to(line, (8, LANE))

    def stat_go(j, carry):
        p = lax.rem(me + j, n)
        remote(stat.at[me], stat.at[me], st.at[0], st.at[1], (p, core)).start()
        return carry

    lax.fori_loop(1, n, stat_go, 0)

    advance(LAST)
    block = stat.at[pl.ds(0, n - 1)]
    remote(block, block, st.at[0], st.at[1], sib).wait()
    totals = jnp.sum(stat[...], axis=0)
    count = jnp.sum(jnp.where(iota((8, LANE), 1) == 4, totals, 0.0), axis=-1, keepdims=True)
    o_rms[...] = jnp.sqrt(totals / (count * width))

    for b in range(width // LANE):
        o_small[:, b * LANE : (b + 1) * LANE] = red_s[
            b * z.small_rows : (b + 1) * z.small_rows, :
        ].astype(F32)
    for i in range(4):
        a2a_sent(i)
    for copy in stores:
        copy.wait()


def last_kernel(
    z,
    i_tok,
    i_gtok,
    x_t,
    sg,
    hid_t,
    gp,
    red_w,
    red_u,
    i_small,
    i_bei,
    i_beo,
    i_rms,
    o_tok,
    o_gtok,
    o_ln1g,
    o_ln1b,
    o_wqkv,
    o_bqv,
    o_wo,
    o_bo,
    o_ln2g,
    o_ln2b,
    o_router,
    o_win,
    o_bin,
    o_wout,
    o_bout,
    o_rms,
    wqkv,
    wo,
    win,
    wout,
    back_t,
    osem,
):
    ne, width, hw = z.experts, z.width, z.hw
    stores = []

    def store(src, dst, i):
        copy = pltpu.make_async_copy(src, dst, osem.at[i])
        copy.start()
        stores.append(copy)

    store(i_tok, o_tok, 0)
    store(i_gtok, o_gtok, 1)
    for ref, i in ((o_ln1g, 0), (o_ln1b, 1), (o_ln2g, 2), (o_ln2b, 3), (o_bo, 4)):
        ref[...] = i_small[ne + i : ne + i + 1, :].reshape(width)
    o_router[...] = i_small[0:ne, :]
    o_bqv[...] = i_small[ne + 5 : ne + 7, 0:hw]
    o_bin[...] = i_bei[...]
    o_bout[...] = i_beo[...]
    o_rms[...] = i_rms[0:1, 0:4].reshape(4)

    each = z.chain_rows // hw
    for b in range(width // LANE):
        rows = slice(b % each * hw, (b % each + 1) * hw)
        wo[:, b * LANE : (b + 1) * LANE] = red_w[b // each, rows, :].astype(F32)
    store(wo, o_wo, 2)
    tiles = z.ff // TILE
    for t in range(tiles):
        cols = slice(t * TILE, (t + 1) * TILE)
        win[:, cols] = dot(x_t[...], gp[:, cols])
        store(win.at[:, cols], o_win.at[0, :, cols], 4 + t)
    halve, double, _ = sum_plan(z.bits, z.pairs, z.cuts)
    nbits = len(z.bits)
    piece = math.gcd(z.cut, z.share)
    for p in range(z.pairs):
        for i in range(z.cuts * z.n):
            i, c = divmod(i, z.n)
            order = double[3 + p * z.cuts + i]
            device = sum(b for k, b in enumerate(order) if c >> (nbits - 1 - k) & 1)
            q = 0
            for b in halve[3 + p]:
                q = 2 * q + (device // b) % 2
            for t in range(0, z.cut, piece):
                row = q * z.unit + i * z.cut + t
                if row < z.unit_rows:
                    b, j = divmod(row, z.share)
                    goal = device % QUAD * z.share + j
                    back_t[goal : goal + piece, b * LANE : (b + 1) * LANE] = red_u[
                        p * z.cuts + i, c * z.cut + t : c * z.cut + t + piece, :
                    ]
        for c in range(3):
            value = jnp.transpose(back_t[c * LANE : (c + 1) * LANE, :])
            wqkv[c, :, p * LANE : (p + 1) * LANE] = value.astype(F32)
    store(wqkv, o_wqkv, 3)
    for t in range(tiles):
        rows = slice(t * TILE, (t + 1) * TILE)
        wout[rows, :] = dot(hid_t[rows, :], sg[...])
        store(wout.at[rows, :], o_wout.at[0, rows, :], 4 + tiles + t)
    for copy in stores:
        copy.wait()


def per_device(
    tokens,
    grad_out,
    valid_mask,
    routes,
    slot_index,
    ln1_gain,
    ln1_bias,
    w_qkv,
    bias_qv,
    w_attn_out,
    b_attn_out,
    ln2_gain,
    ln2_bias,
    router,
    w_expert_in,
    b_expert_in,
    w_expert_out,
    b_expert_out,
):
    tok, width = tokens.shape
    hw = w_qkv.shape[2]
    ff = w_expert_in.shape[2]
    z = Sizes(lax.axis_size("dp"), tok, width, hw, ff, router.shape[1])
    n, tp, tk = z.n, z.tp, z.tk
    nbits = len(z.bits)
    vmem = pl.BlockSpec(memory_space=pltpu.VMEM)
    any_ = pl.BlockSpec(memory_space=pl.ANY)
    shape = jax.ShapeDtypeStruct
    groups = 4 + z.pairs
    pieces = 4 + z.pairs * z.cuts
    kept = pltpu.VMEM if n <= 16 else shape
    keep = lambda a: pltpu.with_memory_space_constraint(a, pltpu.VMEM) if n <= 16 else a
    V = pltpu.VMEM
    scratch = [
        V((tok, width), BF16),
        V((tok, width), BF16),
        V((1, tok), jnp.int32),
        V((2, tok), jnp.int32),
        V((2, tok), jnp.int32),
        V((width,), F32),
        V((width,), F32),
        V((2, hw), F32),
        V((width,), F32),
        V((width,), F32),
        V((width,), F32),
        V((z.experts, width), BF16),
        V((1, ff), F32),
        V((1, width), F32),
        V((tok, width), BF16),
        V((tok, width), F32),
        V((3, width, hw), BF16),
        V((hw, width), BF16),
        V((width, ff), BF16),
        V((ff, width), BF16),
        V((tp, width), F32),
        V((tp, width), F32),
        V((tk, width), BF16),
        V((QUAD, 2, tk, z.half), BF16),
        V((z.pairs, LANE, tk), BF16),
        V((z.pairs, LANE, tk), BF16),
        V((hw, tk), BF16),
        V((z.pairs, 3 * LANE, tk), BF16),
        V((z.pairs, QUAD, z.share, tk), BF16),
        V((tk, width), BF16),
        V((tk, hw), BF16),
        V((tk, hw), BF16),
        V((tk, hw), BF16),
        V((2 * z.pairs, tp, tk), F32),
        V((tk, hw), BF16),
        V((tp, width), F32),
        V((tp, width), F32),
        V((tp, width), F32),
        V((tp, width), F32),
        V((tk, width), BF16),
        V((z.slots, tk), BF16),
        V((8, tk), F32),
        V((tk, 8), F32),
        V((z.slots, width), BF16),
        V((z.slots, width), BF16),
        V((z.slots, width), BF16),
        V((z.slots, ff), F32),
        V((z.rows, ff), F32),
        V((z.slots, ff), BF16),
        V((z.slots, 1), F32),
        V((z.slots, LANE), F32),
        V((2, GROUPS, z.rows, z.half), BF16),
        V((2, GROUPS, z.rows, z.half), BF16),
        V((GROUPS, z.rows, z.half), F32),
        V((z.rows, width), F32),
        V((ff, width), BF16),
        V((width, ff), BF16),
        V((tp, width), F32),
        V((tk, width), BF16),
        V((tp, hw), BF16),
        V((tp, width), BF16),
        V((tp, width), BF16),
        V((z.small_rows, width), F32),
        V((n, 8, LANE), F32),
        V((4, n, z.msg, LANE), BF16),
        V((4, n, z.msg, LANE), BF16),
        V((4, n, z.msg, LANE), BF16),
        V((3, n * z.chunk, LANE), BF16),
        V((z.pairs, n // QUAD * z.unit, LANE), BF16),
        V((n * z.small, LANE), BF16),
    ]
    scratch += [V((3, (n >> (s + 1)) * z.chunk, LANE), BF16) for s in range(nbits)]
    scratch += [V(((n >> (s + 1)) * z.small, LANE), BF16) for s in range(nbits)]
    scratch += [
        V((z.pairs, (n // QUAD >> (s + 1)) * z.unit, LANE), BF16) for s in range(nbits - 2)
    ]
    scratch += [
        V((n * z.small, LANE), BF16),
        DMA((18,)),
        DMA((2,)),
        DMA((3, GROUPS)),
        DMA((3, GROUPS)),
        DMA((4,)),
        DMA((4, GROUPS)),
        DMA((4,)),
        DMA((4, GROUPS)),
        DMA((groups,)),
        DMA((groups, nbits)),
        DMA((pieces,)),
        DMA((pieces, nbits)),
        DMA((2,)),
        DMA((4,)),
        DMA((z.pairs,)),
        DMA((z.pairs,)),
    ]
    row = lambda v: v.reshape(1, -1)
    outs = pl.pallas_call(
        functools.partial(mega_kernel, z),
        out_shape=(
            kept((tok, width), BF16),
            kept((tok, width), F32),
            kept((width, z.slots), BF16),
            kept((z.slots, width), BF16),
            kept((ff, z.slots), BF16),
            kept((z.slots, ff), BF16),
            kept((3, n * z.chunk, LANE), BF16),
            kept((z.pairs * z.cuts, n * z.cut, LANE), BF16),
            kept((z.small_rows, width), F32),
            kept((1, ff), F32),
            kept((1, width), F32),
            kept((8, LANE), F32),
        ),
        in_specs=[any_] * 18,
        out_specs=(any_,) * 2 + (vmem,) * 10,
        scratch_shapes=scratch,
        compiler_params=pltpu.CompilerParams(
            collective_id=0,
            has_side_effects=True,
            vmem_limit_bytes=(54 if n <= 16 else 61) * 2**20,
        ),
    )(*(
        pltpu.with_memory_space_constraint(a, pltpu.HBM)
        for a in (
        tokens,
        grad_out,
        row(valid_mask),
        routes.T,
        slot_index.T,
        ln1_gain,
        ln1_bias,
        jnp.transpose(w_qkv, (1, 0, 2)),
        bias_qv,
        w_attn_out,
        b_attn_out,
        ln2_gain,
        ln2_bias,
        router.T,
        w_expert_in[0],
        b_expert_in,
        w_expert_out[0],
        b_expert_out,
        )
    ))
    ne = z.experts
    vec = shape((width,), F32)
    last = pl.pallas_call(
        functools.partial(last_kernel, z),
        out_shape=(
            shape((tok, width), BF16),
            shape((tok, width), F32),
            vec,
            vec,
            shape((3, width, hw), F32),
            shape((2, hw), F32),
            shape((hw, width), F32),
            vec,
            vec,
            vec,
            shape((ne, width), F32),
            shape((1, width, ff), F32),
            shape((1, ff), F32),
            shape((1, ff, width), F32),
            shape((1, width), F32),
            shape((4,), F32),
        ),
        in_specs=[any_] * 2 + [vmem] * 10,
        out_specs=(
            [any_] * 2
            + [vmem] * 2
            + [any_, vmem, any_]
            + [vmem] * 4
            + [any_, vmem, any_, vmem, vmem]
        ),
        scratch_shapes=[
            V((3, width, hw), F32),
            V((hw, width), F32),
            V((width, ff), F32),
            V((ff, width), F32),
            V((3 * LANE, width), BF16),
            DMA((4 + 2 * (ff // TILE),)),
        ],
        compiler_params=pltpu.CompilerParams(vmem_limit_bytes=(30 if n <= 16 else 48) * 2**20),
    )(*(keep(a) for a in outs))
    return (
        last[0],
        last[1],
        last[2],
        last[3],
        jnp.transpose(last[4], (1, 0, 2)),
        *last[5:10],
        last[10].T,
        *last[11:],
    )


def solution(mesh):
    return jax.shard_map(
        per_device,
        mesh=mesh,
        in_specs=(
            P("dp", None),
            P("dp", None),
            P("dp"),
            P("dp", None),
            P("dp", None),
            P(),
            P(),
            P(None, None, "tensor"),
            P(None, "tensor"),
            P("tensor", None),
            P(),
            P(),
            P(),
            P(),
            P("dp", None, "tensor"),
            P("dp", "tensor"),
            P("dp", "tensor", None),
            P("dp", None),
        ),
        out_specs=(
            P("dp", None),
            P("dp", None),
            P(),
            P(),
            P(None, None, "tensor"),
            P(None, "tensor"),
            P("tensor", None),
            P(),
            P(),
            P(),
            P(),
            P("dp", None, "tensor"),
            P("dp", "tensor"),
            P("dp", "tensor", None),
            P("dp", None),
            P(),
        ),
        check_vma=False,
    )
```
